256 devices in a mesh: member: 4 (over z_lo), space: 64 (over z_hi, y, x, core).
Axes of the slice: x: 4, y: 4, z: 8 (z_hi: 2, z_lo: 4; z = z_hi * 4 + z_lo), core: 2. Of those that a mesh axis runs over, the one named last changes fastest.
Arguments:
- tracers: float32 [8, 48, 8, 512, 128], P('member', None, None, 'space'), may hold values from -6 to 6
- horiz_mix: float32 [8, 512, 128], P(None, 'space'), may hold values from 0.05 to 0.22
- vert_mix: float32 [7, 512, 128], P(None, 'space'), may hold values from 0.02 to 0.2
- sunlit: int32 [512], replicated, may hold values from 0 to 1, as said below
- interaction: float32 [48, 48], replicated, may hold values from -0.875 to 0.875
- remin: float32 [48], replicated, may hold values from 0.05 to 0.3
- obs_cell: int32 [4096], replicated, may hold values from 0 to 65535, as said below
- obs_tile: int32 [4096], replicated, may hold values from 0 to 63
- obs_value: float32 [4096], replicated, may hold values from -6 to 6
- obs_noise: float32 [8, 4096], replicated, may hold values from -5 to 5
- obs_var: float32 [4096], replicated, may hold values from 0.25 to 1
Outputs:
- analysis: float32 [8, 48, 8, 512, 128], P('member', None, None, 'space')
The draws below stay inside these ranges and needn't reach their ends.
Inputs may be any that keep to these rules, and one draw needn't show every extreme that they name: The sunlit rows are exactly those of half of the tiles, cyclically consecutive; each tile is wholly sunlit or wholly dark. `obs_cell`: an observation may lie in any tile; every tile uses at least one observation that lies in the tile 64 / 2 tiles on, counted round.
All inputs are finite; a program needn't handle non-finite values.
Results may differ from the reference program's by a relative error of at most 0.0003.
Values sent between devices are 32-bit elements; how exact they have to be, the bound alone decides.
A program may use at most 64 MiB of HBM per device.

```python
import math
import jax
import jax.numpy as jnp
from jax import lax

NTR = 48
L = 8
COLS = 128
R = 8
NSUB = 4
MEMBERS = 8
ROWS = 512
NOBS = 4096
N_SPACE = 64


def draw_sunlit(key, part):
    first_tile = jax.random.randint(key, (), 0, N_SPACE)
    tile_of_row = jnp.arange(ROWS, dtype=jnp.int32) // R
    return ((tile_of_row - first_tile) % N_SPACE < N_SPACE // 2).astype(jnp.int32)


def observation_layout(key):
    base_key = jax.random.fold_in(key, 11)
    key_tile, key_offset, key_place = jax.random.split(base_key, 3)
    obs_ids = jnp.arange(NOBS, dtype=jnp.int32)
    leading = obs_ids < N_SPACE
    tile_number = jnp.where(leading, obs_ids % N_SPACE, jax.random.randint(key_tile, (NOBS,), 0, N_SPACE))
    offset = jnp.where(leading, N_SPACE // 2, jax.random.randint(key_offset, (NOBS,), 0, N_SPACE))
    home_tile = (tile_number + offset) % N_SPACE
    place = jax.random.randint(key_place, (NOBS,), 0, R * COLS)
    return (tile_number.astype(jnp.int32), (home_tile * (R * COLS) + place).astype(jnp.int32))


def draw_obs_cell(key, part):
    return observation_layout(key)[1]


def draw_obs_tile(key, part):
    return observation_layout(key)[0]


def levels(rng, extent, cuts, low, high):
    def one(dim, shards_of):
        heights = jax.random.uniform(jax.random.fold_in(jax.random.fold_in(rng, 6), dim), (shards_of,), jnp.float32, low / len(cuts), high / len(cuts))
        return jnp.repeat(jnp.exp(heights), extent[dim] // shards_of).reshape((-1,) + (1,) * (len(extent) - dim - 1))

    loudness = one(*cuts[0])
    for cut in cuts[1:]:
        loudness = loudness * one(*cut)
    return loudness


def normal_values(key, shape, width, limit, pieces=(), held_as=jnp.bfloat16):
    drawn = jax.random.normal(key, shape, jnp.float32) * width
    if len(pieces) > 0:
        drawn = levels(key, shape, pieces, -0.22, 0.18) * drawn
    return jnp.clip(drawn, min=-limit, max=limit).astype(held_as)


def setup_inputs(seed: int = 0) -> dict:
    keys = jax.random.split(jax.random.key(seed), 12)
    return {
        "tracers": normal_values(keys[0], (MEMBERS, NTR, L, ROWS, COLS), 1.0, 6.0, ((0, 4), (3, 64)), jnp.float32),
        "horiz_mix": jnp.clip(0.05 + 0.17 * jax.random.uniform(keys[1], (L, ROWS, COLS), jnp.float32) ** levels(keys[1], (L, ROWS, COLS), ((1, 64),), -0.2, 0.2), 0.05, 0.22),
        "vert_mix": jnp.clip(0.02 + 0.18 * jax.random.uniform(keys[2], (L - 1, ROWS, COLS), jnp.float32) ** levels(keys[2], (L - 1, ROWS, COLS), ((1, 64),), -0.2, 0.2), 0.02, 0.2),
        "sunlit": draw_sunlit(jax.random.fold_in(keys[11], 71), 0),
        "interaction": normal_values(keys[4], (NTR, NTR), NTR ** -0.5, 0.875, (), jnp.float32),
        "remin": jnp.clip(jnp.exp(jax.random.uniform(keys[5], (NTR,), jnp.float32, math.log(0.05), math.log(0.3))), 0.05, 0.3),
        "obs_cell": draw_obs_cell(jax.random.fold_in(keys[11], 71), 0),
        "obs_tile": draw_obs_tile(jax.random.fold_in(keys[11], 71), 0),
        "obs_value": normal_values(keys[8], (NOBS,), 1.0, 6.0, (), jnp.float32),
        "obs_noise": normal_values(keys[9], (MEMBERS, NOBS), 0.7, 5.0, (), jnp.float32),
        "obs_var": jnp.clip(jnp.exp(jax.random.uniform(keys[10], (NOBS,), jnp.float32, math.log(0.25), math.log(1.0))), 0.25, 1.0),
    }


def sunlit_update(column_block, interaction, remin, light_levels):
    fraction = 1.0 / NSUB
    light_shape = (1, 1, -1) + (1,) * (column_block.ndim - 3)
    remin_shape = (1, -1) + (1,) * (column_block.ndim - 2)
    for substep in range(NSUB):
        uptake = jnp.einsum('ji,mi...->mj...', interaction, column_block, precision=lax.Precision.HIGHEST)
        column_block = column_block + fraction * (light_levels.reshape(light_shape) * jnp.tanh(uptake) - remin.reshape(remin_shape) * column_block)
    return column_block

def dark_update(column_block, remin):
    fraction = 1.0 / NSUB
    remin_shape = (1, -1) + (1,) * (column_block.ndim - 2)
    for substep in range(NSUB):
        column_block = column_block - fraction * (remin.reshape(remin_shape) * column_block)
    return column_block

def vertical_mixing(state, vert_mix):
    vertical_flux = vert_mix[None, None] * (state[:, :, 1:] - state[:, :, :-1])
    zero_layer = jnp.zeros_like(state[:, :, :1])
    return state + jnp.concatenate([vertical_flux, zero_layer], axis=2) - jnp.concatenate([zero_layer, vertical_flux], axis=2)

def reference(tracers, horiz_mix, vert_mix, sunlit, interaction, remin, obs_cell, obs_tile, obs_value, obs_noise, obs_var):
    padded = jnp.pad(tracers, ((0, 0), (0, 0), (0, 0), (1, 1), (1, 1)), mode='edge')
    laplace = padded[..., :-2, 1:-1] + padded[..., 2:, 1:-1] + padded[..., 1:-1, :-2] + padded[..., 1:-1, 2:] - 4.0 * tracers
    state = tracers + horiz_mix[None, None] * laplace
    state = vertical_mixing(state, vert_mix)
    light_levels = 0.6 * jnp.exp(-0.4 * jnp.arange(L, dtype=jnp.float32))
    lit_state = sunlit_update(state, interaction, remin, light_levels)
    dark_state = dark_update(state, remin)
    state = jnp.where((sunlit > 0)[None, None, None, :, None], lit_state, dark_state)
    surface = state[:, 0, 0].reshape(MEMBERS, ROWS * COLS)
    observed = jnp.take(surface, obs_cell, axis=1)
    spread = observed - jnp.mean(observed, axis=0, keepdims=True)
    innov = obs_value[None, :] + obs_noise - observed

    def tile_weights(tile_number):
        selection = jnp.where(obs_tile == tile_number, 1.0 / obs_var, 0.0)
        scaled = spread * selection[None, :]
        gram_matrix = (MEMBERS - 1) * jnp.eye(MEMBERS, dtype=jnp.float32) + jnp.dot(scaled, spread.T, precision=lax.Precision.HIGHEST)
        right_side = jnp.dot(scaled, innov.T, precision=lax.Precision.HIGHEST)
        weights = jnp.linalg.solve(gram_matrix, right_side)
        return weights - jnp.mean(weights, axis=0, keepdims=True)
    all_weights = lax.map(tile_weights, jnp.arange(N_SPACE, dtype=jnp.int32))
    tiled = state.reshape(MEMBERS, NTR, L, N_SPACE, R, COLS)
    increment = jnp.einsum('kabtrc,tkm->mabtrc', tiled, all_weights, precision=lax.Precision.HIGHEST)
    return (tiled + increment).reshape(MEMBERS, NTR, L, ROWS, COLS)
```

```python
import functools

import jax
import jax.numpy as jnp
from jax import lax
from jax.experimental import pallas as pl
from jax.experimental.pallas import tpu as pltpu
from jax.sharding import PartitionSpec as P

NSUB = 4
GROUP = 8
DEEP = 2
QROWS = 2
OBS_STEP = 512
F32 = jnp.float32
MESH = pl.DeviceIdType.MESH
HIGHEST = lax.Precision.HIGHEST


def split_coefficients(interaction):
    high = lax.reduce_precision(interaction, 8, 7)
    low = interaction - high
    return jnp.concatenate([high, high, low], axis=1).astype(jnp.bfloat16)


def kernel(
    sizes,
    sunlit,
    tracers,
    horiz_mix,
    vert_mix,
    coefficients,
    remin,
    obs_cell,
    obs_tile,
    obs_value,
    obs_noise,
    obs_var,
    out,
    raw,
    mixed,
    states,
    results,
    passed,
    surface,
    partial,
    recv_mid,
    held_mid,
    recv_deep,
    held_group,
    recv_group,
    splats,
    load_sem,
    halo_send,
    halo_recv,
    state_send,
    state_recv,
    result_send,
    result_recv,
    store_sem,
    mid_send,
    mid_recv,
    deep_send,
    deep_recv,
    group_send,
    group_recv,
):
    tiles, mids, deeps = sizes
    ntr, levels, rows, cols = tracers.shape[1:]
    pair, quarters = 2, rows // QROWS
    members = 8
    pieces = levels * quarters
    me = lax.axis_index("member")
    tile = lax.axis_index("space")
    inner = (me == 1) | (me == 2)
    outer = jnp.logical_not(inner)
    group_at = lax.rem(tile, GROUP)
    mid_at = lax.rem(tile // GROUP, mids)
    deep_at = tile // (GROUP * mids)
    near = jnp.where(me == 0, 1, 2)
    beside = jnp.where(me == 1, 0, 3)
    across = jnp.where(inner, 3 - me, jnp.where(me == 0, 2, 1))

    def mid_tile(j):
        return (deep_at * mids + lax.rem(mid_at + j, mids)) * GROUP + group_at

    def deep_tile(j):
        return (lax.rem(deep_at + j, deeps) * mids + mid_at) * GROUP + group_at

    def group_tile(j):
        return (deep_at * mids + mid_at) * GROUP + lax.rem(group_at + j, GROUP)

    def load(level, row, m):
        return pltpu.make_async_copy(
            tracers.at[m, :, level, row], raw.at[level, row + 1, m], load_sem.at[level, row, m]
        )

    def start_level(level, carry):
        for row in (0, rows - 1, *range(1, rows - 1)):
            for m in range(pair):
                load(level, row, m).start()
        return carry

    lax.fori_loop(0, levels, start_level, 0)

    barrier = pltpu.get_barrier_semaphore()
    for j in range(1, 4):
        pl.semaphore_signal(
            barrier, 1, device_id=(lax.rem(me + j, 4), tile), device_id_type=MESH
        )

    @pl.when(tile > 0)
    def _():
        pl.semaphore_signal(barrier, 1, device_id=(me, tile - 1), device_id_type=MESH)

    @pl.when(tile < tiles - 1)
    def _():
        pl.semaphore_signal(barrier, 1, device_id=(me, tile + 1), device_id_type=MESH)

    @pl.when(inner)
    def _():
        for j in range(1, mids):
            pl.semaphore_signal(barrier, 1, device_id=(me, mid_tile(j)), device_id_type=MESH)
        for j in range(1, deeps):
            pl.semaphore_signal(barrier, 1, device_id=(me, deep_tile(j)), device_id_type=MESH)
        for j in range(1, GROUP):
            pl.semaphore_signal(barrier, 1, device_id=(me, group_tile(j)), device_id_type=MESH)

    peers = 3 + (tile > 0).astype(jnp.int32) + (tile < tiles - 1).astype(jnp.int32)
    peers += jnp.where(inner, mids + deeps + GROUP - 3, 0)
    pl.semaphore_wait(barrier, peers)

    def halo_up(level):
        return pltpu.make_async_remote_copy(
            src_ref=raw.at[level, rows],
            dst_ref=raw.at[level, 0],
            send_sem=halo_send.at[level, 0],
            recv_sem=halo_recv.at[level, 0],
            device_id=(me, lax.rem(tile + 1, tiles)),
            device_id_type=MESH,
        )

    def halo_down(level):
        return pltpu.make_async_remote_copy(
            src_ref=raw.at[level, 1],
            dst_ref=raw.at[level, rows + 1],
            send_sem=halo_send.at[level, 1],
            recv_sem=halo_recv.at[level, 1],
            device_id=(me, lax.rem(tile + tiles - 1, tiles)),
            device_id_type=MESH,
        )

    def send_edges(level, carry):
        for row in (0, rows - 1):
            for m in range(pair):
                load(level, row, m).wait()

        @pl.when(tile < tiles - 1)
        def _():
            halo_up(level).start()

        @pl.when(tile > 0)
        def _():
            halo_down(level).start()

        return carry

    lax.fori_loop(0, levels, send_edges, 0)

    lane = lax.broadcasted_iota(jnp.int32, (ntr, cols), 1)

    def mix_level(level):
        for row in range(1, rows - 1):
            for m in range(pair):
                load(level, row, m).wait()

        @pl.when(tile > 0)
        def _():
            halo_up(level).wait_recv()

        @pl.when(tile == 0)
        def _():
            raw[level, 0] = raw[level, 1]

        @pl.when(tile < tiles - 1)
        def _():
            halo_down(level).wait_recv()

        @pl.when(tile == tiles - 1)
        def _():
            raw[level, rows + 1] = raw[level, rows]

        def mix_row(row, carry):
            strength = horiz_mix[level, pl.ds(row, 1), :]
            for m in range(pair):
                own = raw[level, row + 1, m]
                west = jnp.where(lane == 0, own, pltpu.roll(own, 1, 1))
                east = jnp.where(lane == cols - 1, own, pltpu.roll(own, cols - 1, 1))
                laplace = raw[level, row, m] + raw[level, row + 2, m] + west + east - 4.0 * own
                mixed[level, row, m] = own + strength * laplace
            return carry

        lax.fori_loop(0, rows, mix_row, 0)

    def state_copy(piece, to, which):
        level, quarter = piece // quarters, lax.rem(piece, quarters)
        block = states.at[level, quarter, pl.ds(2 * me, 2)]
        return pltpu.make_async_remote_copy(
            src_ref=block,
            dst_ref=block,
            send_sem=state_send.at[piece, which],
            recv_sem=state_recv.at[piece, me],
            device_id=(to, tile),
            device_id_type=MESH,
        )

    loss = jnp.broadcast_to(remin[...], (ntr, cols))
    loss = jnp.concatenate([loss] * (QROWS * pair), axis=1)
    taken = coefficients[...]

    def grow_piece(piece, carry):
        level, quarter = piece // quarters, lax.rem(piece, quarters)
        below, above = jnp.minimum(level + 1, levels - 1), jnp.maximum(level - 1, 0)
        light = 0.6 * jnp.exp(-0.4 * jnp.full((1, cols), level, jnp.int32).astype(F32))
        blocks, lights = [], []
        for r in range(QROWS):
            row = quarter * QROWS + r
            lit = (sunlit[tile * rows + row] > 0).astype(F32)
            down_mix = vert_mix[jnp.minimum(level, levels - 2), pl.ds(row, 1), :]
            up_mix = vert_mix[above, pl.ds(row, 1), :]
            for m in range(pair):
                here = mixed[level, row, m]
                down = down_mix * (mixed[below, row, m] - here)
                up = up_mix * (here - mixed[above, row, m])
                blocks.append(here + down - up)
                lights.append(light * lit)
        value = jnp.concatenate(blocks, axis=1)
        light = jnp.concatenate(lights, axis=1)
        for _ in range(NSUB):
            high = value.astype(jnp.bfloat16)
            low = (value - high.astype(F32)).astype(jnp.bfloat16)
            uptake = jnp.dot(
                taken, jnp.concatenate([high, low, high], axis=0), preferred_element_type=F32
            )
            value = value + (1.0 / NSUB) * (light * jnp.tanh(uptake) - loss * value)
        for r in range(QROWS):
            for m in range(pair):
                at = (r * pair + m) * cols
                states[level, quarter, 2 * me + m, r] = value[:, at : at + cols]
        state_copy(piece, across, 0).start()

        @pl.when(outer)
        def _():
            state_copy(piece, near, 1).start()

        return carry

    mix_level(0)

    def step_level(level, carry):
        @pl.when(level < levels - 1)
        def _():
            mix_level(level + 1)

        return lax.fori_loop(level * quarters, (level + 1) * quarters, grow_piece, carry)

    lax.fori_loop(0, levels, step_level, 0)

    def wait_states(piece):
        level, quarter = piece // quarters, lax.rem(piece, quarters)
        for j in range(1, 4):
            source = lax.rem(me + j, 4)
            block = states.at[level, quarter, pl.ds(2 * source, 2)]
            pltpu.make_async_remote_copy(
                src_ref=block,
                dst_ref=block,
                send_sem=state_send.at[piece, 0],
                recv_sem=state_recv.at[piece, source],
                device_id=(source, tile),
                device_id_type=MESH,
            ).wait_recv()

    def result_copy(piece):
        return pltpu.make_async_remote_copy(
            src_ref=passed.at[piece],
            dst_ref=results.at[piece],
            send_sem=result_send.at[piece],
            recv_sem=result_recv.at[piece],
            device_id=(beside, tile),
            device_id_type=MESH,
        )

    def stores(piece):
        level, quarter = piece // quarters, lax.rem(piece, quarters)
        return [
            pltpu.make_async_copy(
                results.at[piece, m, r],
                out.at[m, :, level, quarter * QROWS + r],
                store_sem.at[piece, m, r],
            )
            for m in range(pair)
            for r in range(QROWS)
        ]

    def small_copy(source, target, send, recv, at):
        return pltpu.make_async_remote_copy(
            src_ref=source,
            dst_ref=target,
            send_sem=send,
            recv_sem=recv,
            device_id=(me, at),
            device_id_type=MESH,
        )

    def partial_sums():
        for quarter in range(quarters):
            for r in range(QROWS):
                for m in range(members):
                    at = (quarter * QROWS + r) * members + m
                    surface[at : at + 1, :] = states[0, quarter, m, r, 0:1, :]
        picked_from = surface[...]
        width = OBS_STEP // cols
        column_ids = lax.broadcasted_iota(jnp.int32, (cols, OBS_STEP), 0)
        tile_ids = lax.broadcasted_iota(jnp.int32, (tiles, OBS_STEP), 0)

        def flat(ref, step):
            return jnp.concatenate(
                [ref[pl.ds(step * width + i, 1), :] for i in range(width)], axis=1
            )

        def step_obs(step, total):
            local = flat(obs_cell, step) - tile * (rows * cols)
            column = jnp.bitwise_and(local, cols - 1)
            row_of = jnp.right_shift(local, cols.bit_length() - 1)
            one_hot = (column_ids == column).astype(F32)
            picked = jnp.dot(
                picked_from, one_hot, precision=HIGHEST, preferred_element_type=F32
            )
            observed = jnp.zeros((members, OBS_STEP), F32)
            for r in range(rows):
                observed += jnp.where(
                    row_of == r, picked[r * members : (r + 1) * members], 0.0
                )
            inside = (row_of >= 0) & (row_of < rows)
            weight = jnp.where(inside, 1.0 / flat(obs_var, step), 0.0)
            spread = observed - jnp.sum(observed, axis=0, keepdims=True) * (1.0 / members)
            noise = obs_noise[:, pl.ds(pl.multiple_of(step * OBS_STEP, OBS_STEP), OBS_STEP)]
            innov = flat(obs_value, step) + noise - observed
            scaled = spread * weight
            both = jnp.concatenate([spread, innov], axis=0)
            products = jnp.concatenate(
                [scaled[a : a + 1] * both for a in range(members)], axis=0
            )
            chosen = (tile_ids == flat(obs_tile, step)).astype(F32)
            return total + lax.dot_general(
                chosen,
                products,
                (((1,), (1,)), ((), ())),
                precision=HIGHEST,
                preferred_element_type=F32,
            )

        steps = obs_noise.shape[1] // OBS_STEP
        total = lax.fori_loop(0, steps, step_obs, jnp.zeros((tiles, 128), F32))
        for d in range(deeps):
            for b in range(mids):
                at = (d * mids + b) * GROUP
                partial[b, d] = total[at : at + GROUP]

        copies = []
        for j in range(1, mids):
            other = lax.rem(mid_at + j, mids)
            copies.append(
                small_copy(
                    partial.at[other],
                    recv_mid.at[mid_at],
                    mid_send.at[j],
                    mid_recv.at[mid_at],
                    mid_tile(j),
                )
            )
        for copy in copies:
            copy.start()
        sums = partial[mid_at]
        for j in range(1, mids):
            other = lax.rem(mid_at + j, mids)
            small_copy(
                recv_mid.at[other],
                recv_mid.at[other],
                mid_send.at[j],
                mid_recv.at[other],
                mid_tile(j),
            ).wait_recv()
            sums = sums + recv_mid[other]
        held_mid[...] = sums
        for j in range(1, deeps):
            other = lax.rem(deep_at + j, deeps)
            copies.append(
                small_copy(
                    held_mid.at[other],
                    recv_deep.at[deep_at],
                    deep_send.at[j],
                    deep_recv.at[deep_at],
                    deep_tile(j),
                )
            )
            copies[-1].start()
        sums = held_mid[deep_at]
        for j in range(1, deeps):
            other = lax.rem(deep_at + j, deeps)
            small_copy(
                recv_deep.at[other],
                recv_deep.at[other],
                deep_send.at[j],
                deep_recv.at[other],
                deep_tile(j),
            ).wait_recv()
            sums = sums + recv_deep[other]
        held_group[...] = sums
        for j in range(1, GROUP):
            copies.append(
                small_copy(
                    held_group,
                    recv_group.at[group_at],
                    group_send.at[j],
                    group_recv.at[group_at],
                    group_tile(j),
                )
            )
            copies[-1].start()
        for j in range(1, GROUP):
            other = lax.rem(group_at + j, GROUP)
            small_copy(
                held_group,
                recv_group.at[other],
                group_send.at[j],
                group_recv.at[other],
                group_tile(j),
            ).wait_recv()
            sums = sums + recv_group[other]
        for copy in copies:
            copy.wait_send()
        return sums

    def weights_of(sums):
        sub = lax.broadcasted_iota(jnp.int32, (8, 128), 0)
        lane8 = lax.broadcasted_iota(jnp.int32, (8, 128), 1)
        own = jnp.sum(jnp.where(sub == group_at, sums, 0.0), axis=0, keepdims=True)
        parts = jnp.where(
            jnp.right_shift(lane8, 4) == sub, jnp.broadcast_to(own, (8, 128)), 0.0
        )
        fold_from = lax.broadcasted_iota(jnp.int32, (128, 128), 0)
        fold_to = lax.broadcasted_iota(jnp.int32, (128, 128), 1)
        fold = (jnp.bitwise_and(fold_from, 15) == fold_to).astype(F32)
        system = jnp.dot(parts, fold, precision=HIGHEST, preferred_element_type=F32)
        system = system + jnp.where(lane8 == sub, float(members - 1), 0.0)
        for k in range(members):
            column = jnp.sum(jnp.where(lane8 == k, system, 0.0), axis=1, keepdims=True)
            pivot = system[k : k + 1] / column[k : k + 1]
            system = jnp.where(sub == k, pivot, system - column * pivot)
        return system - jnp.sum(system, axis=0, keepdims=True) * (1.0 / members)

    def spread_weights(centered):
        sub = lax.broadcasted_iota(jnp.int32, (8, 128), 0)
        lane8 = lax.broadcasted_iota(jnp.int32, (8, 128), 1)
        for j in range(4):
            member = 2 * me + j if j < 2 else 2 * beside + j - 2
            column = jnp.sum(
                jnp.where(lane8 == members + member, centered, 0.0), axis=1, keepdims=True
            )
            wide = jnp.broadcast_to(column, (8, 128))
            wide = wide + jnp.where(sub == member, 1.0, 0.0)
            for k in range(members):
                splats[j, k] = jnp.broadcast_to(wide[k : k + 1], (8, 128))

    def analyse(piece):
        level, quarter = piece // quarters, lax.rem(piece, quarters)

        def analyse_part(at, carry):
            r, first = at // (ntr // 8), pl.multiple_of(lax.rem(at, ntr // 8) * 8, 8)
            sums = [None] * 4
            for k in range(members):
                value = states[level, quarter, k, r, pl.ds(first, 8), :]
                for j in range(4):
                    term = value * splats[j, k]
                    sums[j] = term if k == 0 else sums[j] + term
            for m in range(pair):
                results[piece, m, r, pl.ds(first, 8), :] = sums[m]
                passed[piece, m, r, pl.ds(first, 8), :] = sums[2 + m]
            return carry

        lax.fori_loop(0, QROWS * (ntr // 8), analyse_part, 0)
        result_copy(piece).start()
        for store in stores(piece):
            store.start()

    @pl.when(inner)
    def _():
        def wait_top(piece, carry):
            wait_states(piece)
            return carry

        lax.fori_loop(0, quarters, wait_top, 0)
        spread_weights(weights_of(partial_sums()))

        def analyse_top(piece, carry):
            analyse(piece)
            return carry

        def analyse_next(piece, carry):
            wait_states(piece)
            analyse(piece)
            return carry

        lax.fori_loop(0, quarters, analyse_top, 0)
        lax.fori_loop(quarters, pieces, analyse_next, 0)

    @pl.when(outer)
    def _():
        def take(piece, carry):
            result_copy(piece).wait_recv()
            for store in stores(piece):
                store.start()
            return carry

        lax.fori_loop(0, pieces, take, 0)

    def finish_level(level, carry):
        @pl.when(tile < tiles - 1)
        def _():
            halo_up(level).wait_send()

        @pl.when(tile > 0)
        def _():
            halo_down(level).wait_send()

        return carry

    lax.fori_loop(0, levels, finish_level, 0)

    def finish(piece, carry):
        state_copy(piece, across, 0).wait_send()

        @pl.when(outer)
        def _():
            state_copy(piece, near, 1).wait_send()

        @pl.when(inner)
        def _():
            result_copy(piece).wait_send()

        for store in stores(piece):
            store.wait()
        return carry

    lax.fori_loop(0, pieces, finish, 0)


def on_device(
    tracers,
    horiz_mix,
    vert_mix,
    sunlit,
    interaction,
    remin,
    obs_cell,
    obs_tile,
    obs_value,
    obs_noise,
    obs_var,
):
    pair, ntr, levels, rows, cols = tracers.shape
    tiles = lax.axis_size("space")
    deeps = DEEP if tiles > GROUP else 1
    mids = tiles // (deeps * GROUP)
    quarters = rows // QROWS
    pieces = levels * quarters
    count = obs_cell.shape[0]
    obs_rows = (count // cols, cols)
    vmem = pl.BlockSpec(memory_space=pltpu.VMEM)
    anywhere = pl.BlockSpec(memory_space=pl.ANY)
    dma = pltpu.SemaphoreType.DMA
    result = pl.pallas_call(
        functools.partial(kernel, (tiles, mids, deeps)),
        out_shape=jax.ShapeDtypeStruct(tracers.shape, F32),
        in_specs=[pl.BlockSpec(memory_space=pltpu.SMEM), anywhere] + [vmem] * 9,
        out_specs=anywhere,
        scratch_shapes=[
            pltpu.VMEM((levels, rows + 2, pair, ntr, cols), F32),
            pltpu.VMEM((levels, rows, pair, ntr, cols), F32),
            pltpu.VMEM((levels, quarters, 8, QROWS, ntr, cols), F32),
            pltpu.VMEM((pieces, pair, QROWS, ntr, cols), F32),
            pltpu.VMEM((pieces, pair, QROWS, ntr, cols), F32),
            pltpu.VMEM((rows * 8, cols), F32),
            pltpu.VMEM((mids, deeps, GROUP, 128), F32),
            pltpu.VMEM((mids, deeps, GROUP, 128), F32),
            pltpu.VMEM((deeps, GROUP, 128), F32),
            pltpu.VMEM((deeps, GROUP, 128), F32),
            pltpu.VMEM((GROUP, 128), F32),
            pltpu.VMEM((GROUP, GROUP, 128), F32),
            pltpu.VMEM((4, 8, 8, 128), F32),
            dma((levels, rows, pair)),
            dma((levels, 2)),
            dma((levels, 2)),
            dma((pieces, 2)),
            dma((pieces, 4)),
            dma((pieces,)),
            dma((pieces,)),
            dma((pieces, pair, QROWS)),
            dma((mids,)),
            dma((mids,)),
            dma((deeps,)),
            dma((deeps,)),
            dma((GROUP,)),
            dma((GROUP,)),
        ],
        compiler_params=pltpu.CompilerParams(
            collective_id=0, has_side_effects=True, vmem_limit_bytes=56 * 1024 * 1024
        ),
        cost_estimate=pl.CostEstimate(
            flops=500_000_000, bytes_accessed=8_000_000, transcendentals=3_000_000
        ),
        name="step_and_analysis",
    )(
        sunlit,
        tracers,
        horiz_mix,
        vert_mix,
        split_coefficients(interaction),
        remin.reshape(ntr, 1),
        obs_cell.reshape(obs_rows),
        obs_tile.reshape(obs_rows),
        obs_value.reshape(obs_rows),
        obs_noise,
        obs_var.reshape(obs_rows),
    )
    return result


def solution(mesh):
    return jax.shard_map(
        on_device,
        mesh=mesh,
        in_specs=(
            P("member", None, None, "space", None),
            P(None, "space", None),
            P(None, "space", None),
            P(),
            P(),
            P(),
            P(),
            P(),
            P(),
            P(),
            P(),
        ),
        out_specs=P("member", None, None, "space", None),
        check_vma=False,
    )
```

```python
import functools

import jax
import jax.numpy as jnp
from jax import lax
from jax.experimental import pallas as pl
from jax.experimental.pallas import tpu as pltpu
from jax.sharding import PartitionSpec as P

NSUB = 4
GROUP = 8
DEEP = 2
QROWS = 2
LAG = 2
VMEM_BYTES = 34 * 1024 * 1024
OBS_STEP = 512
F32 = jnp.float32
MESH = pl.DeviceIdType.MESH
HIGHEST = lax.Precision.HIGHEST


def kernel(
    sizes,
    tracers,
    horiz_from,
    vert_from,
    sunlit_from,
    interaction_from,
    remin_from,
    cell_from,
    chosen_from,
    value_from,
    noise_from,
    var_from,
    out,
    horiz_mix,
    vert_mix,
    sunlit,
    interaction,
    remin,
    obs_cell,
    obs_tile,
    obs_value,
    obs_noise,
    obs_var,
    lit,
    relayed,
    raw,
    mixed,
    states,
    results,
    passed,
    surface,
    partial,
    recv_mid,
    held_mid,
    recv_deep,
    held_group,
    recv_group,
    splats,
    small_sem,
    load_sem,
    relay_send,
    relay_recv,
    halo_send,
    halo_recv,
    state_send,
    state_recv,
    result_send,
    result_recv,
    store_sem,
    mid_send,
    mid_recv,
    deep_send,
    deep_recv,
    group_send,
    group_recv,
):
    tiles, mids, deeps = sizes
    ntr, levels, rows, cols = tracers.shape[1:]
    pair, quarters = 2, rows // QROWS
    members = 8
    pieces = levels * quarters
    me = lax.axis_index("member")
    tile = lax.axis_index("space")
    inner = (me == 1) | (me == 2)
    outer = jnp.logical_not(inner)
    group_at = lax.rem(tile, GROUP)
    mid_at = lax.rem(tile // GROUP, mids)
    deep_at = tile // (GROUP * mids)
    half = tiles // 2
    is_up_relay = (tile < half) & (lax.rem(tile, 4) == 2)
    is_down_relay = (tile >= half) & (lax.rem(tile, 4) == 1)

    def up_relay(level):
        return 4 * level + 2

    def down_relay(level):
        return half + 4 * level + 1

    near = jnp.where(me == 0, 1, 2)
    beside = jnp.where(me == 1, 0, 3)
    across = jnp.where(inner, 3 - me, jnp.where(me == 0, 2, 1))

    def mid_tile(j):
        return (deep_at * mids + lax.rem(mid_at + j, mids)) * GROUP + group_at

    def deep_tile(j):
        return (lax.rem(deep_at + j, deeps) * mids + mid_at) * GROUP + group_at

    def group_tile(j):
        return (deep_at * mids + mid_at) * GROUP + lax.rem(group_at + j, GROUP)

    def load(level, row):
        return pltpu.make_async_copy(
            tracers.at[:, :, level, row], raw.at[level, row + 1], load_sem.at[level, row]
        )

    barrier = pltpu.get_barrier_semaphore()
    for j in range(1, 4):
        pl.semaphore_signal(
            barrier, 1, device_id=(lax.rem(me + j, 4), tile), device_id_type=MESH
        )

    @pl.when(tile > 0)
    def _():
        pl.semaphore_signal(barrier, 1, device_id=(me, tile - 1), device_id_type=MESH)

    @pl.when(tile < tiles - 1)
    def _():
        pl.semaphore_signal(barrier, 1, device_id=(me, tile + 1), device_id_type=MESH)

    @pl.when(inner)
    def _():
        for j in range(1, mids):
            pl.semaphore_signal(barrier, 1, device_id=(me, mid_tile(j)), device_id_type=MESH)
        for j in range(1, deeps):
            pl.semaphore_signal(barrier, 1, device_id=(me, deep_tile(j)), device_id_type=MESH)
        for j in range(1, GROUP):
            pl.semaphore_signal(barrier, 1, device_id=(me, group_tile(j)), device_id_type=MESH)

    if deeps > 1:

        @pl.when(tile == half - 1)
        def _():
            for level in range(levels):
                pl.semaphore_signal(
                    barrier, 1, device_id=(me, down_relay(level)), device_id_type=MESH
                )

        @pl.when(tile == half)
        def _():
            for level in range(levels):
                pl.semaphore_signal(
                    barrier, 1, device_id=(me, up_relay(level)), device_id_type=MESH
                )

        @pl.when(is_up_relay)
        def _():
            pl.semaphore_signal(barrier, 1, device_id=(me, half - 1), device_id_type=MESH)

        @pl.when(is_down_relay)
        def _():
            pl.semaphore_signal(barrier, 1, device_id=(me, half), device_id_type=MESH)

    def small(at):
        source, held = (
            (interaction_from, interaction),
            (remin_from, remin),
            (sunlit_from, sunlit),
            (horiz_from, horiz_mix),
            (vert_from, vert_mix),
            (cell_from, obs_cell),
            (chosen_from, obs_tile),
            (value_from, obs_value),
            (noise_from, obs_noise),
            (var_from, obs_var),
        )[at]
        return pltpu.make_async_copy(source, held, small_sem.at[at])

    for at in range(5):
        small(at).start()

    def start_middle(level, carry):
        for row in range(1, rows - 1):
            load(level, row).start()
        return carry

    def start_edges(level, carry):
        for row in (0, rows - 1):
            load(level, row).start()
        return carry

    lax.fori_loop(0, 2, start_middle, 0)

    def halo_up(level):
        return pltpu.make_async_remote_copy(
            src_ref=raw.at[level, rows],
            dst_ref=raw.at[level, 0],
            send_sem=halo_send.at[level, 0],
            recv_sem=halo_recv.at[level, 0],
            device_id=(me, lax.rem(tile + 1, tiles)),
            device_id_type=MESH,
        )

    def halo_down(level):
        return pltpu.make_async_remote_copy(
            src_ref=raw.at[level, 1],
            dst_ref=raw.at[level, rows + 1],
            send_sem=halo_send.at[level, 1],
            recv_sem=halo_recv.at[level, 1],
            device_id=(me, lax.rem(tile + tiles - 1, tiles)),
            device_id_type=MESH,
        )

    def to_relay(level, row, way, at):
        return pltpu.make_async_remote_copy(
            src_ref=raw.at[level, row],
            dst_ref=relayed,
            send_sem=halo_send.at[level, way],
            recv_sem=relay_recv,
            device_id=(me, at),
            device_id_type=MESH,
        )

    def from_relay(level, row, way, at):
        return pltpu.make_async_remote_copy(
            src_ref=relayed,
            dst_ref=raw.at[level, row],
            send_sem=relay_send,
            recv_sem=halo_recv.at[level, way],
            device_id=(me, at),
            device_id_type=MESH,
        )

    def pass_on():
        @pl.when(is_up_relay)
        def _():
            level = tile // 4
            to_relay(level, rows, 0, half - 1).wait_recv()
            from_relay(level, 0, 0, half).start()

        @pl.when(is_down_relay)
        def _():
            level = (tile - half) // 4
            to_relay(level, 1, 1, half).wait_recv()
            from_relay(level, rows + 1, 1, half - 1).start()

    def end_pass():
        @pl.when(is_up_relay)
        def _():
            from_relay(tile // 4, 0, 0, half).wait_send()

        @pl.when(is_down_relay)
        def _():
            from_relay((tile - half) // 4, rows + 1, 1, half - 1).wait_send()

    def send_edges(level, carry):
        for row in (0, rows - 1):
            load(level, row).wait()

        @pl.when((tile < tiles - 1) & (tile != half - 1))
        def _():
            halo_up(level).start()

        @pl.when((tile > 0) & (tile != half))
        def _():
            halo_down(level).start()

        if deeps > 1:

            @pl.when(tile == half - 1)
            def _():
                to_relay(level, rows, 0, up_relay(level)).start()

            @pl.when(tile == half)
            def _():
                to_relay(level, 1, 1, down_relay(level)).start()

        return carry

    lane = lax.broadcasted_iota(jnp.int32, (ntr, cols), 1)

    def mix_row(level, row):
        strength = horiz_mix[level, pl.ds(row, 1), :]
        for m in range(pair):
            own = raw[level, row + 1, m]
            west = jnp.where(lane == 0, own, pltpu.roll(own, 1, 1))
            east = jnp.where(lane == cols - 1, own, pltpu.roll(own, cols - 1, 1))
            laplace = raw[level, row, m] + raw[level, row + 2, m] + west + east - 4.0 * own
            mixed[level, row, m] = own + strength * laplace

    def mix_middle(level):
        for row in range(1, rows - 1):
            load(level, row).wait()

        def mix_one(row, carry):
            mix_row(level, row)
            return carry

        lax.fori_loop(QROWS, rows - QROWS, mix_one, 0)

    def mix_edges(level):
        @pl.when(tile > 0)
        def _():
            halo_up(level).wait_recv()

        @pl.when(tile == 0)
        def _():
            raw[level, 0] = raw[level, 1]

        @pl.when(tile < tiles - 1)
        def _():
            halo_down(level).wait_recv()

        @pl.when(tile == tiles - 1)
        def _():
            raw[level, rows + 1] = raw[level, rows]

        def mix_two(row, carry):
            mix_row(level, row)
            mix_row(level, rows - 1 - row)
            return carry

        lax.fori_loop(0, QROWS, mix_two, 0)

    def state_copy(piece, to, which):
        level, quarter = piece // quarters, lax.rem(piece, quarters)
        block = states.at[level, quarter, pl.ds(2 * me, 2)]
        return pltpu.make_async_remote_copy(
            src_ref=block,
            dst_ref=block,
            send_sem=state_send.at[piece, which],
            recv_sem=state_recv.at[piece, me],
            device_id=(to, tile),
            device_id_type=MESH,
        )

    for at in range(5):
        small(at).wait()
    same = lax.broadcasted_iota(jnp.int32, (ntr, ntr), 0) == lax.broadcasted_iota(
        jnp.int32, (ntr, ntr), 1
    )
    loss = jnp.sum(
        jnp.where(same, jnp.broadcast_to(remin[...], (ntr, ntr)), 0.0), axis=1, keepdims=True
    )
    loss = jnp.broadcast_to(loss, (ntr, cols))
    loss = jnp.concatenate([loss] * (QROWS * pair), axis=1)
    place_from = lax.broadcasted_iota(jnp.int32, (ntr, 3 * ntr), 0)
    place_to = lax.broadcasted_iota(jnp.int32, (ntr, 3 * ntr), 1)
    place = (lax.rem(place_to, ntr) == place_from).astype(F32)
    wide = jnp.dot(interaction[...], place, precision=HIGHEST, preferred_element_type=F32)
    wide_high = wide.astype(jnp.bfloat16).astype(F32)
    taken = jnp.where(place_to < 2 * ntr, wide_high, wide - wide_high).astype(jnp.bfloat16)

    flags = (sunlit[pl.ds(tile * rows // cols, 1), :] > 0).astype(F32)
    flag_lane = lax.broadcasted_iota(jnp.int32, (1, cols), 1)
    for row in range(rows):
        flag = jnp.where(flag_lane == lax.rem(tile * rows, cols) + row, flags, 0.0)
        lit[row : row + 1, :] = jnp.broadcast_to(
            jnp.sum(flag, axis=1, keepdims=True), (1, cols)
        )

    def grow(level, quarter):
        below, above = jnp.minimum(level + 1, levels - 1), jnp.maximum(level - 1, 0)
        light = 0.6 * jnp.exp(-0.4 * jnp.full((1, cols), level, jnp.int32).astype(F32))
        blocks, lights = [], []
        for r in range(QROWS):
            row = quarter * QROWS + r
            down_mix = vert_mix[jnp.minimum(level, levels - 2), pl.ds(row, 1), :]
            up_mix = vert_mix[above, pl.ds(row, 1), :]
            for m in range(pair):
                here = mixed[level, row, m]
                down = down_mix * (mixed[below, row, m] - here)
                up = up_mix * (here - mixed[above, row, m])
                blocks.append(here + down - up)
                lights.append(light * lit[pl.ds(row, 1), :])
        value = jnp.concatenate(blocks, axis=1)
        light = jnp.concatenate(lights, axis=1)
        for _ in range(NSUB):
            high = value.astype(jnp.bfloat16)
            low = (value - high.astype(F32)).astype(jnp.bfloat16)
            uptake = jnp.dot(
                taken, jnp.concatenate([high, low, high], axis=0), preferred_element_type=F32
            )
            value = value + (1.0 / NSUB) * (light * jnp.tanh(uptake) - loss * value)
        for r in range(QROWS):
            for m in range(pair):
                at = (r * pair + m) * cols
                states[level, quarter, 2 * me + m, r] = value[:, at : at + cols]

    def send(level, quarter):
        piece = level * quarters + quarter
        state_copy(piece, across, 0).start()

        @pl.when(outer)
        def _():
            state_copy(piece, near, 1).start()

    lax.fori_loop(0, levels, start_edges, 0)
    lax.fori_loop(2, levels, start_middle, 0)

    @pl.when(inner)
    def _():
        for at in range(5, 10):
            small(at).start()

    mix_middle(0)
    mix_middle(1)
    grow(0, 1)

    peers = 3 + (tile > 0).astype(jnp.int32) + (tile < tiles - 1).astype(jnp.int32)
    peers += jnp.where(inner, mids + deeps + GROUP - 3, 0)
    if deeps > 1:
        peers += (is_up_relay | is_down_relay).astype(jnp.int32)
        peers += jnp.where((tile == half - 1) | (tile == half), levels, 0)
    pl.semaphore_wait(barrier, peers)

    send(0, 1)
    for quarter in range(2, quarters - 1):
        grow(0, quarter)
        send(0, quarter)
    lax.fori_loop(0, levels, send_edges, 0)

    if levels > 2:
        mix_middle(2)

    for quarter in range(1, quarters - 1):
        grow(1, quarter)
        send(1, quarter)
    if deeps > 1:
        pass_on()
    mix_edges(0)
    mix_edges(1)
    for quarter in (0, quarters - 1):
        grow(0, quarter)
        send(0, quarter)

    def step_level(level, carry):
        @pl.when(level < levels - 1)
        def _():
            mix_middle(level + 1)

        for quarter in range(1, quarters - 1):
            grow(level, quarter)
            send(level, quarter)
        mix_edges(level)
        for quarter in (0, quarters - 1):
            grow(level - 1, quarter)
            send(level - 1, quarter)
        return carry

    lax.fori_loop(2, levels, step_level, 0)
    for quarter in (0, quarters - 1):
        grow(levels - 1, quarter)
        send(levels - 1, quarter)

    def in_order(step):
        later = step - 2
        level, turn = 1 + later // 4, lax.rem(later, 4)
        piece = jnp.where(
            turn < 2, level * quarters + 1 + turn, (level - 1) * quarters + 3 * (turn - 2)
        )
        piece = jnp.where(step < 2, 1 + step, piece)
        ending = step - (pieces - 2)
        return jnp.where(ending < 0, piece, (levels - 1) * quarters + 3 * ending)

    def wait_states(piece):
        level, quarter = piece // quarters, lax.rem(piece, quarters)
        for j in range(1, 4):
            source = lax.rem(me + j, 4)
            block = states.at[level, quarter, pl.ds(2 * source, 2)]
            pltpu.make_async_remote_copy(
                src_ref=block,
                dst_ref=block,
                send_sem=state_send.at[piece, 0],
                recv_sem=state_recv.at[piece, source],
                device_id=(source, tile),
                device_id_type=MESH,
            ).wait_recv()

    def result_copy(piece):
        return pltpu.make_async_remote_copy(
            src_ref=passed.at[piece],
            dst_ref=results.at[piece],
            send_sem=result_send.at[piece],
            recv_sem=result_recv.at[piece],
            device_id=(beside, tile),
            device_id_type=MESH,
        )

    def stores(piece):
        level, quarter = piece // quarters, lax.rem(piece, quarters)
        return [
            pltpu.make_async_copy(
                results.at[piece, r],
                out.at[:, :, level, quarter * QROWS + r],
                store_sem.at[piece, r],
            )
            for r in range(QROWS)
        ]

    def small_copy(source, target, send, recv, at):
        return pltpu.make_async_remote_copy(
            src_ref=source,
            dst_ref=target,
            send_sem=send,
            recv_sem=recv,
            device_id=(me, at),
            device_id_type=MESH,
        )

    def partial_sums():
        for quarter in range(quarters):
            for r in range(QROWS):
                for m in range(members):
                    at = (quarter * QROWS + r) * members + m
                    surface[at : at + 1, :] = states[0, quarter, m, r, 0:1, :]
        picked_from = surface[...]
        width = OBS_STEP // cols
        column_ids = lax.broadcasted_iota(jnp.int32, (cols, OBS_STEP), 0)
        tile_ids = lax.broadcasted_iota(jnp.int32, (tiles, OBS_STEP), 0)

        def flat(ref, step):
            return jnp.concatenate(
                [ref[pl.ds(step * width + i, 1), :] for i in range(width)], axis=1
            )

        def step_obs(step, total):
            local = flat(obs_cell, step) - tile * (rows * cols)
            column = jnp.bitwise_and(local, cols - 1)
            row_of = jnp.right_shift(local, cols.bit_length() - 1)
            one_hot = (column_ids == column).astype(F32)
            picked = jnp.dot(
                picked_from, one_hot, precision=HIGHEST, preferred_element_type=F32
            )
            observed = jnp.zeros((members, OBS_STEP), F32)
            for r in range(rows):
                observed += jnp.where(
                    row_of == r, picked[r * members : (r + 1) * members], 0.0
                )
            inside = (row_of >= 0) & (row_of < rows)
            weight = jnp.where(inside, 1.0 / flat(obs_var, step), 0.0)
            spread = observed - jnp.sum(observed, axis=0, keepdims=True) * (1.0 / members)
            noise = obs_noise[:, pl.ds(pl.multiple_of(step * OBS_STEP, OBS_STEP), OBS_STEP)]
            innov = flat(obs_value, step) + noise - observed
            scaled = spread * weight
            both = jnp.concatenate([spread, innov], axis=0)
            products = jnp.concatenate(
                [scaled[a : a + 1] * both for a in range(members)], axis=0
            )
            chosen = (tile_ids == flat(obs_tile, step)).astype(F32)
            return total + lax.dot_general(
                chosen,
                products,
                (((1,), (1,)), ((), ())),
                precision=HIGHEST,
                preferred_element_type=F32,
            )

        steps = obs_noise.shape[1] // OBS_STEP
        total = lax.fori_loop(0, steps, step_obs, jnp.zeros((tiles, 128), F32))
        for d in range(deeps):
            for b in range(mids):
                at = (d * mids + b) * GROUP
                partial[b, d] = total[at : at + GROUP]

        copies = []
        for j in range(1, mids):
            other = lax.rem(mid_at + j, mids)
            copies.append(
                small_copy(
                    partial.at[other],
                    recv_mid.at[mid_at],
                    mid_send.at[j],
                    mid_recv.at[mid_at],
                    mid_tile(j),
                )
            )
        for copy in copies:
            copy.start()
        sums = partial[mid_at]
        for j in range(1, mids):
            other = lax.rem(mid_at + j, mids)
            small_copy(
                recv_mid.at[other],
                recv_mid.at[other],
                mid_send.at[j],
                mid_recv.at[other],
                mid_tile(j),
            ).wait_recv()
            sums = sums + recv_mid[other]
        held_mid[...] = sums
        for j in range(1, deeps):
            other = lax.rem(deep_at + j, deeps)
            copies.append(
                small_copy(
                    held_mid.at[other],
                    recv_deep.at[deep_at],
                    deep_send.at[j],
                    deep_recv.at[deep_at],
                    deep_tile(j),
                )
            )
            copies[-1].start()
        sums = held_mid[deep_at]
        for j in range(1, deeps):
            other = lax.rem(deep_at + j, deeps)
            small_copy(
                recv_deep.at[other],
                recv_deep.at[other],
                deep_send.at[j],
                deep_recv.at[other],
                deep_tile(j),
            ).wait_recv()
            sums = sums + recv_deep[other]
        held_group[...] = sums
        for j in range(1, GROUP):
            copies.append(
                small_copy(
                    held_group,
                    recv_group.at[group_at],
                    group_send.at[j],
                    group_recv.at[group_at],
                    group_tile(j),
                )
            )
            copies[-1].start()
        for j in range(1, GROUP):
            other = lax.rem(group_at + j, GROUP)
            small_copy(
                held_group,
                recv_group.at[other],
                group_send.at[j],
                group_recv.at[other],
                group_tile(j),
            ).wait_recv()
            sums = sums + recv_group[other]
        for copy in copies:
            copy.wait_send()
        return sums

    def weights_of(sums):
        sub = lax.broadcasted_iota(jnp.int32, (8, 128), 0)
        lane8 = lax.broadcasted_iota(jnp.int32, (8, 128), 1)
        own = jnp.sum(jnp.where(sub == group_at, sums, 0.0), axis=0, keepdims=True)
        parts = jnp.where(
            jnp.right_shift(lane8, 4) == sub, jnp.broadcast_to(own, (8, 128)), 0.0
        )
        fold_from = lax.broadcasted_iota(jnp.int32, (128, 128), 0)
        fold_to = lax.broadcasted_iota(jnp.int32, (128, 128), 1)
        fold = (jnp.bitwise_and(fold_from, 15) == fold_to).astype(F32)
        system = jnp.dot(parts, fold, precision=HIGHEST, preferred_element_type=F32)
        system = system + jnp.where(lane8 == sub, float(members - 1), 0.0)
        for k in range(members):
            column = jnp.sum(jnp.where(lane8 == k, system, 0.0), axis=1, keepdims=True)
            pivot = system[k : k + 1] / column[k : k + 1]
            system = jnp.where(sub == k, pivot, system - column * pivot)
        return system - jnp.sum(system, axis=0, keepdims=True) * (1.0 / members)

    def spread_weights(centered):
        sub = lax.broadcasted_iota(jnp.int32, (8, 128), 0)
        lane8 = lax.broadcasted_iota(jnp.int32, (8, 128), 1)
        for j in range(4):
            member = 2 * me + j if j < 2 else 2 * beside + j - 2
            column = jnp.sum(
                jnp.where(lane8 == members + member, centered, 0.0), axis=1, keepdims=True
            )
            wide = jnp.broadcast_to(column, (8, 128))
            wide = wide + jnp.where(sub == member, 1.0, 0.0)
            for k in range(members):
                splats[j, k] = jnp.broadcast_to(wide[k : k + 1], (8, 128))

    def analyse(piece):
        level, quarter = piece // quarters, lax.rem(piece, quarters)

        def analyse_part(at, carry):
            r, first = at // (ntr // 8), pl.multiple_of(lax.rem(at, ntr // 8) * 8, 8)
            sums = [None] * 4
            for k in range(members):
                value = states[level, quarter, k, r, pl.ds(first, 8), :]
                for j in range(4):
                    term = value * splats[j, k]
                    sums[j] = term if k == 0 else sums[j] + term
            for m in range(pair):
                results[piece, r, m, pl.ds(first, 8), :] = sums[m]
                passed[piece, r, m, pl.ds(first, 8), :] = sums[2 + m]
            return carry

        lax.fori_loop(0, QROWS * (ntr // 8), analyse_part, 0)
        result_copy(piece).start()
        for store in stores(piece):
            store.start()

    def settle(piece):
        state_copy(piece, across, 0).wait_send()

        @pl.when(outer)
        def _():
            state_copy(piece, near, 1).wait_send()

        @pl.when(inner)
        def _():
            result_copy(piece).wait_send()

        for store in stores(piece):
            store.wait()

    def finish_level(level, carry):
        @pl.when(tile < tiles - 1)
        def _():
            halo_up(level).wait_send()

        @pl.when(tile > 0)
        def _():
            halo_down(level).wait_send()

        return carry

    lax.fori_loop(0, levels, finish_level, 0)
    if deeps > 1:
        end_pass()

    @pl.when(inner)
    def _():
        for at in range(5, 10):
            small(at).wait()
        for quarter in range(1, quarters - 1):
            wait_states(quarter)
        for quarter in (0, quarters - 1):
            wait_states(quarter)
        spread_weights(weights_of(partial_sums()))

        def analyse_next(step, carry):
            piece = in_order(step)

            @pl.when(piece >= quarters)
            def _():
                wait_states(piece)

            analyse(piece)

            @pl.when(step >= LAG)
            def _():
                settle(in_order(step - LAG))

            return carry

        lax.fori_loop(0, pieces, analyse_next, 0)

    @pl.when(outer)
    def _():
        def take(step, carry):
            piece = in_order(step)
            result_copy(piece).wait_recv()
            for store in stores(piece):
                store.start()

            @pl.when(step >= LAG)
            def _():
                settle(in_order(step - LAG))

            return carry

        lax.fori_loop(0, pieces, take, 0)

    def finish(step, carry):
        settle(in_order(step))
        return carry

    lax.fori_loop(pieces - LAG, pieces, finish, 0)


def on_device(
    tracers,
    horiz_mix,
    vert_mix,
    sunlit,
    interaction,
    remin,
    obs_cell,
    obs_tile,
    obs_value,
    obs_noise,
    obs_var,
):
    pair, ntr, levels, rows, cols = tracers.shape
    tiles = lax.axis_size("space")
    deeps = DEEP if tiles > GROUP else 1
    mids = tiles // (deeps * GROUP)
    quarters = rows // QROWS
    pieces = levels * quarters
    count = obs_cell.shape[0]
    obs_rows = (count // cols, cols)
    pinned = pl.BlockSpec(memory_space=pltpu.HBM)
    anywhere = pl.BlockSpec(memory_space=pl.ANY)
    dma = pltpu.SemaphoreType.DMA
    operands = (
        tracers,
        horiz_mix,
        vert_mix,
        sunlit.reshape(-1, cols),
        interaction,
        remin.reshape(1, ntr),
        obs_cell.reshape(obs_rows),
        obs_tile.reshape(obs_rows),
        obs_value.reshape(obs_rows),
        obs_noise,
        obs_var.reshape(obs_rows),
    )
    operands = [pltpu.with_memory_space_constraint(value, pltpu.HBM) for value in operands]
    return pl.pallas_call(
        functools.partial(kernel, (tiles, mids, deeps)),
        out_shape=jax.ShapeDtypeStruct(tracers.shape, F32),
        in_specs=[pinned] * len(operands),
        out_specs=anywhere,
        scratch_shapes=[
            *[pltpu.VMEM(value.shape, value.dtype) for value in operands[1:]],
            pltpu.VMEM((rows, cols), F32),
            pltpu.VMEM((pair, ntr, cols), F32),
            pltpu.VMEM((levels, rows + 2, pair, ntr, cols), F32),
            pltpu.VMEM((levels, rows, pair, ntr, cols), F32),
            pltpu.VMEM((levels, quarters, 8, QROWS, ntr, cols), F32),
            pltpu.VMEM((pieces, QROWS, pair, ntr, cols), F32),
            pltpu.VMEM((pieces, QROWS, pair, ntr, cols), F32),
            pltpu.VMEM((rows * 8, cols), F32),
            pltpu.VMEM((mids, deeps, GROUP, 128), F32),
            pltpu.VMEM((mids, deeps, GROUP, 128), F32),
            pltpu.VMEM((deeps, GROUP, 128), F32),
            pltpu.VMEM((deeps, GROUP, 128), F32),
            pltpu.VMEM((GROUP, 128), F32),
            pltpu.VMEM((GROUP, GROUP, 128), F32),
            pltpu.VMEM((4, 8, 8, 128), F32),
            dma((10,)),
            dma((levels, rows)),
            dma,
            dma,
            dma((levels, 2)),
            dma((levels, 2)),
            dma((pieces, 2)),
            dma((pieces, 4)),
            dma((pieces,)),
            dma((pieces,)),
            dma((pieces, QROWS)),
            dma((mids,)),
            dma((mids,)),
            dma((deeps,)),
            dma((deeps,)),
            dma((GROUP,)),
            dma((GROUP,)),
        ],
        compiler_params=pltpu.CompilerParams(
            collective_id=0, has_side_effects=True, vmem_limit_bytes=VMEM_BYTES
        ),
        cost_estimate=pl.CostEstimate(
            flops=500_000_000, bytes_accessed=8_000_000, transcendentals=3_000_000
        ),
        name="step_and_analysis",
    )(*operands)


def solution(mesh):
    return jax.shard_map(
        on_device,
        mesh=mesh,
        in_specs=(
            P("member", None, None, "space", None),
            P(None, "space", None),
            P(None, "space", None),
            P(),
            P(),
            P(),
            P(),
            P(),
            P(),
            P(),
            P(),
        ),
        out_specs=P("member", None, None, "space", None),
        check_vma=False,
    )
```

```python
import functools

import jax
import jax.numpy as jnp
from jax import lax
from jax.experimental import pallas as pl
from jax.experimental.pallas import tpu as pltpu
from jax.sharding import PartitionSpec as P

NSUB = 4
GROUP = 8
DEEP = 2
QROWS = 2
VMEM_BYTES = 34 * 1024 * 1024
OBS_STEP = 512
F32 = jnp.float32
MESH = pl.DeviceIdType.MESH
HIGHEST = lax.Precision.HIGHEST


def kernel(
    sizes,
    tracers,
    horiz_from,
    vert_from,
    sunlit_from,
    interaction_from,
    remin_from,
    cell_from,
    chosen_from,
    value_from,
    noise_from,
    var_from,
    out,
    horiz_mix,
    vert_mix,
    sunlit,
    interaction,
    remin,
    obs_cell,
    obs_tile,
    obs_value,
    obs_noise,
    obs_var,
    lit,
    relayed,
    raw,
    mixed,
    states,
    results,
    passed,
    surface,
    partial,
    recv_mid,
    held_group,
    recv_group,
    held_deep,
    recv_deep,
    splats,
    small_sem,
    load_sem,
    edge_sem,
    relay_send,
    relay_recv,
    halo_send,
    halo_recv,
    state_send,
    piece_recv,
    result_send,
    store_sem,
    mid_sem,
    group_sem,
    deep_sem,
):
    tiles, mids, deeps = sizes
    ntr, levels, rows, cols = tracers.shape[1:]
    pair, quarters = 2, rows // QROWS
    members = 8
    pieces = levels * quarters
    me = lax.axis_index("member")
    tile = lax.axis_index("space")
    inner = (me == 1) | (me == 2)
    outer = jnp.logical_not(inner)
    group_at = lax.rem(tile, GROUP)
    mid_at = lax.rem(tile // GROUP, mids)
    deep_at = tile // (GROUP * mids)
    half = tiles // 2
    even = lax.rem(tile, 2) == 0
    other_half = lax.rem(tile + half, tiles)
    linked_up, linked_down = tile < tiles - 1, tile > 0
    if deeps > 1:
        linked_up, linked_down = linked_up & (tile != half - 1), linked_down & (tile != half)
    is_up_relay = (tile < half) & (lax.rem(tile, 4) == 2)
    is_down_relay = (tile >= half) & (lax.rem(tile, 4) == 1)

    def up_relay(level):
        return 4 * level + 2

    def down_relay(level):
        return half + 4 * level + 1

    near = jnp.where(me == 0, 1, 2)
    beside = jnp.where(me == 1, 0, 3)
    across = jnp.where(inner, 3 - me, jnp.where(me == 0, 2, 1))

    def mid_tile(j):
        return (deep_at * mids + lax.rem(mid_at + j, mids)) * GROUP + group_at

    def group_tile(j):
        return (deep_at * mids + mid_at) * GROUP + lax.rem(group_at + j, GROUP)

    def load(level, row, sem):
        return pltpu.make_async_copy(tracers.at[:, :, level, row], raw.at[level, row + 1], sem)

    barrier = pltpu.get_barrier_semaphore()
    for j in range(1, 4):
        pl.semaphore_signal(
            barrier, 1, device_id=(lax.rem(me + j, 4), tile), device_id_type=MESH
        )

    @pl.when(linked_down)
    def _():
        pl.semaphore_signal(barrier, 1, device_id=(me, tile - 1), device_id_type=MESH)

    @pl.when(linked_up)
    def _():
        pl.semaphore_signal(barrier, 1, device_id=(me, tile + 1), device_id_type=MESH)

    @pl.when(inner)
    def _():
        for j in range(1, mids):
            pl.semaphore_signal(barrier, 1, device_id=(me, mid_tile(j)), device_id_type=MESH)
        for j in range(1, GROUP):
            pl.semaphore_signal(barrier, 1, device_id=(me, group_tile(j)), device_id_type=MESH)

    if deeps > 1:

        @pl.when(inner & even)
        def _():
            pl.semaphore_signal(barrier, 1, device_id=(me, other_half), device_id_type=MESH)

        @pl.when(tile == half - 1)
        def _():
            for level in range(levels):
                pl.semaphore_signal(
                    barrier, 1, device_id=(me, down_relay(level)), device_id_type=MESH
                )

        @pl.when(tile == half)
        def _():
            for level in range(levels):
                pl.semaphore_signal(
                    barrier, 1, device_id=(me, up_relay(level)), device_id_type=MESH
                )

        @pl.when(is_up_relay)
        def _():
            pl.semaphore_signal(barrier, 1, device_id=(me, half - 1), device_id_type=MESH)

        @pl.when(is_down_relay)
        def _():
            pl.semaphore_signal(barrier, 1, device_id=(me, half), device_id_type=MESH)

    def small(at):
        source, held = (
            (interaction_from, interaction),
            (remin_from, remin),
            (sunlit_from, sunlit),
            (horiz_from, horiz_mix),
            (vert_from, vert_mix),
            (cell_from, obs_cell),
            (chosen_from, obs_tile),
            (value_from, obs_value),
            (noise_from, obs_noise),
            (var_from, obs_var),
        )[at]
        return pltpu.make_async_copy(source, held, small_sem.at[at])

    for at in range(5):
        small(at).start()

    def start_middle(level, carry):
        for row in range(1, rows - 1):
            load(level, row, load_sem.at[level]).start()
        return carry

    def start_edges(level, carry):
        for end in range(2):
            load(level, end * (rows - 1), edge_sem.at[level, end]).start()
        return carry

    lax.fori_loop(0, 2, start_middle, 0)

    def halo_up(level):
        return pltpu.make_async_remote_copy(
            src_ref=raw.at[level, rows],
            dst_ref=raw.at[level, 0],
            send_sem=halo_send.at[0],
            recv_sem=halo_recv.at[level, 0],
            device_id=(me, lax.rem(tile + 1, tiles)),
            device_id_type=MESH,
        )

    def halo_down(level):
        return pltpu.make_async_remote_copy(
            src_ref=raw.at[level, 1],
            dst_ref=raw.at[level, rows + 1],
            send_sem=halo_send.at[1],
            recv_sem=halo_recv.at[level, 1],
            device_id=(me, lax.rem(tile + tiles - 1, tiles)),
            device_id_type=MESH,
        )

    def to_relay(level, row, way, at):
        return pltpu.make_async_remote_copy(
            src_ref=raw.at[level, row],
            dst_ref=relayed,
            send_sem=halo_send.at[way],
            recv_sem=relay_recv,
            device_id=(me, at),
            device_id_type=MESH,
        )

    def from_relay(level, row, way, at):
        return pltpu.make_async_remote_copy(
            src_ref=relayed,
            dst_ref=raw.at[level, row],
            send_sem=relay_send,
            recv_sem=halo_recv.at[level, way],
            device_id=(me, at),
            device_id_type=MESH,
        )

    def pass_on():
        @pl.when(is_up_relay)
        def _():
            level = tile // 4
            to_relay(level, rows, 0, half - 1).wait_recv()
            from_relay(level, 0, 0, half).start()

        @pl.when(is_down_relay)
        def _():
            level = (tile - half) // 4
            to_relay(level, 1, 1, half).wait_recv()
            from_relay(level, rows + 1, 1, half - 1).start()

    def end_pass():
        @pl.when(is_up_relay)
        def _():
            from_relay(tile // 4, 0, 0, half).wait_send()

        @pl.when(is_down_relay)
        def _():
            from_relay((tile - half) // 4, rows + 1, 1, half - 1).wait_send()

    def send_edges(level, carry):
        for end in range(2):
            load(level, end * (rows - 1), edge_sem.at[level, end]).wait()

        @pl.when(linked_up)
        def _():
            halo_up(level).start()

        @pl.when(linked_down)
        def _():
            halo_down(level).start()

        if deeps > 1:

            @pl.when(tile == half - 1)
            def _():
                to_relay(level, rows, 0, up_relay(level)).start()

            @pl.when(tile == half)
            def _():
                to_relay(level, 1, 1, down_relay(level)).start()

        return carry

    lane = lax.broadcasted_iota(jnp.int32, (ntr, cols), 1)

    def mix_row(level, row):
        strength = horiz_mix[level, pl.ds(row, 1), :]
        for m in range(pair):
            own = raw[level, row + 1, m]
            west = jnp.where(lane == 0, own, pltpu.roll(own, 1, 1))
            east = jnp.where(lane == cols - 1, own, pltpu.roll(own, cols - 1, 1))
            laplace = raw[level, row, m] + raw[level, row + 2, m] + west + east - 4.0 * own
            mixed[level, row, m] = own + strength * laplace

    def mix_middle(level):
        middle = raw.at[level, pl.ds(2, rows - 2)]
        pltpu.make_async_copy(middle, middle, load_sem.at[level]).wait()

        def mix_one(row, carry):
            mix_row(level, row)
            return carry

        lax.fori_loop(QROWS, rows - QROWS, mix_one, 0)

    def mix_edges(level):
        @pl.when(tile > 0)
        def _():
            halo_up(level).wait_recv()

        @pl.when(tile == 0)
        def _():
            raw[level, 0] = raw[level, 1]

        @pl.when(tile < tiles - 1)
        def _():
            halo_down(level).wait_recv()

        @pl.when(tile == tiles - 1)
        def _():
            raw[level, rows + 1] = raw[level, rows]

        def mix_two(row, carry):
            mix_row(level, row)
            mix_row(level, rows - 1 - row)
            return carry

        lax.fori_loop(0, QROWS, mix_two, 0)

    def state_copy(piece, to, which):
        level, quarter = piece // quarters, lax.rem(piece, quarters)
        block = states.at[level, quarter, pl.ds(2 * me, 2)]
        return pltpu.make_async_remote_copy(
            src_ref=block,
            dst_ref=block,
            send_sem=state_send.at[which],
            recv_sem=piece_recv.at[piece],
            device_id=(to, tile),
            device_id_type=MESH,
        )

    for at in range(5):
        small(at).wait()
    same = lax.broadcasted_iota(jnp.int32, (ntr, ntr), 0) == lax.broadcasted_iota(
        jnp.int32, (ntr, ntr), 1
    )
    loss = jnp.sum(
        jnp.where(same, jnp.broadcast_to(remin[...], (ntr, ntr)), 0.0), axis=1, keepdims=True
    )
    loss = jnp.broadcast_to(loss, (ntr, cols))
    loss = jnp.concatenate([loss] * (QROWS * pair), axis=1)
    place_from = lax.broadcasted_iota(jnp.int32, (ntr, 3 * ntr), 0)
    place_to = lax.broadcasted_iota(jnp.int32, (ntr, 3 * ntr), 1)
    place = (lax.rem(place_to, ntr) == place_from).astype(F32)
    wide = jnp.dot(interaction[...], place, precision=HIGHEST, preferred_element_type=F32)
    wide_high = wide.astype(jnp.bfloat16).astype(F32)
    taken = jnp.where(place_to < 2 * ntr, wide_high, wide - wide_high).astype(jnp.bfloat16)

    flags = (sunlit[pl.ds(tile * rows // cols, 1), :] > 0).astype(F32)
    flag_lane = lax.broadcasted_iota(jnp.int32, (1, cols), 1)
    for row in range(rows):
        flag = jnp.where(flag_lane == lax.rem(tile * rows, cols) + row, flags, 0.0)
        lit[row : row + 1, :] = jnp.broadcast_to(
            jnp.sum(flag, axis=1, keepdims=True), (1, cols)
        )

    def grow(level, quarter):
        below, above = jnp.minimum(level + 1, levels - 1), jnp.maximum(level - 1, 0)
        light = 0.6 * jnp.exp(-0.4 * jnp.full((1, cols), level, jnp.int32).astype(F32))
        blocks, lights = [], []
        for r in range(QROWS):
            row = quarter * QROWS + r
            down_mix = vert_mix[jnp.minimum(level, levels - 2), pl.ds(row, 1), :]
            up_mix = vert_mix[above, pl.ds(row, 1), :]
            for m in range(pair):
                here = mixed[level, row, m]
                down = down_mix * (mixed[below, row, m] - here)
                up = up_mix * (here - mixed[above, row, m])
                blocks.append(here + down - up)
                lights.append(light * lit[pl.ds(row, 1), :])
        value = jnp.concatenate(blocks, axis=1)
        light = jnp.concatenate(lights, axis=1)
        for _ in range(NSUB):
            high = value.astype(jnp.bfloat16)
            low = (value - high.astype(F32)).astype(jnp.bfloat16)
            uptake = jnp.dot(
                taken, jnp.concatenate([high, low, high], axis=0), preferred_element_type=F32
            )
            value = value + (1.0 / NSUB) * (light * jnp.tanh(uptake) - loss * value)
        for r in range(QROWS):
            for m in range(pair):
                at = (r * pair + m) * cols
                states[level, quarter, 2 * me + m, r] = value[:, at : at + cols]

    def send(level, quarter):
        piece = level * quarters + quarter
        state_copy(piece, across, 0).start()

        @pl.when(outer)
        def _():
            state_copy(piece, near, 1).start()

    lax.fori_loop(0, levels, start_edges, 0)
    lax.fori_loop(2, levels, start_middle, 0)

    @pl.when(inner)
    def _():
        for at in range(5, 10):
            small(at).start()

    mix_middle(0)
    mix_middle(1)
    grow(0, 1)

    peers = 3 + linked_up.astype(jnp.int32) + linked_down.astype(jnp.int32)
    peers += jnp.where(inner, mids + GROUP - 2, 0)
    if deeps > 1:
        peers += (inner & even).astype(jnp.int32)
        peers += (is_up_relay | is_down_relay).astype(jnp.int32)
        peers += jnp.where((tile == half - 1) | (tile == half), levels, 0)
    pl.semaphore_wait(barrier, peers)

    send(0, 1)
    for quarter in range(2, quarters - 1):
        grow(0, quarter)
        send(0, quarter)
    lax.fori_loop(0, levels, send_edges, 0)

    if levels > 2:
        mix_middle(2)

    for quarter in range(1, quarters - 1):
        grow(1, quarter)
        send(1, quarter)
    if deeps > 1:
        pass_on()
    mix_edges(0)
    mix_edges(1)
    for quarter in (0, quarters - 1):
        grow(0, quarter)
        send(0, quarter)

    def step_level(level, carry):
        @pl.when(level < levels - 1)
        def _():
            mix_middle(level + 1)

        for quarter in range(1, quarters - 1):
            grow(level, quarter)
            send(level, quarter)
        mix_edges(level)
        for quarter in (0, quarters - 1):
            grow(level - 1, quarter)
            send(level - 1, quarter)
        return carry

    lax.fori_loop(2, levels, step_level, 0)
    for quarter in (0, quarters - 1):
        grow(levels - 1, quarter)
        send(levels - 1, quarter)

    def in_order(step):
        later = step - 2
        level, turn = 1 + later // 4, lax.rem(later, 4)
        piece = jnp.where(
            turn < 2, level * quarters + 1 + turn, (level - 1) * quarters + 3 * (turn - 2)
        )
        piece = jnp.where(step < 2, 1 + step, piece)
        ending = step - (pieces - 2)
        return jnp.where(ending < 0, piece, (levels - 1) * quarters + 3 * ending)

    def sent(source, sem):
        pltpu.make_async_remote_copy(
            src_ref=source,
            dst_ref=source,
            send_sem=sem,
            recv_sem=sem,
            device_id=(3 - me, tile),
            device_id_type=MESH,
        ).wait_send()

    def landed(target, sem):
        pltpu.make_async_remote_copy(
            src_ref=target,
            dst_ref=target,
            send_sem=sem,
            recv_sem=sem,
            device_id=(3 - me, tile),
            device_id_type=MESH,
        ).wait_recv()

    def wait_states(piece):
        level, quarter = piece // quarters, lax.rem(piece, quarters)
        landed(states.at[level, quarter, pl.ds(0, members - pair)], piece_recv.at[piece])

    def result_copy(piece):
        return pltpu.make_async_remote_copy(
            src_ref=passed.at[piece],
            dst_ref=results.at[piece],
            send_sem=result_send,
            recv_sem=piece_recv.at[piece],
            device_id=(beside, tile),
            device_id_type=MESH,
        )

    def stores(piece):
        level, quarter = piece // quarters, lax.rem(piece, quarters)
        return [
            pltpu.make_async_copy(
                results.at[piece, r],
                out.at[:, :, level, quarter * QROWS + r],
                store_sem,
            )
            for r in range(QROWS)
        ]

    def small_copy(source, target, send, recv, at):
        return pltpu.make_async_remote_copy(
            src_ref=source,
            dst_ref=target,
            send_sem=send,
            recv_sem=recv,
            device_id=(me, at),
            device_id_type=MESH,
        )

    def partial_sums():
        for quarter in range(quarters):
            for r in range(QROWS):
                for m in range(members):
                    at = (quarter * QROWS + r) * members + m
                    surface[at : at + 1, :] = states[0, quarter, m, r, 0:1, :]
        picked_from = surface[...]
        width = OBS_STEP // cols
        column_ids = lax.broadcasted_iota(jnp.int32, (cols, OBS_STEP), 0)
        tile_ids = lax.broadcasted_iota(jnp.int32, (tiles, OBS_STEP), 0)

        def flat(ref, step):
            return jnp.concatenate(
                [ref[pl.ds(step * width + i, 1), :] for i in range(width)], axis=1
            )

        def step_obs(step, total):
            local = flat(obs_cell, step) - tile * (rows * cols)
            column = jnp.bitwise_and(local, cols - 1)
            row_of = jnp.right_shift(local, cols.bit_length() - 1)
            one_hot = (column_ids == column).astype(F32)
            picked = jnp.dot(
                picked_from, one_hot, precision=HIGHEST, preferred_element_type=F32
            )
            observed = jnp.zeros((members, OBS_STEP), F32)
            for r in range(rows):
                observed += jnp.where(
                    row_of == r, picked[r * members : (r + 1) * members], 0.0
                )
            inside = (row_of >= 0) & (row_of < rows)
            weight = jnp.where(inside, 1.0 / flat(obs_var, step), 0.0)
            spread = observed - jnp.sum(observed, axis=0, keepdims=True) * (1.0 / members)
            noise = obs_noise[:, pl.ds(pl.multiple_of(step * OBS_STEP, OBS_STEP), OBS_STEP)]
            innov = flat(obs_value, step) + noise - observed
            scaled = spread * weight
            both = jnp.concatenate([spread, innov], axis=0)
            products = jnp.concatenate(
                [scaled[a : a + 1] * both for a in range(members)], axis=0
            )
            chosen = (tile_ids == flat(obs_tile, step)).astype(F32)
            return total + lax.dot_general(
                chosen,
                products,
                (((1,), (1,)), ((), ())),
                precision=HIGHEST,
                preferred_element_type=F32,
            )

        steps = obs_noise.shape[1] // OBS_STEP
        total = lax.fori_loop(0, steps, step_obs, jnp.zeros((tiles, 128), F32))
        for d in range(deeps):
            for b in range(mids):
                at = (d * mids + b) * GROUP
                partial[b, d] = total[at : at + GROUP]

        sums = partial[mid_at]
        if mids > 1:
            for j in range(1, mids):
                small_copy(
                    partial.at[lax.rem(mid_at + j, mids)],
                    recv_mid.at[mid_at],
                    mid_sem.at[0],
                    mid_sem.at[1],
                    mid_tile(j),
                ).start()
            landed(recv_mid.at[pl.ds(0, mids - 1)], mid_sem.at[1])
            for j in range(1, mids):
                sums = sums + recv_mid[lax.rem(mid_at + j, mids)]
        held_group[...] = sums
        for j in range(1, GROUP):
            small_copy(
                held_group,
                recv_group.at[group_at],
                group_sem.at[0],
                group_sem.at[1],
                group_tile(j),
            ).start()
        landed(recv_group.at[pl.ds(0, GROUP - 1)], group_sem.at[1])
        for j in range(1, GROUP):
            sums = sums + recv_group[lax.rem(group_at + j, GROUP)]
        if mids > 1:
            sent(partial.at[pl.ds(0, mids - 1)], mid_sem.at[0])
        sent(recv_group.at[pl.ds(0, GROUP - 1)], group_sem.at[0])
        if deeps == 1:
            return sums[0]
        held_deep[...] = sums
        across_half = small_copy(
            held_deep.at[1 - deep_at], recv_deep, deep_sem.at[0], deep_sem.at[1], other_half
        )
        handed = small_copy(
            recv_deep, recv_deep, deep_sem.at[0], deep_sem.at[1], jnp.minimum(tile + 1, tiles - 1)
        )

        @pl.when(even)
        def _():
            across_half.start()
            across_half.wait()
            handed.start()
            handed.wait_send()

        @pl.when(jnp.logical_not(even))
        def _():
            handed.wait_recv()

        sums = held_deep[deep_at] + recv_deep[...]
        return sums

    def weights_of(sums):
        sub = lax.broadcasted_iota(jnp.int32, (8, 128), 0)
        lane8 = lax.broadcasted_iota(jnp.int32, (8, 128), 1)
        own = jnp.sum(jnp.where(sub == group_at, sums, 0.0), axis=0, keepdims=True)
        parts = jnp.where(
            jnp.right_shift(lane8, 4) == sub, jnp.broadcast_to(own, (8, 128)), 0.0
        )
        fold_from = lax.broadcasted_iota(jnp.int32, (128, 128), 0)
        fold_to = lax.broadcasted_iota(jnp.int32, (128, 128), 1)
        fold = (jnp.bitwise_and(fold_from, 15) == fold_to).astype(F32)
        system = jnp.dot(parts, fold, precision=HIGHEST, preferred_element_type=F32)
        system = system + jnp.where(lane8 == sub, float(members - 1), 0.0)
        for k in range(members):
            column = jnp.sum(jnp.where(lane8 == k, system, 0.0), axis=1, keepdims=True)
            pivot = system[k : k + 1] / column[k : k + 1]
            system = jnp.where(sub == k, pivot, system - column * pivot)
        return system - jnp.sum(system, axis=0, keepdims=True) * (1.0 / members)

    def spread_weights(centered):
        sub = lax.broadcasted_iota(jnp.int32, (8, 128), 0)
        lane8 = lax.broadcasted_iota(jnp.int32, (8, 128), 1)
        for j in range(4):
            member = 2 * me + j if j < 2 else 2 * beside + j - 2
            column = jnp.sum(
                jnp.where(lane8 == members + member, centered, 0.0), axis=1, keepdims=True
            )
            wide = jnp.broadcast_to(column, (8, 128))
            wide = wide + jnp.where(sub == member, 1.0, 0.0)
            for k in range(members):
                splats[j, k] = jnp.broadcast_to(wide[k : k + 1], (8, 128))

    def analyse(piece):
        level, quarter = piece // quarters, lax.rem(piece, quarters)

        def analyse_part(at, carry):
            r, first = at // (ntr // 8), pl.multiple_of(lax.rem(at, ntr // 8) * 8, 8)
            sums = [None] * 4
            for k in range(members):
                value = states[level, quarter, k, r, pl.ds(first, 8), :]
                for j in range(4):
                    term = value * splats[j, k]
                    sums[j] = term if k == 0 else sums[j] + term
            for m in range(pair):
                results[piece, r, m, pl.ds(first, 8), :] = sums[m]
                passed[piece, r, m, pl.ds(first, 8), :] = sums[2 + m]
            return carry

        lax.fori_loop(0, QROWS * (ntr // 8), analyse_part, 0)
        result_copy(piece).start()
        for store in stores(piece):
            store.start()

    own_states = states.at[:, :, pl.ds(2 * me, 2)]

    @pl.when(tile < tiles - 1)
    def _():
        sent(raw.at[:, rows], halo_send.at[0])

    @pl.when(tile > 0)
    def _():
        sent(raw.at[:, 1], halo_send.at[1])

    if deeps > 1:
        end_pass()

    @pl.when(inner)
    def _():
        for at in range(5, 10):
            small(at).wait()
        for quarter in range(1, quarters - 1):
            wait_states(quarter)
        for quarter in (0, quarters - 1):
            wait_states(quarter)
        spread_weights(weights_of(partial_sums()))

        def analyse_next(step, carry):
            piece = in_order(step)

            @pl.when(piece >= quarters)
            def _():
                wait_states(piece)

            analyse(piece)
            return carry

        lax.fori_loop(0, pieces, analyse_next, 0)
        sent(passed, result_send)
        sent(own_states, state_send.at[0])

    @pl.when(outer)
    def _():
        def take(step, carry):
            piece = in_order(step)
            result_copy(piece).wait_recv()
            for store in stores(piece):
                store.start()
            return carry

        lax.fori_loop(0, pieces, take, 0)
        sent(own_states, state_send.at[0])
        sent(own_states, state_send.at[1])

    pltpu.make_async_copy(results, results, store_sem).wait()


def on_device(
    tracers,
    horiz_mix,
    vert_mix,
    sunlit,
    interaction,
    remin,
    obs_cell,
    obs_tile,
    obs_value,
    obs_noise,
    obs_var,
):
    pair, ntr, levels, rows, cols = tracers.shape
    tiles = lax.axis_size("space")
    deeps = DEEP if tiles > GROUP else 1
    mids = tiles // (deeps * GROUP)
    quarters = rows // QROWS
    pieces = levels * quarters
    count = obs_cell.shape[0]
    obs_rows = (count // cols, cols)
    pinned = pl.BlockSpec(memory_space=pltpu.HBM)
    anywhere = pl.BlockSpec(memory_space=pl.ANY)
    dma = pltpu.SemaphoreType.DMA
    operands = (
        tracers,
        horiz_mix,
        vert_mix,
        sunlit.reshape(-1, cols),
        interaction,
        remin.reshape(1, ntr),
        obs_cell.reshape(obs_rows),
        obs_tile.reshape(obs_rows),
        obs_value.reshape(obs_rows),
        obs_noise,
        obs_var.reshape(obs_rows),
    )
    operands = [pltpu.with_memory_space_constraint(value, pltpu.HBM) for value in operands]
    return pl.pallas_call(
        functools.partial(kernel, (tiles, mids, deeps)),
        out_shape=jax.ShapeDtypeStruct(tracers.shape, F32),
        in_specs=[pinned] * len(operands),
        out_specs=anywhere,
        scratch_shapes=[
            *[pltpu.VMEM(value.shape, value.dtype) for value in operands[1:]],
            pltpu.VMEM((rows, cols), F32),
            pltpu.VMEM((pair, ntr, cols), F32),
            pltpu.VMEM((levels, rows + 2, pair, ntr, cols), F32),
            pltpu.VMEM((levels, rows, pair, ntr, cols), F32),
            pltpu.VMEM((levels, quarters, 8, QROWS, ntr, cols), F32),
            pltpu.VMEM((pieces, QROWS, pair, ntr, cols), F32),
            pltpu.VMEM((pieces, QROWS, pair, ntr, cols), F32),
            pltpu.VMEM((rows * 8, cols), F32),
            pltpu.VMEM((mids, deeps, GROUP, 128), F32),
            pltpu.VMEM((mids, deeps, GROUP, 128), F32),
            pltpu.VMEM((deeps, GROUP, 128), F32),
            pltpu.VMEM((GROUP, deeps, GROUP, 128), F32),
            pltpu.VMEM((deeps, GROUP, 128), F32),
            pltpu.VMEM((GROUP, 128), F32),
            pltpu.VMEM((4, 8, 8, 128), F32),
            dma((10,)),
            dma((levels,)),
            dma((levels, 2)),
            dma,
            dma,
            dma((2,)),
            dma((levels, 2)),
            dma((2,)),
            dma((pieces,)),
            dma,
            dma,
            dma((2,)),
            dma((2,)),
            dma((2,)),
        ],
        compiler_params=pltpu.CompilerParams(
            collective_id=0, has_side_effects=True, vmem_limit_bytes=VMEM_BYTES
        ),
        cost_estimate=pl.CostEstimate(
            flops=500_000_000, bytes_accessed=8_000_000, transcendentals=3_000_000
        ),
        name="step_and_analysis",
    )(*operands)


def solution(mesh):
    return jax.shard_map(
        on_device,
        mesh=mesh,
        in_specs=(
            P("member", None, None, "space", None),
            P(None, "space", None),
            P(None, "space", None),
            P(),
            P(),
            P(),
            P(),
            P(),
            P(),
            P(),
            P(),
        ),
        out_specs=P("member", None, None, "space", None),
        check_vma=False,
    )
```

```python
import functools

import jax
import jax.numpy as jnp
from jax import lax
from jax.experimental import pallas as pl
from jax.experimental.pallas import tpu as pltpu
from jax.sharding import PartitionSpec as P

NSUB = 4
GROUP = 8
DEEP = 2
TAIL = 2
AHEAD = 9
QROWS = 2
VMEM_BYTES = 34 * 1024 * 1024
OBS_STEP = 512
F32 = jnp.float32
MESH = pl.DeviceIdType.MESH
HIGHEST = lax.Precision.HIGHEST


def kernel(
    sizes,
    tracers,
    horiz_from,
    vert_from,
    sunlit_from,
    interaction_from,
    remin_from,
    cell_from,
    chosen_from,
    value_from,
    noise_from,
    var_from,
    out,
    horiz_mix,
    vert_mix,
    sunlit,
    interaction,
    remin,
    obs_cell,
    obs_tile,
    obs_value,
    obs_noise,
    obs_var,
    lit,
    relayed,
    raw,
    mixed,
    states,
    results,
    passed,
    surface,
    partial,
    recv_mid,
    held_group,
    recv_group,
    held_deep,
    recv_deep,
    splats,
    splats_across,
    tail_out,
    tail_in,
    small_sem,
    load_sem,
    edge_sem,
    relay_send,
    relay_recv,
    halo_send,
    halo_recv,
    state_send,
    piece_recv,
    result_send,
    store_sem,
    tail_sem,
    tail_recv,
    mid_sem,
    group_sem,
    deep_sem,
):
    tiles, mids, deeps = sizes
    ntr, levels, rows, cols = tracers.shape[1:]
    pair, quarters = 2, rows // QROWS
    members = 8
    pieces = levels * quarters
    steps = pieces - TAIL
    me = lax.axis_index("member")
    tile = lax.axis_index("space")
    inner = (me == 1) | (me == 2)
    outer = jnp.logical_not(inner)
    group_at = lax.rem(tile, GROUP)
    mid_at = lax.rem(tile // GROUP, mids)
    deep_at = tile // (GROUP * mids)
    half = tiles // 2
    even = lax.rem(tile, 2) == 0
    other_half = lax.rem(tile + half, tiles)
    linked_up, linked_down = tile < tiles - 1, tile > 0
    if deeps > 1:
        linked_up, linked_down = linked_up & (tile != half - 1), linked_down & (tile != half)
    is_up_relay = (tile < half) & (lax.rem(tile, 4) == 2)
    is_down_relay = (tile >= half) & (lax.rem(tile, 4) == 1)

    def up_relay(level):
        return 4 * level + 2

    def down_relay(level):
        return half + 4 * level + 1

    near = jnp.where(me == 0, 1, 2)
    beside = jnp.where(me == 1, 0, 3)
    across = jnp.where(inner, 3 - me, jnp.where(me == 0, 2, 1))

    def mid_tile(j):
        return (deep_at * mids + lax.rem(mid_at + j, mids)) * GROUP + group_at

    def group_tile(j):
        return (deep_at * mids + mid_at) * GROUP + lax.rem(group_at + j, GROUP)

    def load(level, row, sem):
        return pltpu.make_async_copy(tracers.at[:, :, level, row], raw.at[level, row + 1], sem)

    barrier = pltpu.get_barrier_semaphore()
    for j in range(1, 4):
        pl.semaphore_signal(
            barrier, 1, device_id=(lax.rem(me + j, 4), tile), device_id_type=MESH
        )

    @pl.when(linked_down)
    def _():
        pl.semaphore_signal(barrier, 1, device_id=(me, tile - 1), device_id_type=MESH)

    @pl.when(linked_up)
    def _():
        pl.semaphore_signal(barrier, 1, device_id=(me, tile + 1), device_id_type=MESH)

    @pl.when(inner)
    def _():
        for j in range(1, mids):
            pl.semaphore_signal(barrier, 1, device_id=(me, mid_tile(j)), device_id_type=MESH)
        for j in range(1, GROUP):
            pl.semaphore_signal(barrier, 1, device_id=(me, group_tile(j)), device_id_type=MESH)

    if deeps > 1:

        @pl.when(inner & even)
        def _():
            pl.semaphore_signal(barrier, 1, device_id=(me, other_half), device_id_type=MESH)

        @pl.when(tile == half - 1)
        def _():
            for level in range(levels):
                pl.semaphore_signal(
                    barrier, 1, device_id=(me, down_relay(level)), device_id_type=MESH
                )

        @pl.when(tile == half)
        def _():
            for level in range(levels):
                pl.semaphore_signal(
                    barrier, 1, device_id=(me, up_relay(level)), device_id_type=MESH
                )

        @pl.when(is_up_relay)
        def _():
            pl.semaphore_signal(barrier, 1, device_id=(me, half - 1), device_id_type=MESH)

        @pl.when(is_down_relay)
        def _():
            pl.semaphore_signal(barrier, 1, device_id=(me, half), device_id_type=MESH)

    def small(at):
        source, held = (
            (interaction_from, interaction),
            (remin_from, remin),
            (sunlit_from, sunlit),
            (horiz_from, horiz_mix),
            (vert_from, vert_mix),
            (cell_from, obs_cell),
            (chosen_from, obs_tile),
            (value_from, obs_value),
            (noise_from, obs_noise),
            (var_from, obs_var),
        )[at]
        return pltpu.make_async_copy(source, held, small_sem.at[at])

    for at in range(5):
        small(at).start()

    def start_middle(level, carry):
        for row in range(1, rows - 1):
            load(level, row, load_sem.at[level]).start()
        return carry

    def start_edges(level, carry):
        for end in range(2):
            load(level, end * (rows - 1), edge_sem.at[level, end]).start()
        return carry

    lax.fori_loop(0, 2, start_middle, 0)

    def halo_up(level):
        return pltpu.make_async_remote_copy(
            src_ref=raw.at[level, rows],
            dst_ref=raw.at[level, 0],
            send_sem=halo_send.at[0],
            recv_sem=halo_recv.at[level, 0],
            device_id=(me, lax.rem(tile + 1, tiles)),
            device_id_type=MESH,
        )

    def halo_down(level):
        return pltpu.make_async_remote_copy(
            src_ref=raw.at[level, 1],
            dst_ref=raw.at[level, rows + 1],
            send_sem=halo_send.at[1],
            recv_sem=halo_recv.at[level, 1],
            device_id=(me, lax.rem(tile + tiles - 1, tiles)),
            device_id_type=MESH,
        )

    def to_relay(level, row, way, at):
        return pltpu.make_async_remote_copy(
            src_ref=raw.at[level, row],
            dst_ref=relayed,
            send_sem=halo_send.at[way],
            recv_sem=relay_recv,
            device_id=(me, at),
            device_id_type=MESH,
        )

    def from_relay(level, row, way, at):
        return pltpu.make_async_remote_copy(
            src_ref=relayed,
            dst_ref=raw.at[level, row],
            send_sem=relay_send,
            recv_sem=halo_recv.at[level, way],
            device_id=(me, at),
            device_id_type=MESH,
        )

    def pass_on():
        @pl.when(is_up_relay)
        def _():
            level = tile // 4
            to_relay(level, rows, 0, half - 1).wait_recv()
            from_relay(level, 0, 0, half).start()

        @pl.when(is_down_relay)
        def _():
            level = (tile - half) // 4
            to_relay(level, 1, 1, half).wait_recv()
            from_relay(level, rows + 1, 1, half - 1).start()

    def end_pass():
        @pl.when(is_up_relay)
        def _():
            from_relay(tile // 4, 0, 0, half).wait_send()

        @pl.when(is_down_relay)
        def _():
            from_relay((tile - half) // 4, rows + 1, 1, half - 1).wait_send()

    def send_edges(level, carry):
        for end in range(2):
            load(level, end * (rows - 1), edge_sem.at[level, end]).wait()

        @pl.when(linked_up)
        def _():
            halo_up(level).start()

        @pl.when(linked_down)
        def _():
            halo_down(level).start()

        if deeps > 1:

            @pl.when(tile == half - 1)
            def _():
                to_relay(level, rows, 0, up_relay(level)).start()

            @pl.when(tile == half)
            def _():
                to_relay(level, 1, 1, down_relay(level)).start()

        return carry

    lane = lax.broadcasted_iota(jnp.int32, (ntr, cols), 1)

    def mix_row(level, row):
        strength = horiz_mix[level, pl.ds(row, 1), :]
        for m in range(pair):
            own = raw[level, row + 1, m]
            west = jnp.where(lane == 0, own, pltpu.roll(own, 1, 1))
            east = jnp.where(lane == cols - 1, own, pltpu.roll(own, cols - 1, 1))
            laplace = raw[level, row, m] + raw[level, row + 2, m] + west + east - 4.0 * own
            mixed[level, row, m] = own + strength * laplace

    def mix_middle(level):
        middle = raw.at[level, pl.ds(2, rows - 2)]
        pltpu.make_async_copy(middle, middle, load_sem.at[level]).wait()

        def mix_one(row, carry):
            mix_row(level, row)
            return carry

        lax.fori_loop(QROWS, rows - QROWS, mix_one, 0)

    def mix_edges(level):
        @pl.when(tile > 0)
        def _():
            halo_up(level).wait_recv()

        @pl.when(tile == 0)
        def _():
            raw[level, 0] = raw[level, 1]

        @pl.when(tile < tiles - 1)
        def _():
            halo_down(level).wait_recv()

        @pl.when(tile == tiles - 1)
        def _():
            raw[level, rows + 1] = raw[level, rows]

        def mix_two(row, carry):
            mix_row(level, row)
            mix_row(level, rows - 1 - row)
            return carry

        lax.fori_loop(0, QROWS, mix_two, 0)

    def state_copy(piece, to, which):
        level, quarter = piece // quarters, lax.rem(piece, quarters)
        block = states.at[level, quarter, pl.ds(2 * me, 2)]
        return pltpu.make_async_remote_copy(
            src_ref=block,
            dst_ref=block,
            send_sem=state_send.at[which],
            recv_sem=piece_recv.at[piece],
            device_id=(to, tile),
            device_id_type=MESH,
        )

    for at in range(5):
        small(at).wait()
    same = lax.broadcasted_iota(jnp.int32, (ntr, ntr), 0) == lax.broadcasted_iota(
        jnp.int32, (ntr, ntr), 1
    )
    loss = jnp.sum(
        jnp.where(same, jnp.broadcast_to(remin[...], (ntr, ntr)), 0.0), axis=1, keepdims=True
    )
    loss = jnp.broadcast_to(loss, (ntr, cols))
    loss = jnp.concatenate([loss] * (QROWS * pair), axis=1)
    place_from = lax.broadcasted_iota(jnp.int32, (ntr, 3 * ntr), 0)
    place_to = lax.broadcasted_iota(jnp.int32, (ntr, 3 * ntr), 1)
    place = (lax.rem(place_to, ntr) == place_from).astype(F32)
    wide = jnp.dot(interaction[...], place, precision=HIGHEST, preferred_element_type=F32)
    wide_high = wide.astype(jnp.bfloat16).astype(F32)
    taken = jnp.where(place_to < 2 * ntr, wide_high, wide - wide_high).astype(jnp.bfloat16)

    flags = (sunlit[pl.ds(tile * rows // cols, 1), :] > 0).astype(F32)
    flag_lane = lax.broadcasted_iota(jnp.int32, (1, cols), 1)
    for row in range(rows):
        flag = jnp.where(flag_lane == lax.rem(tile * rows, cols) + row, flags, 0.0)
        lit[row : row + 1, :] = jnp.broadcast_to(
            jnp.sum(flag, axis=1, keepdims=True), (1, cols)
        )

    def grow(level, quarter):
        below, above = jnp.minimum(level + 1, levels - 1), jnp.maximum(level - 1, 0)
        light = 0.6 * jnp.exp(-0.4 * jnp.full((1, cols), level, jnp.int32).astype(F32))
        blocks, lights = [], []
        for r in range(QROWS):
            row = quarter * QROWS + r
            down_mix = vert_mix[jnp.minimum(level, levels - 2), pl.ds(row, 1), :]
            up_mix = vert_mix[above, pl.ds(row, 1), :]
            for m in range(pair):
                here = mixed[level, row, m]
                down = down_mix * (mixed[below, row, m] - here)
                up = up_mix * (here - mixed[above, row, m])
                blocks.append(here + down - up)
                lights.append(light * lit[pl.ds(row, 1), :])
        value = jnp.concatenate(blocks, axis=1)
        light = jnp.concatenate(lights, axis=1)
        for _ in range(NSUB):
            high = value.astype(jnp.bfloat16)
            low = (value - high.astype(F32)).astype(jnp.bfloat16)
            uptake = jnp.dot(
                taken, jnp.concatenate([high, low, high], axis=0), preferred_element_type=F32
            )
            value = value + (1.0 / NSUB) * (light * jnp.tanh(uptake) - loss * value)
        for r in range(QROWS):
            for m in range(pair):
                at = (r * pair + m) * cols
                states[level, quarter, 2 * me + m, r] = value[:, at : at + cols]

    def send(level, quarter, whole=True):
        piece = level * quarters + quarter
        if whole:
            state_copy(piece, across, 0).start()

        @pl.when(outer)
        def _():
            state_copy(piece, near, 1).start()

    lax.fori_loop(0, levels, start_edges, 0)
    lax.fori_loop(2, levels, start_middle, 0)

    @pl.when(inner)
    def _():
        for at in range(5, 10):
            small(at).start()

    mix_middle(0)
    mix_middle(1)
    grow(0, 1)

    peers = 3 + linked_up.astype(jnp.int32) + linked_down.astype(jnp.int32)
    peers += jnp.where(inner, mids + GROUP - 2, 0)
    if deeps > 1:
        peers += (inner & even).astype(jnp.int32)
        peers += (is_up_relay | is_down_relay).astype(jnp.int32)
        peers += jnp.where((tile == half - 1) | (tile == half), levels, 0)
    pl.semaphore_wait(barrier, peers)

    send(0, 1)
    for quarter in range(2, quarters - 1):
        grow(0, quarter)
        send(0, quarter)
    lax.fori_loop(0, levels, send_edges, 0)

    if levels > 2:
        mix_middle(2)

    for quarter in range(1, quarters - 1):
        grow(1, quarter)
        send(1, quarter, whole=False)
    if deeps > 1:
        pass_on()
    mix_edges(0)
    mix_edges(1)
    for quarter in (0, quarters - 1):
        grow(0, quarter)
        send(0, quarter)

    def step_level(level, carry):
        @pl.when(level < levels - 1)
        def _():
            mix_middle(level + 1)

        for quarter in range(1, quarters - 1):
            grow(level, quarter)
            send(level, quarter)
        mix_edges(level)
        for quarter in (0, quarters - 1):
            grow(level - 1, quarter)
            send(level - 1, quarter)
        return carry

    lax.fori_loop(2, levels, step_level, 0)
    for quarter in (0, quarters - 1):
        grow(levels - 1, quarter)
        send(levels - 1, quarter)

    def in_order(step):
        later = step - 4
        level, turn = 2 + later // 4, lax.rem(later, 4)
        piece = jnp.where(
            turn < 2, level * quarters + 1 + turn, (level - 1) * quarters + 3 * (turn - 2)
        )
        piece = jnp.where(step < 4, 3 * (step - 2), piece)
        piece = jnp.where(step < 2, 1 + step, piece)
        ending = step - (steps - 2)
        return jnp.where(ending < 0, piece, (levels - 1) * quarters + 3 * ending)

    def sent(source, sem):
        pltpu.make_async_remote_copy(
            src_ref=source,
            dst_ref=source,
            send_sem=sem,
            recv_sem=sem,
            device_id=(3 - me, tile),
            device_id_type=MESH,
        ).wait_send()

    def landed(target, sem):
        pltpu.make_async_remote_copy(
            src_ref=target,
            dst_ref=target,
            send_sem=sem,
            recv_sem=sem,
            device_id=(3 - me, tile),
            device_id_type=MESH,
        ).wait_recv()

    def wait_states(piece):
        level, quarter = piece // quarters, lax.rem(piece, quarters)
        landed(states.at[level, quarter, pl.ds(0, members - pair)], piece_recv.at[piece])

    def result_copy(piece):
        return pltpu.make_async_remote_copy(
            src_ref=passed.at[piece],
            dst_ref=results.at[piece],
            send_sem=result_send,
            recv_sem=piece_recv.at[piece],
            device_id=(beside, tile),
            device_id_type=MESH,
        )

    def stores(piece):
        level, quarter = piece // quarters, lax.rem(piece, quarters)
        return [
            pltpu.make_async_copy(
                results.at[piece, r],
                out.at[:, :, level, quarter * QROWS + r],
                store_sem,
            )
            for r in range(QROWS)
        ]

    def small_copy(source, target, send, recv, at):
        return pltpu.make_async_remote_copy(
            src_ref=source,
            dst_ref=target,
            send_sem=send,
            recv_sem=recv,
            device_id=(me, at),
            device_id_type=MESH,
        )

    def partial_sums():
        for quarter in range(quarters):
            for r in range(QROWS):
                for m in range(members):
                    at = (quarter * QROWS + r) * members + m
                    surface[at : at + 1, :] = states[0, quarter, m, r, 0:1, :]
        picked_from = surface[...]
        width = OBS_STEP // cols
        column_ids = lax.broadcasted_iota(jnp.int32, (cols, OBS_STEP), 0)
        tile_ids = lax.broadcasted_iota(jnp.int32, (tiles, OBS_STEP), 0)

        def flat(ref, step):
            return jnp.concatenate(
                [ref[pl.ds(step * width + i, 1), :] for i in range(width)], axis=1
            )

        def step_obs(step, total):
            local = flat(obs_cell, step) - tile * (rows * cols)
            column = jnp.bitwise_and(local, cols - 1)
            row_of = jnp.right_shift(local, cols.bit_length() - 1)
            one_hot = (column_ids == column).astype(F32)
            picked = jnp.dot(
                picked_from, one_hot, precision=HIGHEST, preferred_element_type=F32
            )
            observed = jnp.zeros((members, OBS_STEP), F32)
            for r in range(rows):
                observed += jnp.where(
                    row_of == r, picked[r * members : (r + 1) * members], 0.0
                )
            inside = (row_of >= 0) & (row_of < rows)
            weight = jnp.where(inside, 1.0 / flat(obs_var, step), 0.0)
            spread = observed - jnp.sum(observed, axis=0, keepdims=True) * (1.0 / members)
            noise = obs_noise[:, pl.ds(pl.multiple_of(step * OBS_STEP, OBS_STEP), OBS_STEP)]
            innov = flat(obs_value, step) + noise - observed
            scaled = spread * weight
            both = jnp.concatenate([spread, innov], axis=0)
            products = jnp.concatenate(
                [scaled[a : a + 1] * both for a in range(members)], axis=0
            )
            chosen = (tile_ids == flat(obs_tile, step)).astype(F32)
            return total + lax.dot_general(
                chosen,
                products,
                (((1,), (1,)), ((), ())),
                precision=HIGHEST,
                preferred_element_type=F32,
            )

        steps = obs_noise.shape[1] // OBS_STEP
        total = lax.fori_loop(0, steps, step_obs, jnp.zeros((tiles, 128), F32))
        for d in range(deeps):
            for b in range(mids):
                at = (d * mids + b) * GROUP
                partial[b, d] = total[at : at + GROUP]

        sums = partial[mid_at]
        if mids > 1:
            for j in range(1, mids):
                small_copy(
                    partial.at[lax.rem(mid_at + j, mids)],
                    recv_mid.at[mid_at],
                    mid_sem.at[0],
                    mid_sem.at[1],
                    mid_tile(j),
                ).start()
            landed(recv_mid.at[pl.ds(0, mids - 1)], mid_sem.at[1])
            for j in range(1, mids):
                sums = sums + recv_mid[lax.rem(mid_at + j, mids)]
        held_group[...] = sums
        for j in range(1, GROUP):
            small_copy(
                held_group,
                recv_group.at[group_at],
                group_sem.at[0],
                group_sem.at[1],
                group_tile(j),
            ).start()
        landed(recv_group.at[pl.ds(0, GROUP - 1)], group_sem.at[1])
        for j in range(1, GROUP):
            sums = sums + recv_group[lax.rem(group_at + j, GROUP)]
        if mids > 1:
            sent(partial.at[pl.ds(0, mids - 1)], mid_sem.at[0])
        sent(recv_group.at[pl.ds(0, GROUP - 1)], group_sem.at[0])
        if deeps == 1:
            return sums[0]
        held_deep[...] = sums
        across_half = small_copy(
            held_deep.at[1 - deep_at], recv_deep, deep_sem.at[0], deep_sem.at[1], other_half
        )
        handed = small_copy(
            recv_deep, recv_deep, deep_sem.at[0], deep_sem.at[1], jnp.minimum(tile + 1, tiles - 1)
        )

        @pl.when(even)
        def _():
            across_half.start()
            across_half.wait()
            handed.start()
            handed.wait_send()

        @pl.when(jnp.logical_not(even))
        def _():
            handed.wait_recv()

        sums = held_deep[deep_at] + recv_deep[...]
        return sums

    def weights_of(sums):
        sub = lax.broadcasted_iota(jnp.int32, (8, 128), 0)
        lane8 = lax.broadcasted_iota(jnp.int32, (8, 128), 1)
        own = jnp.sum(jnp.where(sub == group_at, sums, 0.0), axis=0, keepdims=True)
        parts = jnp.where(
            jnp.right_shift(lane8, 4) == sub, jnp.broadcast_to(own, (8, 128)), 0.0
        )
        fold_from = lax.broadcasted_iota(jnp.int32, (128, 128), 0)
        fold_to = lax.broadcasted_iota(jnp.int32, (128, 128), 1)
        fold = (jnp.bitwise_and(fold_from, 15) == fold_to).astype(F32)
        system = jnp.dot(parts, fold, precision=HIGHEST, preferred_element_type=F32)
        system = system + jnp.where(lane8 == sub, float(members - 1), 0.0)
        for k in range(members):
            column = jnp.sum(jnp.where(lane8 == k, system, 0.0), axis=1, keepdims=True)
            pivot = system[k : k + 1] / column[k : k + 1]
            system = jnp.where(sub == k, pivot, system - column * pivot)
        return system - jnp.sum(system, axis=0, keepdims=True) * (1.0 / members)

    def spread_weights(centered):
        sub = lax.broadcasted_iota(jnp.int32, (8, 128), 0)
        lane8 = lax.broadcasted_iota(jnp.int32, (8, 128), 1)
        for j in range(4):
            member = 2 * me + j if j < 2 else 2 * beside + j - 2
            column = jnp.sum(
                jnp.where(lane8 == members + member, centered, 0.0), axis=1, keepdims=True
            )
            wide = jnp.broadcast_to(column, (8, 128))
            wide = wide + jnp.where(sub == member, 1.0, 0.0)
            for k in range(members):
                splats[j, k] = jnp.broadcast_to(wide[k : k + 1], (8, 128))

        for j in range(4):
            member = 2 * across + j if j < 2 else 2 * (3 - beside) + j - 2
            column = jnp.sum(
                jnp.where(lane8 == members + member, centered, 0.0), axis=1, keepdims=True
            )
            wide = jnp.broadcast_to(column, (8, 128))
            for k in range(4):
                source = 2 * me + k if k < 2 else 2 * beside + k - 2
                row = jnp.sum(jnp.where(sub == source, wide, 0.0), axis=0, keepdims=True)
                splats_across[j, k] = jnp.broadcast_to(row, (8, 128))

    def tail_piece(at):
        return quarters + 1 + at

    def tail_copy(at, to, which):
        return pltpu.make_async_remote_copy(
            src_ref=tail_out.at[at, which],
            dst_ref=tail_in.at[at],
            send_sem=tail_sem,
            recv_sem=tail_recv.at[at],
            device_id=(to, tile),
            device_id_type=MESH,
        )

    def analyse_tail(at):
        piece = tail_piece(at)
        level, quarter = 1, 1 + at
        near_states = states.at[level, quarter, pl.ds(0, pair)]
        landed(near_states, piece_recv.at[piece])

        def tail_part(part, carry):
            r, first = part // (ntr // 8), pl.multiple_of(lax.rem(part, ntr // 8) * 8, 8)
            values = [
                states[level, quarter, 2 * source + k, r, pl.ds(first, 8), :]
                for source in (me, beside)
                for k in range(pair)
            ]
            for j in range(4):
                same_side, other_side = None, None
                for k in range(4):
                    source = 2 * me + k if k < 2 else 2 * beside + k - 2
                    here = values[k] * splats[j, source]
                    there = values[k] * splats_across[j, k]
                    same_side = here if k == 0 else same_side + here
                    other_side = there if k == 0 else other_side + there
                target = results if j < 2 else passed
                target[piece, r, j % 2, pl.ds(first, 8), :] = same_side
                tail_out[at, j // 2, r, j % 2, pl.ds(first, 8), :] = other_side
            return carry

        lax.fori_loop(0, QROWS * (ntr // 8), tail_part, 0)
        result_copy(piece).start()

    def finish_tail(at):
        piece = tail_piece(at)
        landed(tail_in.at[at], tail_recv.at[at])
        results[piece] = results[piece] + tail_in[at]
        for store in stores(piece):
            store.start()

    def analyse(piece):
        level, quarter = piece // quarters, lax.rem(piece, quarters)

        def analyse_part(at, carry):
            r, first = at // (ntr // 8), pl.multiple_of(lax.rem(at, ntr // 8) * 8, 8)
            sums = [None] * 4
            for k in range(members):
                value = states[level, quarter, k, r, pl.ds(first, 8), :]
                for j in range(4):
                    term = value * splats[j, k]
                    sums[j] = term if k == 0 else sums[j] + term
            for m in range(pair):
                results[piece, r, m, pl.ds(first, 8), :] = sums[m]
                passed[piece, r, m, pl.ds(first, 8), :] = sums[2 + m]
            return carry

        lax.fori_loop(0, QROWS * (ntr // 8), analyse_part, 0)
        result_copy(piece).start()
        for store in stores(piece):
            store.start()

    own_states = states.at[:, :, pl.ds(2 * me, 2)]

    @pl.when(tile < tiles - 1)
    def _():
        sent(raw.at[:, rows], halo_send.at[0])

    @pl.when(tile > 0)
    def _():
        sent(raw.at[:, 1], halo_send.at[1])

    if deeps > 1:
        end_pass()

    @pl.when(inner)
    def _():
        for at in range(5, 10):
            small(at).wait()
        for quarter in range(1, quarters - 1):
            wait_states(quarter)
        for quarter in (0, quarters - 1):
            wait_states(quarter)
        spread_weights(weights_of(partial_sums()))
        for at in range(TAIL):
            analyse_tail(at)

        def analyse_next(step, carry):
            piece = in_order(step)

            @pl.when(piece >= quarters)
            def _():
                wait_states(piece)

            analyse(piece)

            @pl.when(step == steps - AHEAD)
            def _():
                for at in range(TAIL):
                    tail_copy(at, 3 - beside, 1).start()
                    tail_copy(at, across, 0).start()

            return carry

        lax.fori_loop(0, steps, analyse_next, 0)
        for at in range(TAIL):
            finish_tail(at)
        sent(tail_out, tail_sem)
        sent(passed, result_send)
        sent(passed.at[pl.ds(0, steps)], state_send.at[0])

    @pl.when(outer)
    def _():
        def take(step, carry):
            piece = in_order(step)
            result_copy(piece).wait_recv()
            for store in stores(piece):
                store.start()
            return carry

        lax.fori_loop(0, steps, take, 0)
        for at in range(TAIL):
            result_copy(tail_piece(at)).wait_recv()
            finish_tail(at)
        sent(passed.at[pl.ds(0, steps)], state_send.at[0])
        sent(own_states, state_send.at[1])

    pltpu.make_async_copy(results, results, store_sem).wait()


def on_device(
    tracers,
    horiz_mix,
    vert_mix,
    sunlit,
    interaction,
    remin,
    obs_cell,
    obs_tile,
    obs_value,
    obs_noise,
    obs_var,
):
    pair, ntr, levels, rows, cols = tracers.shape
    tiles = lax.axis_size("space")
    deeps = DEEP if tiles > GROUP else 1
    mids = tiles // (deeps * GROUP)
    quarters = rows // QROWS
    pieces = levels * quarters
    count = obs_cell.shape[0]
    obs_rows = (count // cols, cols)
    pinned = pl.BlockSpec(memory_space=pltpu.HBM)
    anywhere = pl.BlockSpec(memory_space=pl.ANY)
    dma = pltpu.SemaphoreType.DMA
    operands = (
        tracers,
        horiz_mix,
        vert_mix,
        sunlit.reshape(-1, cols),
        interaction,
        remin.reshape(1, ntr),
        obs_cell.reshape(obs_rows),
        obs_tile.reshape(obs_rows),
        obs_value.reshape(obs_rows),
        obs_noise,
        obs_var.reshape(obs_rows),
    )
    operands = [pltpu.with_memory_space_constraint(value, pltpu.HBM) for value in operands]
    return pl.pallas_call(
        functools.partial(kernel, (tiles, mids, deeps)),
        out_shape=jax.ShapeDtypeStruct(tracers.shape, F32),
        in_specs=[pinned] * len(operands),
        out_specs=anywhere,
        scratch_shapes=[
            *[pltpu.VMEM(value.shape, value.dtype) for value in operands[1:]],
            pltpu.VMEM((rows, cols), F32),
            pltpu.VMEM((pair, ntr, cols), F32),
            pltpu.VMEM((levels, rows + 2, pair, ntr, cols), F32),
            pltpu.VMEM((levels, rows, pair, ntr, cols), F32),
            pltpu.VMEM((levels, quarters, 8, QROWS, ntr, cols), F32),
            pltpu.VMEM((pieces, QROWS, pair, ntr, cols), F32),
            pltpu.VMEM((pieces, QROWS, pair, ntr, cols), F32),
            pltpu.VMEM((rows * 8, cols), F32),
            pltpu.VMEM((mids, deeps, GROUP, 128), F32),
            pltpu.VMEM((mids, deeps, GROUP, 128), F32),
            pltpu.VMEM((deeps, GROUP, 128), F32),
            pltpu.VMEM((GROUP, deeps, GROUP, 128), F32),
            pltpu.VMEM((deeps, GROUP, 128), F32),
            pltpu.VMEM((GROUP, 128), F32),
            pltpu.VMEM((4, 8, 8, 128), F32),
            pltpu.VMEM((4, 4, 8, 128), F32),
            pltpu.VMEM((TAIL, 2, QROWS, pair, ntr, cols), F32),
            pltpu.VMEM((TAIL, QROWS, pair, ntr, cols), F32),
            dma((10,)),
            dma((levels,)),
            dma((levels, 2)),
            dma,
            dma,
            dma((2,)),
            dma((levels, 2)),
            dma((2,)),
            dma((pieces,)),
            dma,
            dma,
            dma,
            dma((TAIL,)),
            dma((2,)),
            dma((2,)),
            dma((2,)),
        ],
        compiler_params=pltpu.CompilerParams(
            collective_id=0, has_side_effects=True, vmem_limit_bytes=VMEM_BYTES
        ),
        cost_estimate=pl.CostEstimate(
            flops=500_000_000, bytes_accessed=8_000_000, transcendentals=3_000_000
        ),
        name="step_and_analysis",
    )(*operands)


def solution(mesh):
    return jax.shard_map(
        on_device,
        mesh=mesh,
        in_specs=(
            P("member", None, None, "space", None),
            P(None, "space", None),
            P(None, "space", None),
            P(),
            P(),
            P(),
            P(),
            P(),
            P(),
            P(),
            P(),
        ),
        out_specs=P("member", None, None, "space", None),
        check_vma=False,
    )
```

```python
import functools

import jax
import jax.numpy as jnp
from jax import lax
from jax.experimental import pallas as pl
from jax.experimental.pallas import tpu as pltpu
from jax.sharding import PartitionSpec as P

NSUB = 4
GROUP = 8
DEEP = 2
TAIL_LEVELS = 2
TAIL = 2 * TAIL_LEVELS
AHEAD = 9
QROWS = 2
VMEM_BYTES = 34 * 1024 * 1024
OBS_STEP = 512
F32 = jnp.float32
MESH = pl.DeviceIdType.MESH
HIGHEST = lax.Precision.HIGHEST


def kernel(
    sizes,
    tracers,
    horiz_from,
    vert_from,
    sunlit_from,
    interaction_from,
    remin_from,
    cell_from,
    chosen_from,
    value_from,
    noise_from,
    var_from,
    out,
    horiz_mix,
    vert_mix,
    sunlit,
    interaction,
    remin,
    obs_cell,
    obs_tile,
    obs_value,
    obs_noise,
    obs_var,
    lit,
    relayed,
    raw,
    mixed,
    states,
    results,
    passed,
    surface,
    partial,
    recv_mid,
    held_group,
    recv_group,
    held_deep,
    recv_deep,
    splats,
    splats_across,
    tail_out,
    tail_in,
    small_sem,
    load_sem,
    edge_sem,
    relay_send,
    relay_recv,
    halo_send,
    halo_recv,
    state_send,
    piece_recv,
    result_send,
    store_sem,
    tail_sem,
    tail_recv,
    mid_sem,
    group_sem,
    deep_sem,
):
    tiles, mids, deeps = sizes
    ntr, levels, rows, cols = tracers.shape[1:]
    pair, quarters = 2, rows // QROWS
    members = 8
    pieces = levels * quarters
    steps = pieces - TAIL
    me = lax.axis_index("member")
    tile = lax.axis_index("space")
    inner = (me == 1) | (me == 2)
    outer = jnp.logical_not(inner)
    group_at = lax.rem(tile, GROUP)
    mid_at = lax.rem(tile // GROUP, mids)
    deep_at = tile // (GROUP * mids)
    half = tiles // 2
    even = lax.rem(tile, 2) == 0
    other_half = lax.rem(tile + half, tiles)
    linked_up, linked_down = tile < tiles - 1, tile > 0
    if deeps > 1:
        linked_up, linked_down = linked_up & (tile != half - 1), linked_down & (tile != half)
    is_up_relay = (tile < half) & (lax.rem(tile, 4) == 2)
    is_down_relay = (tile >= half) & (lax.rem(tile, 4) == 1)

    def up_relay(level):
        return 4 * level + 2

    def down_relay(level):
        return half + 4 * level + 1

    near = jnp.where(me == 0, 1, 2)
    beside = jnp.where(me == 1, 0, 3)
    across = jnp.where(inner, 3 - me, jnp.where(me == 0, 2, 1))

    def mid_tile(j):
        return (deep_at * mids + lax.rem(mid_at + j, mids)) * GROUP + group_at

    def group_tile(j):
        return (deep_at * mids + mid_at) * GROUP + lax.rem(group_at + j, GROUP)

    def load(level, row, sem):
        return pltpu.make_async_copy(tracers.at[:, :, level, row], raw.at[level, row + 1], sem)

    barrier = pltpu.get_barrier_semaphore()
    for j in range(1, 4):
        pl.semaphore_signal(
            barrier, 1, device_id=(lax.rem(me + j, 4), tile), device_id_type=MESH
        )

    @pl.when(linked_down)
    def _():
        pl.semaphore_signal(barrier, 1, device_id=(me, tile - 1), device_id_type=MESH)

    @pl.when(linked_up)
    def _():
        pl.semaphore_signal(barrier, 1, device_id=(me, tile + 1), device_id_type=MESH)

    @pl.when(inner)
    def _():
        for j in range(1, mids):
            pl.semaphore_signal(barrier, 1, device_id=(me, mid_tile(j)), device_id_type=MESH)
        for j in range(1, GROUP):
            pl.semaphore_signal(barrier, 1, device_id=(me, group_tile(j)), device_id_type=MESH)

    if deeps > 1:

        @pl.when(inner & even)
        def _():
            pl.semaphore_signal(barrier, 1, device_id=(me, other_half), device_id_type=MESH)

        @pl.when(tile == half - 1)
        def _():
            for level in range(levels):
                pl.semaphore_signal(
                    barrier, 1, device_id=(me, down_relay(level)), device_id_type=MESH
                )

        @pl.when(tile == half)
        def _():
            for level in range(levels):
                pl.semaphore_signal(
                    barrier, 1, device_id=(me, up_relay(level)), device_id_type=MESH
                )

        @pl.when(is_up_relay)
        def _():
            pl.semaphore_signal(barrier, 1, device_id=(me, half - 1), device_id_type=MESH)

        @pl.when(is_down_relay)
        def _():
            pl.semaphore_signal(barrier, 1, device_id=(me, half), device_id_type=MESH)

    def small(at):
        source, held = (
            (interaction_from, interaction),
            (remin_from, remin),
            (sunlit_from, sunlit),
            (horiz_from, horiz_mix),
            (vert_from, vert_mix),
            (cell_from, obs_cell),
            (chosen_from, obs_tile),
            (value_from, obs_value),
            (noise_from, obs_noise),
            (var_from, obs_var),
        )[at]
        return pltpu.make_async_copy(source, held, small_sem.at[at])

    for at in range(5):
        small(at).start()

    def start_middle(level, carry):
        for row in range(1, rows - 1):
            load(level, row, load_sem.at[level]).start()
        return carry

    def start_edges(level, carry):
        for end in range(2):
            load(level, end * (rows - 1), edge_sem.at[level, end]).start()
        return carry

    lax.fori_loop(0, 2, start_middle, 0)

    def halo_up(level):
        return pltpu.make_async_remote_copy(
            src_ref=raw.at[level, rows],
            dst_ref=raw.at[level, 0],
            send_sem=halo_send.at[0],
            recv_sem=halo_recv.at[level, 0],
            device_id=(me, lax.rem(tile + 1, tiles)),
            device_id_type=MESH,
        )

    def halo_down(level):
        return pltpu.make_async_remote_copy(
            src_ref=raw.at[level, 1],
            dst_ref=raw.at[level, rows + 1],
            send_sem=halo_send.at[1],
            recv_sem=halo_recv.at[level, 1],
            device_id=(me, lax.rem(tile + tiles - 1, tiles)),
            device_id_type=MESH,
        )

    def to_relay(level, row, way, at):
        return pltpu.make_async_remote_copy(
            src_ref=raw.at[level, row],
            dst_ref=relayed,
            send_sem=halo_send.at[way],
            recv_sem=relay_recv,
            device_id=(me, at),
            device_id_type=MESH,
        )

    def from_relay(level, row, way, at):
        return pltpu.make_async_remote_copy(
            src_ref=relayed,
            dst_ref=raw.at[level, row],
            send_sem=relay_send,
            recv_sem=halo_recv.at[level, way],
            device_id=(me, at),
            device_id_type=MESH,
        )

    def pass_on():
        @pl.when(is_up_relay)
        def _():
            level = tile // 4
            to_relay(level, rows, 0, half - 1).wait_recv()
            from_relay(level, 0, 0, half).start()

        @pl.when(is_down_relay)
        def _():
            level = (tile - half) // 4
            to_relay(level, 1, 1, half).wait_recv()
            from_relay(level, rows + 1, 1, half - 1).start()

    def end_pass():
        @pl.when(is_up_relay)
        def _():
            from_relay(tile // 4, 0, 0, half).wait_send()

        @pl.when(is_down_relay)
        def _():
            from_relay((tile - half) // 4, rows + 1, 1, half - 1).wait_send()

    def send_edges(level, carry):
        for end in range(2):
            load(level, end * (rows - 1), edge_sem.at[level, end]).wait()

        @pl.when(linked_up)
        def _():
            halo_up(level).start()

        @pl.when(linked_down)
        def _():
            halo_down(level).start()

        if deeps > 1:

            @pl.when(tile == half - 1)
            def _():
                to_relay(level, rows, 0, up_relay(level)).start()

            @pl.when(tile == half)
            def _():
                to_relay(level, 1, 1, down_relay(level)).start()

        return carry

    lane = lax.broadcasted_iota(jnp.int32, (ntr, cols), 1)

    def mix_row(level, row):
        strength = horiz_mix[level, pl.ds(row, 1), :]
        for m in range(pair):
            own = raw[level, row + 1, m]
            west = jnp.where(lane == 0, own, pltpu.roll(own, 1, 1))
            east = jnp.where(lane == cols - 1, own, pltpu.roll(own, cols - 1, 1))
            laplace = raw[level, row, m] + raw[level, row + 2, m] + west + east - 4.0 * own
            mixed[level, row, m] = own + strength * laplace

    def mix_middle(level):
        middle = raw.at[level, pl.ds(2, rows - 2)]
        pltpu.make_async_copy(middle, middle, load_sem.at[level]).wait()

        def mix_one(row, carry):
            mix_row(level, row)
            return carry

        lax.fori_loop(QROWS, rows - QROWS, mix_one, 0)

    def mix_edges(level):
        @pl.when(tile > 0)
        def _():
            halo_up(level).wait_recv()

        @pl.when(tile == 0)
        def _():
            raw[level, 0] = raw[level, 1]

        @pl.when(tile < tiles - 1)
        def _():
            halo_down(level).wait_recv()

        @pl.when(tile == tiles - 1)
        def _():
            raw[level, rows + 1] = raw[level, rows]

        def mix_two(row, carry):
            mix_row(level, row)
            mix_row(level, rows - 1 - row)
            return carry

        lax.fori_loop(0, QROWS, mix_two, 0)

    def state_copy(piece, to, which):
        level, quarter = piece // quarters, lax.rem(piece, quarters)
        block = states.at[level, quarter, pl.ds(2 * me, 2)]
        return pltpu.make_async_remote_copy(
            src_ref=block,
            dst_ref=block,
            send_sem=state_send.at[which],
            recv_sem=piece_recv.at[piece],
            device_id=(to, tile),
            device_id_type=MESH,
        )

    for at in range(5):
        small(at).wait()
    same = lax.broadcasted_iota(jnp.int32, (ntr, ntr), 0) == lax.broadcasted_iota(
        jnp.int32, (ntr, ntr), 1
    )
    loss = jnp.sum(
        jnp.where(same, jnp.broadcast_to(remin[...], (ntr, ntr)), 0.0), axis=1, keepdims=True
    )
    loss = jnp.broadcast_to(loss, (ntr, cols))
    loss = jnp.concatenate([loss] * (QROWS * pair), axis=1)
    place_from = lax.broadcasted_iota(jnp.int32, (ntr, 3 * ntr), 0)
    place_to = lax.broadcasted_iota(jnp.int32, (ntr, 3 * ntr), 1)
    place = (lax.rem(place_to, ntr) == place_from).astype(F32)
    wide = jnp.dot(interaction[...], place, precision=HIGHEST, preferred_element_type=F32)
    wide_high = wide.astype(jnp.bfloat16).astype(F32)
    taken = jnp.where(place_to < 2 * ntr, wide_high, wide - wide_high).astype(jnp.bfloat16)

    flags = (sunlit[pl.ds(tile * rows // cols, 1), :] > 0).astype(F32)
    flag_lane = lax.broadcasted_iota(jnp.int32, (1, cols), 1)
    for row in range(rows):
        flag = jnp.where(flag_lane == lax.rem(tile * rows, cols) + row, flags, 0.0)
        lit[row : row + 1, :] = jnp.broadcast_to(
            jnp.sum(flag, axis=1, keepdims=True), (1, cols)
        )

    def grow(level, quarter):
        below, above = jnp.minimum(level + 1, levels - 1), jnp.maximum(level - 1, 0)
        light = 0.6 * jnp.exp(-0.4 * jnp.full((1, cols), level, jnp.int32).astype(F32))
        blocks, lights = [], []
        for r in range(QROWS):
            row = quarter * QROWS + r
            down_mix = vert_mix[jnp.minimum(level, levels - 2), pl.ds(row, 1), :]
            up_mix = vert_mix[above, pl.ds(row, 1), :]
            for m in range(pair):
                here = mixed[level, row, m]
                down = down_mix * (mixed[below, row, m] - here)
                up = up_mix * (here - mixed[above, row, m])
                blocks.append(here + down - up)
                lights.append(light * lit[pl.ds(row, 1), :])
        value = jnp.concatenate(blocks, axis=1)
        light = jnp.concatenate(lights, axis=1)
        for _ in range(NSUB):
            high = value.astype(jnp.bfloat16)
            low = (value - high.astype(F32)).astype(jnp.bfloat16)
            uptake = jnp.dot(
                taken, jnp.concatenate([high, low, high], axis=0), preferred_element_type=F32
            )
            value = value + (1.0 / NSUB) * (light * jnp.tanh(uptake) - loss * value)
        for r in range(QROWS):
            for m in range(pair):
                at = (r * pair + m) * cols
                states[level, quarter, 2 * me + m, r] = value[:, at : at + cols]

    def send(level, quarter, whole=True):
        piece = level * quarters + quarter
        @pl.when(whole)
        def _():
            state_copy(piece, across, 0).start()

        @pl.when(outer)
        def _():
            state_copy(piece, near, 1).start()

    lax.fori_loop(0, levels, start_edges, 0)
    lax.fori_loop(2, levels, start_middle, 0)

    @pl.when(inner)
    def _():
        for at in range(5, 10):
            small(at).start()

    mix_middle(0)
    mix_middle(1)
    grow(0, 1)

    peers = 3 + linked_up.astype(jnp.int32) + linked_down.astype(jnp.int32)
    peers += jnp.where(inner, mids + GROUP - 2, 0)
    if deeps > 1:
        peers += (inner & even).astype(jnp.int32)
        peers += (is_up_relay | is_down_relay).astype(jnp.int32)
        peers += jnp.where((tile == half - 1) | (tile == half), levels, 0)
    pl.semaphore_wait(barrier, peers)

    send(0, 1)
    for quarter in range(2, quarters - 1):
        grow(0, quarter)
        send(0, quarter)
    lax.fori_loop(0, levels, send_edges, 0)

    if levels > 2:
        mix_middle(2)

    for quarter in range(1, quarters - 1):
        grow(1, quarter)
        send(1, quarter, whole=False)
    if deeps > 1:
        pass_on()
    mix_edges(0)
    mix_edges(1)
    for quarter in (0, quarters - 1):
        grow(0, quarter)
        send(0, quarter)

    def step_level(level, carry):
        @pl.when(level < levels - 1)
        def _():
            mix_middle(level + 1)

        for quarter in range(1, quarters - 1):
            grow(level, quarter)
            send(level, quarter, whole=level > TAIL_LEVELS)
        mix_edges(level)
        for quarter in (0, quarters - 1):
            grow(level - 1, quarter)
            send(level - 1, quarter)
        return carry

    lax.fori_loop(2, levels, step_level, 0)
    for quarter in (0, quarters - 1):
        grow(levels - 1, quarter)
        send(levels - 1, quarter)

    def in_order(step):
        edge = step - 2
        later = edge - TAIL
        level, turn = TAIL_LEVELS + 1 + later // 4, lax.rem(later, 4)
        piece = jnp.where(
            turn < 2, level * quarters + 1 + turn, (level - 1) * quarters + 3 * (turn - 2)
        )
        piece = jnp.where(
            edge < TAIL, edge // 2 * quarters + 3 * lax.rem(edge, 2), piece
        )
        piece = jnp.where(step < 2, 1 + step, piece)
        ending = step - (steps - 2)
        return jnp.where(ending < 0, piece, (levels - 1) * quarters + 3 * ending)

    def sent(source, sem):
        pltpu.make_async_remote_copy(
            src_ref=source,
            dst_ref=source,
            send_sem=sem,
            recv_sem=sem,
            device_id=(3 - me, tile),
            device_id_type=MESH,
        ).wait_send()

    def landed(target, sem):
        pltpu.make_async_remote_copy(
            src_ref=target,
            dst_ref=target,
            send_sem=sem,
            recv_sem=sem,
            device_id=(3 - me, tile),
            device_id_type=MESH,
        ).wait_recv()

    def wait_states(piece):
        level, quarter = piece // quarters, lax.rem(piece, quarters)
        landed(states.at[level, quarter, pl.ds(0, members - pair)], piece_recv.at[piece])

    def result_copy(piece):
        return pltpu.make_async_remote_copy(
            src_ref=passed.at[piece],
            dst_ref=results.at[piece],
            send_sem=result_send,
            recv_sem=piece_recv.at[piece],
            device_id=(beside, tile),
            device_id_type=MESH,
        )

    def stores(piece):
        level, quarter = piece // quarters, lax.rem(piece, quarters)
        return [
            pltpu.make_async_copy(
                results.at[piece, r],
                out.at[:, :, level, quarter * QROWS + r],
                store_sem,
            )
            for r in range(QROWS)
        ]

    def small_copy(source, target, send, recv, at):
        return pltpu.make_async_remote_copy(
            src_ref=source,
            dst_ref=target,
            send_sem=send,
            recv_sem=recv,
            device_id=(me, at),
            device_id_type=MESH,
        )

    def partial_sums():
        for quarter in range(quarters):
            for r in range(QROWS):
                for m in range(members):
                    at = (quarter * QROWS + r) * members + m
                    surface[at : at + 1, :] = states[0, quarter, m, r, 0:1, :]
        picked_from = surface[...]
        width = OBS_STEP // cols
        column_ids = lax.broadcasted_iota(jnp.int32, (cols, OBS_STEP), 0)
        tile_ids = lax.broadcasted_iota(jnp.int32, (tiles, OBS_STEP), 0)

        def flat(ref, step):
            return jnp.concatenate(
                [ref[pl.ds(step * width + i, 1), :] for i in range(width)], axis=1
            )

        def step_obs(step, total):
            local = flat(obs_cell, step) - tile * (rows * cols)
            column = jnp.bitwise_and(local, cols - 1)
            row_of = jnp.right_shift(local, cols.bit_length() - 1)
            one_hot = (column_ids == column).astype(F32)
            picked = jnp.dot(
                picked_from, one_hot, precision=HIGHEST, preferred_element_type=F32
            )
            observed = jnp.zeros((members, OBS_STEP), F32)
            for r in range(rows):
                observed += jnp.where(
                    row_of == r, picked[r * members : (r + 1) * members], 0.0
                )
            inside = (row_of >= 0) & (row_of < rows)
            weight = jnp.where(inside, 1.0 / flat(obs_var, step), 0.0)
            spread = observed - jnp.sum(observed, axis=0, keepdims=True) * (1.0 / members)
            noise = obs_noise[:, pl.ds(pl.multiple_of(step * OBS_STEP, OBS_STEP), OBS_STEP)]
            innov = flat(obs_value, step) + noise - observed
            scaled = spread * weight
            both = jnp.concatenate([spread, innov], axis=0)
            products = jnp.concatenate(
                [scaled[a : a + 1] * both for a in range(members)], axis=0
            )
            chosen = (tile_ids == flat(obs_tile, step)).astype(F32)
            return total + lax.dot_general(
                chosen,
                products,
                (((1,), (1,)), ((), ())),
                precision=HIGHEST,
                preferred_element_type=F32,
            )

        steps = obs_noise.shape[1] // OBS_STEP
        total = lax.fori_loop(0, steps, step_obs, jnp.zeros((tiles, 128), F32))
        for d in range(deeps):
            for b in range(mids):
                at = (d * mids + b) * GROUP
                partial[b, d] = total[at : at + GROUP]

        sums = partial[mid_at]
        if mids > 1:
            for j in range(1, mids):
                small_copy(
                    partial.at[lax.rem(mid_at + j, mids)],
                    recv_mid.at[mid_at],
                    mid_sem.at[0],
                    mid_sem.at[1],
                    mid_tile(j),
                ).start()
            landed(recv_mid.at[pl.ds(0, mids - 1)], mid_sem.at[1])
            for j in range(1, mids):
                sums = sums + recv_mid[lax.rem(mid_at + j, mids)]
        held_group[...] = sums
        for j in range(1, GROUP):
            small_copy(
                held_group,
                recv_group.at[group_at],
                group_sem.at[0],
                group_sem.at[1],
                group_tile(j),
            ).start()
        landed(recv_group.at[pl.ds(0, GROUP - 1)], group_sem.at[1])
        for j in range(1, GROUP):
            sums = sums + recv_group[lax.rem(group_at + j, GROUP)]
        if mids > 1:
            sent(partial.at[pl.ds(0, mids - 1)], mid_sem.at[0])
        sent(recv_group.at[pl.ds(0, GROUP - 1)], group_sem.at[0])
        if deeps == 1:
            return sums[0]
        held_deep[...] = sums
        across_half = small_copy(
            held_deep.at[1 - deep_at], recv_deep, deep_sem.at[0], deep_sem.at[1], other_half
        )
        handed = small_copy(
            recv_deep, recv_deep, deep_sem.at[0], deep_sem.at[1], jnp.minimum(tile + 1, tiles - 1)
        )

        @pl.when(even)
        def _():
            across_half.start()
            across_half.wait()
            handed.start()
            handed.wait_send()

        @pl.when(jnp.logical_not(even))
        def _():
            handed.wait_recv()

        sums = held_deep[deep_at] + recv_deep[...]
        return sums

    def weights_of(sums):
        sub = lax.broadcasted_iota(jnp.int32, (8, 128), 0)
        lane8 = lax.broadcasted_iota(jnp.int32, (8, 128), 1)
        own = jnp.sum(jnp.where(sub == group_at, sums, 0.0), axis=0, keepdims=True)
        parts = jnp.where(
            jnp.right_shift(lane8, 4) == sub, jnp.broadcast_to(own, (8, 128)), 0.0
        )
        fold_from = lax.broadcasted_iota(jnp.int32, (128, 128), 0)
        fold_to = lax.broadcasted_iota(jnp.int32, (128, 128), 1)
        fold = (jnp.bitwise_and(fold_from, 15) == fold_to).astype(F32)
        system = jnp.dot(parts, fold, precision=HIGHEST, preferred_element_type=F32)
        system = system + jnp.where(lane8 == sub, float(members - 1), 0.0)
        for k in range(members):
            column = jnp.sum(jnp.where(lane8 == k, system, 0.0), axis=1, keepdims=True)
            pivot = system[k : k + 1] / column[k : k + 1]
            system = jnp.where(sub == k, pivot, system - column * pivot)
        return system - jnp.sum(system, axis=0, keepdims=True) * (1.0 / members)

    def spread_weights(centered):
        sub = lax.broadcasted_iota(jnp.int32, (8, 128), 0)
        lane8 = lax.broadcasted_iota(jnp.int32, (8, 128), 1)
        for j in range(4):
            member = 2 * me + j if j < 2 else 2 * beside + j - 2
            column = jnp.sum(
                jnp.where(lane8 == members + member, centered, 0.0), axis=1, keepdims=True
            )
            wide = jnp.broadcast_to(column, (8, 128))
            wide = wide + jnp.where(sub == member, 1.0, 0.0)
            for k in range(members):
                splats[j, k] = jnp.broadcast_to(wide[k : k + 1], (8, 128))

        for j in range(4):
            member = 2 * across + j if j < 2 else 2 * (3 - beside) + j - 2
            column = jnp.sum(
                jnp.where(lane8 == members + member, centered, 0.0), axis=1, keepdims=True
            )
            wide = jnp.broadcast_to(column, (8, 128))
            for k in range(4):
                source = 2 * me + k if k < 2 else 2 * beside + k - 2
                row = jnp.sum(jnp.where(sub == source, wide, 0.0), axis=0, keepdims=True)
                splats_across[j, k] = jnp.broadcast_to(row, (8, 128))

    def tail_piece(at):
        return (1 + at // 2) * quarters + 1 + at % 2

    def tail_copy(at, to, which):
        return pltpu.make_async_remote_copy(
            src_ref=tail_out.at[at, which],
            dst_ref=tail_in.at[at],
            send_sem=tail_sem,
            recv_sem=tail_recv.at[at],
            device_id=(to, tile),
            device_id_type=MESH,
        )

    def analyse_tail(at):
        piece = tail_piece(at)
        level, quarter = 1 + at // 2, 1 + at % 2
        near_states = states.at[level, quarter, pl.ds(0, pair)]
        landed(near_states, piece_recv.at[piece])

        def tail_part(part, carry):
            r, first = part // (ntr // 8), pl.multiple_of(lax.rem(part, ntr // 8) * 8, 8)
            values = [
                states[level, quarter, 2 * source + k, r, pl.ds(first, 8), :]
                for source in (me, beside)
                for k in range(pair)
            ]
            for j in range(4):
                same_side, other_side = None, None
                for k in range(4):
                    source = 2 * me + k if k < 2 else 2 * beside + k - 2
                    here = values[k] * splats[j, source]
                    there = values[k] * splats_across[j, k]
                    same_side = here if k == 0 else same_side + here
                    other_side = there if k == 0 else other_side + there
                target = results if j < 2 else passed
                target[piece, r, j % 2, pl.ds(first, 8), :] = same_side
                tail_out[at, j // 2, r, j % 2, pl.ds(first, 8), :] = other_side
            return carry

        lax.fori_loop(0, QROWS * (ntr // 8), tail_part, 0)
        result_copy(piece).start()

    def finish_tail(at):
        piece = tail_piece(at)
        landed(tail_in.at[at], tail_recv.at[at])
        results[piece] = results[piece] + tail_in[at]
        for store in stores(piece):
            store.start()

    def analyse(piece):
        level, quarter = piece // quarters, lax.rem(piece, quarters)

        def analyse_part(at, carry):
            r, first = at // (ntr // 8), pl.multiple_of(lax.rem(at, ntr // 8) * 8, 8)
            sums = [None] * 4
            for k in range(members):
                value = states[level, quarter, k, r, pl.ds(first, 8), :]
                for j in range(4):
                    term = value * splats[j, k]
                    sums[j] = term if k == 0 else sums[j] + term
            for m in range(pair):
                results[piece, r, m, pl.ds(first, 8), :] = sums[m]
                passed[piece, r, m, pl.ds(first, 8), :] = sums[2 + m]
            return carry

        lax.fori_loop(0, QROWS * (ntr // 8), analyse_part, 0)
        result_copy(piece).start()
        for store in stores(piece):
            store.start()

    own_states = states.at[:, :, pl.ds(2 * me, 2)]

    @pl.when(tile < tiles - 1)
    def _():
        sent(raw.at[:, rows], halo_send.at[0])

    @pl.when(tile > 0)
    def _():
        sent(raw.at[:, 1], halo_send.at[1])

    if deeps > 1:
        end_pass()

    @pl.when(inner)
    def _():
        for at in range(5, 10):
            small(at).wait()
        for quarter in range(1, quarters - 1):
            wait_states(quarter)
        for quarter in (0, quarters - 1):
            wait_states(quarter)
        spread_weights(weights_of(partial_sums()))
        for at in range(TAIL):
            analyse_tail(at)

        def analyse_next(step, carry):
            piece = in_order(step)

            @pl.when(piece >= quarters)
            def _():
                wait_states(piece)

            analyse(piece)

            @pl.when(step == steps - AHEAD)
            def _():
                for at in range(TAIL):
                    tail_copy(at, 3 - beside, 1).start()
                    tail_copy(at, across, 0).start()

            return carry

        lax.fori_loop(0, steps, analyse_next, 0)
        for at in range(TAIL):
            finish_tail(at)
        sent(tail_out, tail_sem)
        sent(passed, result_send)
        sent(passed.at[pl.ds(0, steps)], state_send.at[0])

    @pl.when(outer)
    def _():
        def take(step, carry):
            piece = in_order(step)
            result_copy(piece).wait_recv()
            for store in stores(piece):
                store.start()
            return carry

        lax.fori_loop(0, steps, take, 0)
        for at in range(TAIL):
            result_copy(tail_piece(at)).wait_recv()
            finish_tail(at)
        sent(passed.at[pl.ds(0, steps)], state_send.at[0])
        sent(own_states, state_send.at[1])

    pltpu.make_async_copy(results, results, store_sem).wait()


def on_device(
    tracers,
    horiz_mix,
    vert_mix,
    sunlit,
    interaction,
    remin,
    obs_cell,
    obs_tile,
    obs_value,
    obs_noise,
    obs_var,
):
    pair, ntr, levels, rows, cols = tracers.shape
    tiles = lax.axis_size("space")
    deeps = DEEP if tiles > GROUP else 1
    mids = tiles // (deeps * GROUP)
    quarters = rows // QROWS
    pieces = levels * quarters
    count = obs_cell.shape[0]
    obs_rows = (count // cols, cols)
    pinned = pl.BlockSpec(memory_space=pltpu.HBM)
    anywhere = pl.BlockSpec(memory_space=pl.ANY)
    dma = pltpu.SemaphoreType.DMA
    operands = (
        tracers,
        horiz_mix,
        vert_mix,
        sunlit.reshape(-1, cols),
        interaction,
        remin.reshape(1, ntr),
        obs_cell.reshape(obs_rows),
        obs_tile.reshape(obs_rows),
        obs_value.reshape(obs_rows),
        obs_noise,
        obs_var.reshape(obs_rows),
    )
    operands = [pltpu.with_memory_space_constraint(value, pltpu.HBM) for value in operands]
    return pl.pallas_call(
        functools.partial(kernel, (tiles, mids, deeps)),
        out_shape=jax.ShapeDtypeStruct(tracers.shape, F32),
        in_specs=[pinned] * len(operands),
        out_specs=anywhere,
        scratch_shapes=[
            *[pltpu.VMEM(value.shape, value.dtype) for value in operands[1:]],
            pltpu.VMEM((rows, cols), F32),
            pltpu.VMEM((pair, ntr, cols), F32),
            pltpu.VMEM((levels, rows + 2, pair, ntr, cols), F32),
            pltpu.VMEM((levels, rows, pair, ntr, cols), F32),
            pltpu.VMEM((levels, quarters, 8, QROWS, ntr, cols), F32),
            pltpu.VMEM((pieces, QROWS, pair, ntr, cols), F32),
            pltpu.VMEM((pieces, QROWS, pair, ntr, cols), F32),
            pltpu.VMEM((rows * 8, cols), F32),
            pltpu.VMEM((mids, deeps, GROUP, 128), F32),
            pltpu.VMEM((mids, deeps, GROUP, 128), F32),
            pltpu.VMEM((deeps, GROUP, 128), F32),
            pltpu.VMEM((GROUP, deeps, GROUP, 128), F32),
            pltpu.VMEM((deeps, GROUP, 128), F32),
            pltpu.VMEM((GROUP, 128), F32),
            pltpu.VMEM((4, 8, 8, 128), F32),
            pltpu.VMEM((4, 4, 8, 128), F32),
            pltpu.VMEM((TAIL, 2, QROWS, pair, ntr, cols), F32),
            pltpu.VMEM((TAIL, QROWS, pair, ntr, cols), F32),
            dma((10,)),
            dma((levels,)),
            dma((levels, 2)),
            dma,
            dma,
            dma((2,)),
            dma((levels, 2)),
            dma((2,)),
            dma((pieces,)),
            dma,
            dma,
            dma,
            dma((TAIL,)),
            dma((2,)),
            dma((2,)),
            dma((2,)),
        ],
        compiler_params=pltpu.CompilerParams(
            collective_id=0, has_side_effects=True, vmem_limit_bytes=VMEM_BYTES
        ),
        cost_estimate=pl.CostEstimate(
            flops=500_000_000, bytes_accessed=8_000_000, transcendentals=3_000_000
        ),
        name="step_and_analysis",
    )(*operands)


def solution(mesh):
    return jax.shard_map(
        on_device,
        mesh=mesh,
        in_specs=(
            P("member", None, None, "space", None),
            P(None, "space", None),
            P(None, "space", None),
            P(),
            P(),
            P(),
            P(),
            P(),
            P(),
            P(),
            P(),
        ),
        out_specs=P("member", None, None, "space", None),
        check_vma=False,
    )
```

```python
import functools

import jax
import jax.numpy as jnp
from jax import lax
from jax.experimental import pallas as pl
from jax.experimental.pallas import tpu as pltpu
from jax.sharding import PartitionSpec as P

NSUB = 4
GROUP = 8
DEEP = 2
TAIL_LEVELS = 2
TAIL = 2 * TAIL_LEVELS
AHEAD = 9
QROWS = 2
VMEM_BYTES = 34 * 1024 * 1024
OBS_STEP = 512
F32 = jnp.float32
MESH = pl.DeviceIdType.MESH
HIGHEST = lax.Precision.HIGHEST


def kernel(
    sizes,
    tracers,
    horiz_from,
    vert_from,
    sunlit_from,
    interaction_from,
    remin_from,
    cell_from,
    chosen_from,
    value_from,
    noise_from,
    var_from,
    out,
    horiz_mix,
    vert_mix,
    sunlit,
    interaction,
    remin,
    obs_cell,
    obs_tile,
    obs_value,
    obs_noise,
    obs_var,
    lit,
    relayed,
    raw,
    mixed,
    states,
    results,
    passed,
    surface,
    partial,
    recv_mid,
    held_group,
    recv_group,
    held_deep,
    recv_deep,
    splats,
    splats_across,
    tail_out,
    tail_in,
    small_sem,
    load_sem,
    edge_sem,
    relay_send,
    relay_recv,
    halo_send,
    halo_recv,
    state_send,
    piece_recv,
    result_send,
    store_sem,
    tail_sem,
    tail_recv,
    mid_sem,
    group_sem,
    deep_sem,
):
    tiles, mids, deeps = sizes
    ntr, levels, rows, cols = tracers.shape[1:]
    pair, quarters = 2, rows // QROWS
    members = 8
    pieces = levels * quarters
    steps = pieces - TAIL
    me = lax.axis_index("member")
    tile = lax.axis_index("space")
    inner = (me == 1) | (me == 2)
    outer = jnp.logical_not(inner)
    group_at = lax.rem(tile, GROUP)
    mid_at = lax.rem(tile // GROUP, mids)
    deep_at = tile // (GROUP * mids)
    half = tiles // 2
    even = lax.rem(tile, 2) == 0
    other_half = lax.rem(tile + half, tiles)
    linked_up, linked_down = tile < tiles - 1, tile > 0
    if deeps > 1:
        linked_up, linked_down = linked_up & (tile != half - 1), linked_down & (tile != half)
    is_up_relay = (tile < half) & (lax.rem(tile, 4) == 2)
    is_down_relay = (tile >= half) & (lax.rem(tile, 4) == 1)

    def up_relay(level):
        return 4 * level + 2

    def down_relay(level):
        return half + 4 * level + 1

    near = jnp.where(me == 0, 1, 2)
    beside = jnp.where(me == 1, 0, 3)
    across = jnp.where(inner, 3 - me, jnp.where(me == 0, 2, 1))

    def mid_tile(j):
        return (deep_at * mids + lax.rem(mid_at + j, mids)) * GROUP + group_at

    def group_tile(j):
        return (deep_at * mids + mid_at) * GROUP + lax.rem(group_at + j, GROUP)

    def load(level, row, sem):
        return pltpu.make_async_copy(tracers.at[:, :, level, row], raw.at[level, row + 1], sem)

    barrier = pltpu.get_barrier_semaphore()
    for j in range(1, 4):
        pl.semaphore_signal(
            barrier, 1, device_id=(lax.rem(me + j, 4), tile), device_id_type=MESH
        )

    @pl.when(linked_down)
    def _():
        pl.semaphore_signal(barrier, 1, device_id=(me, tile - 1), device_id_type=MESH)

    @pl.when(linked_up)
    def _():
        pl.semaphore_signal(barrier, 1, device_id=(me, tile + 1), device_id_type=MESH)

    @pl.when(inner)
    def _():
        for j in range(1, mids):
            pl.semaphore_signal(barrier, 1, device_id=(me, mid_tile(j)), device_id_type=MESH)
        for j in range(1, GROUP):
            pl.semaphore_signal(barrier, 1, device_id=(me, group_tile(j)), device_id_type=MESH)

    if deeps > 1:

        @pl.when(inner & even)
        def _():
            pl.semaphore_signal(barrier, 1, device_id=(me, other_half), device_id_type=MESH)

        @pl.when(tile == half - 1)
        def _():
            for level in range(levels):
                pl.semaphore_signal(
                    barrier, 1, device_id=(me, down_relay(level)), device_id_type=MESH
                )

        @pl.when(tile == half)
        def _():
            for level in range(levels):
                pl.semaphore_signal(
                    barrier, 1, device_id=(me, up_relay(level)), device_id_type=MESH
                )

        @pl.when(is_up_relay)
        def _():
            pl.semaphore_signal(barrier, 1, device_id=(me, half - 1), device_id_type=MESH)

        @pl.when(is_down_relay)
        def _():
            pl.semaphore_signal(barrier, 1, device_id=(me, half), device_id_type=MESH)

    def small(at):
        source, held = (
            (interaction_from, interaction),
            (remin_from, remin),
            (sunlit_from, sunlit),
            (horiz_from, horiz_mix),
            (vert_from, vert_mix),
            (cell_from, obs_cell),
            (chosen_from, obs_tile),
            (value_from, obs_value),
            (noise_from, obs_noise),
            (var_from, obs_var),
        )[at]
        return pltpu.make_async_copy(source, held, small_sem.at[at])

    for at in range(5):
        small(at).start()

    def start_middle(level, carry):
        for row in range(1, rows - 1):
            load(level, row, load_sem.at[level]).start()
        return carry

    def start_edges(level, carry):
        for end in range(2):
            load(level, end * (rows - 1), edge_sem.at[level, end]).start()
        return carry

    lax.fori_loop(0, 2, start_middle, 0)

    def halo_up(level):
        return pltpu.make_async_remote_copy(
            src_ref=raw.at[level, rows],
            dst_ref=raw.at[level, 0],
            send_sem=halo_send.at[0],
            recv_sem=halo_recv.at[level, 0],
            device_id=(me, lax.rem(tile + 1, tiles)),
            device_id_type=MESH,
        )

    def halo_down(level):
        return pltpu.make_async_remote_copy(
            src_ref=raw.at[level, 1],
            dst_ref=raw.at[level, rows + 1],
            send_sem=halo_send.at[1],
            recv_sem=halo_recv.at[level, 1],
            device_id=(me, lax.rem(tile + tiles - 1, tiles)),
            device_id_type=MESH,
        )

    def to_relay(level, row, way, at):
        return pltpu.make_async_remote_copy(
            src_ref=raw.at[level, row],
            dst_ref=relayed,
            send_sem=halo_send.at[way],
            recv_sem=relay_recv,
            device_id=(me, at),
            device_id_type=MESH,
        )

    def from_relay(level, row, way, at):
        return pltpu.make_async_remote_copy(
            src_ref=relayed,
            dst_ref=raw.at[level, row],
            send_sem=relay_send,
            recv_sem=halo_recv.at[level, way],
            device_id=(me, at),
            device_id_type=MESH,
        )

    def pass_on():
        @pl.when(is_up_relay)
        def _():
            level = tile // 4
            to_relay(level, rows, 0, half - 1).wait_recv()
            from_relay(level, 0, 0, half).start()

        @pl.when(is_down_relay)
        def _():
            level = (tile - half) // 4
            to_relay(level, 1, 1, half).wait_recv()
            from_relay(level, rows + 1, 1, half - 1).start()

    def end_pass():
        @pl.when(is_up_relay)
        def _():
            from_relay(tile // 4, 0, 0, half).wait_send()

        @pl.when(is_down_relay)
        def _():
            from_relay((tile - half) // 4, rows + 1, 1, half - 1).wait_send()

    def send_edges(level, carry):
        for end in range(2):
            load(level, end * (rows - 1), edge_sem.at[level, end]).wait()

        @pl.when(linked_up)
        def _():
            halo_up(level).start()

        @pl.when(linked_down)
        def _():
            halo_down(level).start()

        if deeps > 1:

            @pl.when(tile == half - 1)
            def _():
                to_relay(level, rows, 0, up_relay(level)).start()

            @pl.when(tile == half)
            def _():
                to_relay(level, 1, 1, down_relay(level)).start()

        return carry

    lane = lax.broadcasted_iota(jnp.int32, (ntr, cols), 1)

    def mix_row(level, row):
        strength = horiz_mix[level, pl.ds(row, 1), :]
        for m in range(pair):
            own = raw[level, row + 1, m]
            west = jnp.where(lane == 0, own, pltpu.roll(own, 1, 1))
            east = jnp.where(lane == cols - 1, own, pltpu.roll(own, cols - 1, 1))
            laplace = raw[level, row, m] + raw[level, row + 2, m] + west + east - 4.0 * own
            mixed[level, row, m] = own + strength * laplace

    def mix_middle(level):
        middle = raw.at[level, pl.ds(2, rows - 2)]
        pltpu.make_async_copy(middle, middle, load_sem.at[level]).wait()

        def mix_one(row, carry):
            mix_row(level, row)
            return carry

        lax.fori_loop(QROWS, rows - QROWS, mix_one, 0)

    def mix_edges(level):
        @pl.when(tile > 0)
        def _():
            halo_up(level).wait_recv()

        @pl.when(tile == 0)
        def _():
            raw[level, 0] = raw[level, 1]

        @pl.when(tile < tiles - 1)
        def _():
            halo_down(level).wait_recv()

        @pl.when(tile == tiles - 1)
        def _():
            raw[level, rows + 1] = raw[level, rows]

        def mix_two(row, carry):
            mix_row(level, row)
            mix_row(level, rows - 1 - row)
            return carry

        lax.fori_loop(0, QROWS, mix_two, 0)

    def state_copy(piece, to, which):
        level, quarter = piece // quarters, lax.rem(piece, quarters)
        block = states.at[level, quarter, pl.ds(2 * me, 2)]
        return pltpu.make_async_remote_copy(
            src_ref=block,
            dst_ref=block,
            send_sem=state_send.at[which],
            recv_sem=piece_recv.at[piece],
            device_id=(to, tile),
            device_id_type=MESH,
        )

    for at in range(5):
        small(at).wait()
    same = lax.broadcasted_iota(jnp.int32, (ntr, ntr), 0) == lax.broadcasted_iota(
        jnp.int32, (ntr, ntr), 1
    )
    loss = jnp.sum(
        jnp.where(same, jnp.broadcast_to(remin[...], (ntr, ntr)), 0.0), axis=1, keepdims=True
    )
    loss = jnp.broadcast_to(loss, (ntr, cols))
    loss = jnp.concatenate([loss] * (QROWS * pair), axis=1)
    place_from = lax.broadcasted_iota(jnp.int32, (ntr, 3 * ntr), 0)
    place_to = lax.broadcasted_iota(jnp.int32, (ntr, 3 * ntr), 1)
    place = (lax.rem(place_to, ntr) == place_from).astype(F32)
    wide = jnp.dot(interaction[...], place, precision=HIGHEST, preferred_element_type=F32)
    wide_high = wide.astype(jnp.bfloat16).astype(F32)
    taken = jnp.where(place_to < 2 * ntr, wide_high, wide - wide_high).astype(jnp.bfloat16)

    flags = (sunlit[pl.ds(tile * rows // cols, 1), :] > 0).astype(F32)
    flag_lane = lax.broadcasted_iota(jnp.int32, (1, cols), 1)
    for row in range(rows):
        flag = jnp.where(flag_lane == lax.rem(tile * rows, cols) + row, flags, 0.0)
        lit[row : row + 1, :] = jnp.broadcast_to(
            jnp.sum(flag, axis=1, keepdims=True), (1, cols)
        )

    def grow(level, quarter):
        below, above = jnp.minimum(level + 1, levels - 1), jnp.maximum(level - 1, 0)
        light = 0.6 * jnp.exp(-0.4 * jnp.full((1, cols), level, jnp.int32).astype(F32))
        blocks, lights = [], []
        for r in range(QROWS):
            row = quarter * QROWS + r
            down_mix = vert_mix[jnp.minimum(level, levels - 2), pl.ds(row, 1), :]
            up_mix = vert_mix[above, pl.ds(row, 1), :]
            for m in range(pair):
                here = mixed[level, row, m]
                down = down_mix * (mixed[below, row, m] - here)
                up = up_mix * (here - mixed[above, row, m])
                blocks.append(here + down - up)
                lights.append(light * lit[pl.ds(row, 1), :])
        value = jnp.concatenate(blocks, axis=1)
        light = jnp.concatenate(lights, axis=1)
        for _ in range(NSUB):
            high = value.astype(jnp.bfloat16)
            low = (value - high.astype(F32)).astype(jnp.bfloat16)
            uptake = jnp.dot(
                taken, jnp.concatenate([high, low, high], axis=0), preferred_element_type=F32
            )
            value = value + (1.0 / NSUB) * (light * jnp.tanh(uptake) - loss * value)
        for r in range(QROWS):
            for m in range(pair):
                at = (r * pair + m) * cols
                states[level, quarter, 2 * me + m, r] = value[:, at : at + cols]

    def send(level, quarter, whole=True):
        piece = level * quarters + quarter
        @pl.when(whole)
        def _():
            state_copy(piece, across, 0).start()

        @pl.when(outer)
        def _():
            state_copy(piece, near, 1).start()

    lax.fori_loop(0, levels, start_edges, 0)
    lax.fori_loop(2, levels, start_middle, 0)

    @pl.when(inner)
    def _():
        for at in range(5, 10):
            small(at).start()

    mix_middle(0)
    mix_middle(1)
    grow(0, 1)

    peers = 3 + linked_up.astype(jnp.int32) + linked_down.astype(jnp.int32)
    peers += jnp.where(inner, mids + GROUP - 2, 0)
    if deeps > 1:
        peers += (inner & even).astype(jnp.int32)
        peers += (is_up_relay | is_down_relay).astype(jnp.int32)
        peers += jnp.where((tile == half - 1) | (tile == half), levels, 0)
    pl.semaphore_wait(barrier, peers)

    send(0, 1)
    for quarter in range(2, quarters - 1):
        grow(0, quarter)
        send(0, quarter)
    lax.fori_loop(0, levels, send_edges, 0)

    if levels > 2:
        mix_middle(2)

    for quarter in range(1, quarters - 1):
        grow(1, quarter)
        send(1, quarter, whole=False)
    if deeps > 1:
        pass_on()
    mix_edges(0)
    mix_edges(1)
    for quarter in (0, quarters - 1):
        grow(0, quarter)
        send(0, quarter)

    def step_level(level, carry):
        @pl.when(level < levels - 1)
        def _():
            mix_middle(level + 1)

        for quarter in range(1, quarters - 1):
            grow(level, quarter)
            send(level, quarter, whole=level > TAIL_LEVELS)
        mix_edges(level)
        for quarter in (0, quarters - 1):
            grow(level - 1, quarter)
            send(level - 1, quarter)
        return carry

    lax.fori_loop(2, levels, step_level, 0)
    for quarter in (0, quarters - 1):
        grow(levels - 1, quarter)
        send(levels - 1, quarter)

    def in_order(step):
        edge = step - 2
        later = edge - TAIL
        level, turn = TAIL_LEVELS + 1 + later // 4, lax.rem(later, 4)
        piece = jnp.where(
            turn < 2, level * quarters + 1 + turn, (level - 1) * quarters + 3 * (turn - 2)
        )
        piece = jnp.where(
            edge < TAIL, edge // 2 * quarters + 3 * lax.rem(edge, 2), piece
        )
        piece = jnp.where(step < 2, 1 + step, piece)
        ending = step - (steps - 2)
        return jnp.where(ending < 0, piece, (levels - 1) * quarters + 3 * ending)

    def sent(source, sem):
        pltpu.make_async_remote_copy(
            src_ref=source,
            dst_ref=source,
            send_sem=sem,
            recv_sem=sem,
            device_id=(3 - me, tile),
            device_id_type=MESH,
        ).wait_send()

    def landed(target, sem):
        pltpu.make_async_remote_copy(
            src_ref=target,
            dst_ref=target,
            send_sem=sem,
            recv_sem=sem,
            device_id=(3 - me, tile),
            device_id_type=MESH,
        ).wait_recv()

    def wait_states(piece):
        level, quarter = piece // quarters, lax.rem(piece, quarters)
        landed(states.at[level, quarter, pl.ds(0, members - pair)], piece_recv.at[piece])

    def result_copy(piece):
        return pltpu.make_async_remote_copy(
            src_ref=passed.at[piece],
            dst_ref=results.at[piece],
            send_sem=result_send,
            recv_sem=piece_recv.at[piece],
            device_id=(beside, tile),
            device_id_type=MESH,
        )

    def stores(piece):
        level, quarter = piece // quarters, lax.rem(piece, quarters)
        return [
            pltpu.make_async_copy(
                results.at[piece, r],
                out.at[:, :, level, quarter * QROWS + r],
                store_sem,
            )
            for r in range(QROWS)
        ]

    def small_copy(source, target, send, recv, at):
        return pltpu.make_async_remote_copy(
            src_ref=source,
            dst_ref=target,
            send_sem=send,
            recv_sem=recv,
            device_id=(me, at),
            device_id_type=MESH,
        )

    def partial_sums():
        for quarter in range(quarters):
            for r in range(QROWS):
                for m in range(members):
                    at = (quarter * QROWS + r) * members + m
                    surface[at : at + 1, :] = states[0, quarter, m, r, 0:1, :]
        picked_from = surface[...]
        width = OBS_STEP // cols
        column_ids = lax.broadcasted_iota(jnp.int32, (cols, OBS_STEP), 0)
        tile_ids = lax.broadcasted_iota(jnp.int32, (tiles, OBS_STEP), 0)

        def flat(ref, step):
            return jnp.concatenate(
                [ref[pl.ds(step * width + i, 1), :] for i in range(width)], axis=1
            )

        def step_obs(step, total):
            local = flat(obs_cell, step) - tile * (rows * cols)
            column = jnp.bitwise_and(local, cols - 1)
            row_of = jnp.right_shift(local, cols.bit_length() - 1)
            one_hot = (column_ids == column).astype(F32)
            picked = jnp.dot(
                picked_from, one_hot, precision=HIGHEST, preferred_element_type=F32
            )
            observed = jnp.zeros((members, OBS_STEP), F32)
            for r in range(rows):
                observed += jnp.where(
                    row_of == r, picked[r * members : (r + 1) * members], 0.0
                )
            inside = (row_of >= 0) & (row_of < rows)
            weight = jnp.where(inside, 1.0 / flat(obs_var, step), 0.0)
            spread = observed - jnp.sum(observed, axis=0, keepdims=True) * (1.0 / members)
            noise = obs_noise[:, pl.ds(pl.multiple_of(step * OBS_STEP, OBS_STEP), OBS_STEP)]
            innov = flat(obs_value, step) + noise - observed
            scaled = spread * weight
            both = jnp.concatenate([spread, innov], axis=0)
            products = jnp.concatenate(
                [scaled[a : a + 1] * both for a in range(members)], axis=0
            )
            chosen = (tile_ids == flat(obs_tile, step)).astype(F32)
            return total + lax.dot_general(
                chosen,
                products,
                (((1,), (1,)), ((), ())),
                precision=HIGHEST,
                preferred_element_type=F32,
            )

        steps = obs_noise.shape[1] // OBS_STEP
        total = lax.fori_loop(0, steps, step_obs, jnp.zeros((tiles, 128), F32))
        for d in range(deeps):
            for b in range(mids):
                at = (d * mids + b) * GROUP
                partial[b, d] = total[at : at + GROUP]

        sums = partial[mid_at]
        if mids > 1:
            for j in range(1, mids):
                small_copy(
                    partial.at[lax.rem(mid_at + j, mids)],
                    recv_mid.at[mid_at],
                    mid_sem.at[0],
                    mid_sem.at[1],
                    mid_tile(j),
                ).start()
            landed(recv_mid.at[pl.ds(0, mids - 1)], mid_sem.at[1])
            for j in range(1, mids):
                sums = sums + recv_mid[lax.rem(mid_at + j, mids)]
        held_group[...] = sums
        for j in range(1, GROUP):
            small_copy(
                held_group,
                recv_group.at[group_at],
                group_sem.at[0],
                group_sem.at[1],
                group_tile(j),
            ).start()
        landed(recv_group.at[pl.ds(0, GROUP - 1)], group_sem.at[1])
        for j in range(1, GROUP):
            sums = sums + recv_group[lax.rem(group_at + j, GROUP)]
        if mids > 1:
            sent(partial.at[pl.ds(0, mids - 1)], mid_sem.at[0])
        sent(recv_group.at[pl.ds(0, GROUP - 1)], group_sem.at[0])
        if deeps == 1:
            return sums[0]
        held_deep[...] = sums
        across_half = small_copy(
            held_deep.at[1 - deep_at], recv_deep, deep_sem.at[0], deep_sem.at[1], other_half
        )
        handed = small_copy(
            recv_deep, recv_deep, deep_sem.at[0], deep_sem.at[1], jnp.minimum(tile + 1, tiles - 1)
        )

        @pl.when(even)
        def _():
            across_half.start()
            across_half.wait()
            handed.start()
            handed.wait_send()

        @pl.when(jnp.logical_not(even))
        def _():
            handed.wait_recv()

        sums = held_deep[deep_at] + recv_deep[...]
        return sums

    def weights_of(sums):
        sub = lax.broadcasted_iota(jnp.int32, (8, 128), 0)
        lane8 = lax.broadcasted_iota(jnp.int32, (8, 128), 1)
        own = jnp.sum(jnp.where(sub == group_at, sums, 0.0), axis=0, keepdims=True)
        parts = jnp.where(
            jnp.right_shift(lane8, 4) == sub, jnp.broadcast_to(own, (8, 128)), 0.0
        )
        fold_from = lax.broadcasted_iota(jnp.int32, (128, 128), 0)
        fold_to = lax.broadcasted_iota(jnp.int32, (128, 128), 1)
        fold = (jnp.bitwise_and(fold_from, 15) == fold_to).astype(F32)
        system = jnp.dot(parts, fold, precision=HIGHEST, preferred_element_type=F32)
        system = system + jnp.where(lane8 == sub, float(members - 1), 0.0)
        for k in range(members):
            column = jnp.sum(jnp.where(lane8 == k, system, 0.0), axis=1, keepdims=True)
            pivot = system[k : k + 1] / column[k : k + 1]
            system = jnp.where(sub == k, pivot, system - column * pivot)
        return system - jnp.sum(system, axis=0, keepdims=True) * (1.0 / members)

    def spread_weights(centered):
        sub = lax.broadcasted_iota(jnp.int32, (8, 128), 0)
        lane8 = lax.broadcasted_iota(jnp.int32, (8, 128), 1)
        for j in range(4):
            member = 2 * me + j if j < 2 else 2 * beside + j - 2
            column = jnp.sum(
                jnp.where(lane8 == members + member, centered, 0.0), axis=1, keepdims=True
            )
            wide = jnp.broadcast_to(column, (8, 128))
            wide = wide + jnp.where(sub == member, 1.0, 0.0)
            for k in range(members):
                splats[j, k] = jnp.broadcast_to(wide[k : k + 1], (8, 128))

        for j in range(4):
            member = 2 * across + j if j < 2 else 2 * (3 - beside) + j - 2
            column = jnp.sum(
                jnp.where(lane8 == members + member, centered, 0.0), axis=1, keepdims=True
            )
            wide = jnp.broadcast_to(column, (8, 128))
            for k in range(4):
                source = 2 * me + k if k < 2 else 2 * beside + k - 2
                row = jnp.sum(jnp.where(sub == source, wide, 0.0), axis=0, keepdims=True)
                splats_across[j, k] = jnp.broadcast_to(row, (8, 128))

    def tail_piece(at):
        return (1 + at // 2) * quarters + 1 + at % 2

    def tail_copy(at, to, which):
        return pltpu.make_async_remote_copy(
            src_ref=tail_out.at[at, which],
            dst_ref=tail_in.at[at],
            send_sem=tail_sem,
            recv_sem=tail_recv.at[at],
            device_id=(to, tile),
            device_id_type=MESH,
        )

    def analyse_tail(at):
        piece = tail_piece(at)
        level, quarter = 1 + at // 2, 1 + at % 2
        near_states = states.at[level, quarter, pl.ds(0, pair)]
        landed(near_states, piece_recv.at[piece])

        def tail_part(part, carry):
            r, first = part // (ntr // 8), pl.multiple_of(lax.rem(part, ntr // 8) * 8, 8)
            values = [
                states[level, quarter, 2 * source + k, r, pl.ds(first, 8), :]
                for source in (me, beside)
                for k in range(pair)
            ]
            for j in range(4):
                same_side, other_side = None, None
                for k in range(4):
                    source = 2 * me + k if k < 2 else 2 * beside + k - 2
                    here = values[k] * splats[j, source]
                    there = values[k] * splats_across[j, k]
                    same_side = here if k == 0 else same_side + here
                    other_side = there if k == 0 else other_side + there
                target = results if j < 2 else passed
                target[piece, r, j % 2, pl.ds(first, 8), :] = same_side
                tail_out[at, j // 2, r, j % 2, pl.ds(first, 8), :] = other_side
            return carry

        lax.fori_loop(0, QROWS * (ntr // 8), tail_part, 0)
        result_copy(piece).start()

    def finish_tail(at):
        piece = tail_piece(at)
        landed(tail_in.at[at], tail_recv.at[at])
        results[piece] = results[piece] + tail_in[at]
        for store in stores(piece):
            store.start()

    def analyse(piece):
        level, quarter = piece // quarters, lax.rem(piece, quarters)

        def analyse_part(at, carry):
            r, first = at // (ntr // 8), pl.multiple_of(lax.rem(at, ntr // 8) * 8, 8)
            sums = [None] * 4
            for k in range(members):
                value = states[level, quarter, k, r, pl.ds(first, 8), :]
                for j in range(4):
                    term = value * splats[j, k]
                    sums[j] = term if k == 0 else sums[j] + term
            for m in range(pair):
                results[piece, r, m, pl.ds(first, 8), :] = sums[m]
                passed[piece, r, m, pl.ds(first, 8), :] = sums[2 + m]
            return carry

        lax.fori_loop(0, QROWS * (ntr // 8), analyse_part, 0)
        result_copy(piece).start()
        for store in stores(piece):
            store.start()

    own_states = states.at[:, :, pl.ds(2 * me, 2)]

    @pl.when(tile < tiles - 1)
    def _():
        sent(raw.at[:, rows], halo_send.at[0])

    @pl.when(tile > 0)
    def _():
        sent(raw.at[:, 1], halo_send.at[1])

    if deeps > 1:
        end_pass()

    @pl.when(inner)
    def _():
        for at in range(5, 10):
            small(at).wait()
        for quarter in range(1, quarters - 1):
            wait_states(quarter)
        for quarter in (0, quarters - 1):
            wait_states(quarter)
        spread_weights(weights_of(partial_sums()))
        for at in range(TAIL):
            analyse_tail(at)

        def analyse_next(step, carry):
            piece = in_order(step)

            @pl.when(piece >= quarters)
            def _():
                wait_states(piece)

            analyse(piece)

            @pl.when(step == steps - AHEAD)
            def _():
                for at in range(TAIL):
                    tail_copy(at, 3 - beside, 1).start()
                for at in range(TAIL):
                    tail_copy(at, across, 0).start()

            return carry

        lax.fori_loop(0, steps, analyse_next, 0)
        for at in range(TAIL):
            finish_tail(at)
        sent(tail_out, tail_sem)
        sent(passed, result_send)
        sent(passed.at[pl.ds(0, steps)], state_send.at[0])

    @pl.when(outer)
    def _():
        def take(step, carry):
            piece = in_order(step)
            result_copy(piece).wait_recv()
            for store in stores(piece):
                store.start()
            return carry

        lax.fori_loop(0, steps, take, 0)
        for at in range(TAIL):
            result_copy(tail_piece(at)).wait_recv()
            finish_tail(at)
        sent(passed.at[pl.ds(0, steps)], state_send.at[0])
        sent(own_states, state_send.at[1])

    pltpu.make_async_copy(results, results, store_sem).wait()


def on_device(
    tracers,
    horiz_mix,
    vert_mix,
    sunlit,
    interaction,
    remin,
    obs_cell,
    obs_tile,
    obs_value,
    obs_noise,
    obs_var,
):
    pair, ntr, levels, rows, cols = tracers.shape
    tiles = lax.axis_size("space")
    deeps = DEEP if tiles > GROUP else 1
    mids = tiles // (deeps * GROUP)
    quarters = rows // QROWS
    pieces = levels * quarters
    count = obs_cell.shape[0]
    obs_rows = (count // cols, cols)
    pinned = pl.BlockSpec(memory_space=pltpu.HBM)
    anywhere = pl.BlockSpec(memory_space=pl.ANY)
    dma = pltpu.SemaphoreType.DMA
    operands = (
        tracers,
        horiz_mix,
        vert_mix,
        sunlit.reshape(-1, cols),
        interaction,
        remin.reshape(1, ntr),
        obs_cell.reshape(obs_rows),
        obs_tile.reshape(obs_rows),
        obs_value.reshape(obs_rows),
        obs_noise,
        obs_var.reshape(obs_rows),
    )
    operands = [pltpu.with_memory_space_constraint(value, pltpu.HBM) for value in operands]
    return pl.pallas_call(
        functools.partial(kernel, (tiles, mids, deeps)),
        out_shape=jax.ShapeDtypeStruct(tracers.shape, F32),
        in_specs=[pinned] * len(operands),
        out_specs=anywhere,
        scratch_shapes=[
            *[pltpu.VMEM(value.shape, value.dtype) for value in operands[1:]],
            pltpu.VMEM((rows, cols), F32),
            pltpu.VMEM((pair, ntr, cols), F32),
            pltpu.VMEM((levels, rows + 2, pair, ntr, cols), F32),
            pltpu.VMEM((levels, rows, pair, ntr, cols), F32),
            pltpu.VMEM((levels, quarters, 8, QROWS, ntr, cols), F32),
            pltpu.VMEM((pieces, QROWS, pair, ntr, cols), F32),
            pltpu.VMEM((pieces, QROWS, pair, ntr, cols), F32),
            pltpu.VMEM((rows * 8, cols), F32),
            pltpu.VMEM((mids, deeps, GROUP, 128), F32),
            pltpu.VMEM((mids, deeps, GROUP, 128), F32),
            pltpu.VMEM((deeps, GROUP, 128), F32),
            pltpu.VMEM((GROUP, deeps, GROUP, 128), F32),
            pltpu.VMEM((deeps, GROUP, 128), F32),
            pltpu.VMEM((GROUP, 128), F32),
            pltpu.VMEM((4, 8, 8, 128), F32),
            pltpu.VMEM((4, 4, 8, 128), F32),
            pltpu.VMEM((TAIL, 2, QROWS, pair, ntr, cols), F32),
            pltpu.VMEM((TAIL, QROWS, pair, ntr, cols), F32),
            dma((10,)),
            dma((levels,)),
            dma((levels, 2)),
            dma,
            dma,
            dma((2,)),
            dma((levels, 2)),
            dma((2,)),
            dma((pieces,)),
            dma,
            dma,
            dma,
            dma((TAIL,)),
            dma((2,)),
            dma((2,)),
            dma((2,)),
        ],
        compiler_params=pltpu.CompilerParams(
            collective_id=0, has_side_effects=True, vmem_limit_bytes=VMEM_BYTES
        ),
        cost_estimate=pl.CostEstimate(
            flops=500_000_000, bytes_accessed=8_000_000, transcendentals=3_000_000
        ),
        name="step_and_analysis",
    )(*operands)


def solution(mesh):
    return jax.shard_map(
        on_device,
        mesh=mesh,
        in_specs=(
            P("member", None, None, "space", None),
            P(None, "space", None),
            P(None, "space", None),
            P(),
            P(),
            P(),
            P(),
            P(),
            P(),
            P(),
            P(),
        ),
        out_specs=P("member", None, None, "space", None),
        check_vma=False,
    )
```

```python
import functools

import jax
import jax.numpy as jnp
from jax import lax
from jax.experimental import pallas as pl
from jax.experimental.pallas import tpu as pltpu
from jax.sharding import PartitionSpec as P

NSUB = 4
GROUP = 8
DEEP = 2
TAIL_LEVELS = 2
TAIL_FROM = 3
TAIL = 2 * TAIL_LEVELS
AHEAD = 9
QROWS = 2
VMEM_BYTES = 34 * 1024 * 1024
OBS_STEP = 512
F32 = jnp.float32
MESH = pl.DeviceIdType.MESH
HIGHEST = lax.Precision.HIGHEST


def kernel(
    sizes,
    tracers,
    horiz_from,
    vert_from,
    sunlit_from,
    interaction_from,
    remin_from,
    cell_from,
    chosen_from,
    value_from,
    noise_from,
    var_from,
    out,
    horiz_mix,
    vert_mix,
    sunlit,
    interaction,
    remin,
    obs_cell,
    obs_tile,
    obs_value,
    obs_noise,
    obs_var,
    lit,
    relayed,
    raw,
    mixed,
    states,
    results,
    passed,
    surface,
    partial,
    recv_mid,
    held_group,
    recv_group,
    held_deep,
    recv_deep,
    splats,
    splats_across,
    tail_out,
    tail_in,
    small_sem,
    load_sem,
    edge_sem,
    relay_send,
    relay_recv,
    halo_send,
    halo_recv,
    state_send,
    piece_recv,
    result_send,
    store_sem,
    tail_sem,
    tail_recv,
    mid_sem,
    group_sem,
    deep_sem,
):
    tiles, mids, deeps = sizes
    ntr, levels, rows, cols = tracers.shape[1:]
    pair, quarters = 2, rows // QROWS
    members = 8
    pieces = levels * quarters
    steps = pieces - TAIL
    me = lax.axis_index("member")
    tile = lax.axis_index("space")
    inner = (me == 1) | (me == 2)
    outer = jnp.logical_not(inner)
    group_at = lax.rem(tile, GROUP)
    mid_at = lax.rem(tile // GROUP, mids)
    deep_at = tile // (GROUP * mids)
    half = tiles // 2
    even = lax.rem(tile, 2) == 0
    other_half = lax.rem(tile + half, tiles)
    linked_up, linked_down = tile < tiles - 1, tile > 0
    if deeps > 1:
        linked_up, linked_down = linked_up & (tile != half - 1), linked_down & (tile != half)
    is_up_relay = (tile < half) & (lax.rem(tile, 4) == 2)
    is_down_relay = (tile >= half) & (lax.rem(tile, 4) == 1)

    def up_relay(level):
        return 4 * level + 2

    def down_relay(level):
        return half + 4 * level + 1

    near = jnp.where(me == 0, 1, 2)
    beside = jnp.where(me == 1, 0, 3)
    across = jnp.where(inner, 3 - me, jnp.where(me == 0, 2, 1))

    def mid_tile(j):
        return (deep_at * mids + lax.rem(mid_at + j, mids)) * GROUP + group_at

    def group_tile(j):
        return (deep_at * mids + mid_at) * GROUP + lax.rem(group_at + j, GROUP)

    def load(level, row, sem):
        return pltpu.make_async_copy(tracers.at[:, :, level, row], raw.at[level, row + 1], sem)

    barrier = pltpu.get_barrier_semaphore()
    for j in range(1, 4):
        pl.semaphore_signal(
            barrier, 1, device_id=(lax.rem(me + j, 4), tile), device_id_type=MESH
        )

    @pl.when(linked_down)
    def _():
        pl.semaphore_signal(barrier, 1, device_id=(me, tile - 1), device_id_type=MESH)

    @pl.when(linked_up)
    def _():
        pl.semaphore_signal(barrier, 1, device_id=(me, tile + 1), device_id_type=MESH)

    @pl.when(inner)
    def _():
        for j in range(1, mids):
            pl.semaphore_signal(barrier, 1, device_id=(me, mid_tile(j)), device_id_type=MESH)
        for j in range(1, GROUP):
            pl.semaphore_signal(barrier, 1, device_id=(me, group_tile(j)), device_id_type=MESH)

    if deeps > 1:

        @pl.when(inner & even)
        def _():
            pl.semaphore_signal(barrier, 1, device_id=(me, other_half), device_id_type=MESH)

        @pl.when(tile == half - 1)
        def _():
            for level in range(levels):
                pl.semaphore_signal(
                    barrier, 1, device_id=(me, down_relay(level)), device_id_type=MESH
                )

        @pl.when(tile == half)
        def _():
            for level in range(levels):
                pl.semaphore_signal(
                    barrier, 1, device_id=(me, up_relay(level)), device_id_type=MESH
                )

        @pl.when(is_up_relay)
        def _():
            pl.semaphore_signal(barrier, 1, device_id=(me, half - 1), device_id_type=MESH)

        @pl.when(is_down_relay)
        def _():
            pl.semaphore_signal(barrier, 1, device_id=(me, half), device_id_type=MESH)

    def small(at):
        source, held = (
            (interaction_from, interaction),
            (remin_from, remin),
            (sunlit_from, sunlit),
            (horiz_from, horiz_mix),
            (vert_from, vert_mix),
            (cell_from, obs_cell),
            (chosen_from, obs_tile),
            (value_from, obs_value),
            (noise_from, obs_noise),
            (var_from, obs_var),
        )[at]
        return pltpu.make_async_copy(source, held, small_sem.at[at])

    for at in range(5):
        small(at).start()

    def start_middle(level, carry):
        for row in range(1, rows - 1):
            load(level, row, load_sem.at[level]).start()
        return carry

    def start_edges(level, carry):
        for end in range(2):
            load(level, end * (rows - 1), edge_sem.at[level, end]).start()
        return carry

    lax.fori_loop(0, 2, start_middle, 0)

    def halo_up(level):
        return pltpu.make_async_remote_copy(
            src_ref=raw.at[level, rows],
            dst_ref=raw.at[level, 0],
            send_sem=halo_send.at[0],
            recv_sem=halo_recv.at[level, 0],
            device_id=(me, lax.rem(tile + 1, tiles)),
            device_id_type=MESH,
        )

    def halo_down(level):
        return pltpu.make_async_remote_copy(
            src_ref=raw.at[level, 1],
            dst_ref=raw.at[level, rows + 1],
            send_sem=halo_send.at[1],
            recv_sem=halo_recv.at[level, 1],
            device_id=(me, lax.rem(tile + tiles - 1, tiles)),
            device_id_type=MESH,
        )

    def to_relay(level, row, way, at):
        return pltpu.make_async_remote_copy(
            src_ref=raw.at[level, row],
            dst_ref=relayed,
            send_sem=halo_send.at[way],
            recv_sem=relay_recv,
            device_id=(me, at),
            device_id_type=MESH,
        )

    def from_relay(level, row, way, at):
        return pltpu.make_async_remote_copy(
            src_ref=relayed,
            dst_ref=raw.at[level, row],
            send_sem=relay_send,
            recv_sem=halo_recv.at[level, way],
            device_id=(me, at),
            device_id_type=MESH,
        )

    def pass_on():
        @pl.when(is_up_relay)
        def _():
            level = tile // 4
            to_relay(level, rows, 0, half - 1).wait_recv()
            from_relay(level, 0, 0, half).start()

        @pl.when(is_down_relay)
        def _():
            level = (tile - half) // 4
            to_relay(level, 1, 1, half).wait_recv()
            from_relay(level, rows + 1, 1, half - 1).start()

    def end_pass():
        @pl.when(is_up_relay)
        def _():
            from_relay(tile // 4, 0, 0, half).wait_send()

        @pl.when(is_down_relay)
        def _():
            from_relay((tile - half) // 4, rows + 1, 1, half - 1).wait_send()

    def send_edges(level, carry):
        for end in range(2):
            load(level, end * (rows - 1), edge_sem.at[level, end]).wait()

        @pl.when(linked_up)
        def _():
            halo_up(level).start()

        @pl.when(linked_down)
        def _():
            halo_down(level).start()

        if deeps > 1:

            @pl.when(tile == half - 1)
            def _():
                to_relay(level, rows, 0, up_relay(level)).start()

            @pl.when(tile == half)
            def _():
                to_relay(level, 1, 1, down_relay(level)).start()

        return carry

    lane = lax.broadcasted_iota(jnp.int32, (ntr, cols), 1)

    def mix_row(level, row):
        strength = horiz_mix[level, pl.ds(row, 1), :]
        for m in range(pair):
            own = raw[level, row + 1, m]
            west = jnp.where(lane == 0, own, pltpu.roll(own, 1, 1))
            east = jnp.where(lane == cols - 1, own, pltpu.roll(own, cols - 1, 1))
            laplace = raw[level, row, m] + raw[level, row + 2, m] + west + east - 4.0 * own
            mixed[level, row, m] = own + strength * laplace

    def mix_middle(level):
        middle = raw.at[level, pl.ds(2, rows - 2)]
        pltpu.make_async_copy(middle, middle, load_sem.at[level]).wait()

        def mix_one(row, carry):
            mix_row(level, row)
            return carry

        lax.fori_loop(QROWS, rows - QROWS, mix_one, 0)

    def mix_edges(level):
        @pl.when(tile > 0)
        def _():
            halo_up(level).wait_recv()

        @pl.when(tile == 0)
        def _():
            raw[level, 0] = raw[level, 1]

        @pl.when(tile < tiles - 1)
        def _():
            halo_down(level).wait_recv()

        @pl.when(tile == tiles - 1)
        def _():
            raw[level, rows + 1] = raw[level, rows]

        def mix_two(row, carry):
            mix_row(level, row)
            mix_row(level, rows - 1 - row)
            return carry

        lax.fori_loop(0, QROWS, mix_two, 0)

    def state_copy(piece, to, which):
        level, quarter = piece // quarters, lax.rem(piece, quarters)
        block = states.at[level, quarter, pl.ds(2 * me, 2)]
        return pltpu.make_async_remote_copy(
            src_ref=block,
            dst_ref=block,
            send_sem=state_send.at[which],
            recv_sem=piece_recv.at[piece],
            device_id=(to, tile),
            device_id_type=MESH,
        )

    for at in range(5):
        small(at).wait()
    same = lax.broadcasted_iota(jnp.int32, (ntr, ntr), 0) == lax.broadcasted_iota(
        jnp.int32, (ntr, ntr), 1
    )
    loss = jnp.sum(
        jnp.where(same, jnp.broadcast_to(remin[...], (ntr, ntr)), 0.0), axis=1, keepdims=True
    )
    loss = jnp.broadcast_to(loss, (ntr, cols))
    loss = jnp.concatenate([loss] * (QROWS * pair), axis=1)
    place_from = lax.broadcasted_iota(jnp.int32, (ntr, 3 * ntr), 0)
    place_to = lax.broadcasted_iota(jnp.int32, (ntr, 3 * ntr), 1)
    place = (lax.rem(place_to, ntr) == place_from).astype(F32)
    wide = jnp.dot(interaction[...], place, precision=HIGHEST, preferred_element_type=F32)
    wide_high = wide.astype(jnp.bfloat16).astype(F32)
    taken = jnp.where(place_to < 2 * ntr, wide_high, wide - wide_high).astype(jnp.bfloat16)

    flags = (sunlit[pl.ds(tile * rows // cols, 1), :] > 0).astype(F32)
    flag_lane = lax.broadcasted_iota(jnp.int32, (1, cols), 1)
    for row in range(rows):
        flag = jnp.where(flag_lane == lax.rem(tile * rows, cols) + row, flags, 0.0)
        lit[row : row + 1, :] = jnp.broadcast_to(
            jnp.sum(flag, axis=1, keepdims=True), (1, cols)
        )

    def grow(level, quarter):
        below, above = jnp.minimum(level + 1, levels - 1), jnp.maximum(level - 1, 0)
        light = 0.6 * jnp.exp(-0.4 * jnp.full((1, cols), level, jnp.int32).astype(F32))
        blocks, lights = [], []
        for r in range(QROWS):
            row = quarter * QROWS + r
            down_mix = vert_mix[jnp.minimum(level, levels - 2), pl.ds(row, 1), :]
            up_mix = vert_mix[above, pl.ds(row, 1), :]
            for m in range(pair):
                here = mixed[level, row, m]
                down = down_mix * (mixed[below, row, m] - here)
                up = up_mix * (here - mixed[above, row, m])
                blocks.append(here + down - up)
                lights.append(light * lit[pl.ds(row, 1), :])
        value = jnp.concatenate(blocks, axis=1)
        light = jnp.concatenate(lights, axis=1)
        for _ in range(NSUB):
            high = value.astype(jnp.bfloat16)
            low = (value - high.astype(F32)).astype(jnp.bfloat16)
            uptake = jnp.dot(
                taken, jnp.concatenate([high, low, high], axis=0), preferred_element_type=F32
            )
            value = value + (1.0 / NSUB) * (light * jnp.tanh(uptake) - loss * value)
        for r in range(QROWS):
            for m in range(pair):
                at = (r * pair + m) * cols
                states[level, quarter, 2 * me + m, r] = value[:, at : at + cols]

    def send(level, quarter, whole=True):
        piece = level * quarters + quarter
        @pl.when(whole)
        def _():
            state_copy(piece, across, 0).start()

        @pl.when(outer)
        def _():
            state_copy(piece, near, 1).start()

    lax.fori_loop(0, levels, start_edges, 0)
    lax.fori_loop(2, levels, start_middle, 0)

    @pl.when(inner)
    def _():
        for at in range(5, 10):
            small(at).start()

    mix_middle(0)
    mix_middle(1)
    grow(0, 1)

    peers = 3 + linked_up.astype(jnp.int32) + linked_down.astype(jnp.int32)
    peers += jnp.where(inner, mids + GROUP - 2, 0)
    if deeps > 1:
        peers += (inner & even).astype(jnp.int32)
        peers += (is_up_relay | is_down_relay).astype(jnp.int32)
        peers += jnp.where((tile == half - 1) | (tile == half), levels, 0)
    pl.semaphore_wait(barrier, peers)

    send(0, 1)
    for quarter in range(2, quarters - 1):
        grow(0, quarter)
        send(0, quarter)
    lax.fori_loop(0, levels, send_edges, 0)

    if levels > 2:
        mix_middle(2)

    for quarter in range(1, quarters - 1):
        grow(1, quarter)
        send(1, quarter, whole=TAIL_FROM > 1)
    if deeps > 1:
        pass_on()
    mix_edges(0)
    mix_edges(1)
    for quarter in (0, quarters - 1):
        grow(0, quarter)
        send(0, quarter)

    def step_level(level, carry):
        @pl.when(level < levels - 1)
        def _():
            mix_middle(level + 1)

        for quarter in range(1, quarters - 1):
            grow(level, quarter)
            send(level, quarter, whole=(level < TAIL_FROM) | (level >= TAIL_FROM + TAIL_LEVELS))
        mix_edges(level)
        for quarter in (0, quarters - 1):
            grow(level - 1, quarter)
            send(level - 1, quarter)
        return carry

    lax.fori_loop(2, levels, step_level, 0)
    for quarter in (0, quarters - 1):
        grow(levels - 1, quarter)
        send(levels - 1, quarter)

    def in_order(step):
        for turn in range(TAIL_LEVELS):
            step = jnp.where(step >= 4 * (TAIL_FROM + turn) - 2, step + 2, step)
        later = step - 2
        level, turn = 1 + later // 4, lax.rem(later, 4)
        piece = jnp.where(
            turn < 2, level * quarters + 1 + turn, (level - 1) * quarters + 3 * (turn - 2)
        )
        piece = jnp.where(step < 2, 1 + step, piece)
        ending = step - (pieces - 2)
        return jnp.where(ending < 0, piece, (levels - 1) * quarters + 3 * ending)

    def sent(source, sem):
        pltpu.make_async_remote_copy(
            src_ref=source,
            dst_ref=source,
            send_sem=sem,
            recv_sem=sem,
            device_id=(3 - me, tile),
            device_id_type=MESH,
        ).wait_send()

    def landed(target, sem):
        pltpu.make_async_remote_copy(
            src_ref=target,
            dst_ref=target,
            send_sem=sem,
            recv_sem=sem,
            device_id=(3 - me, tile),
            device_id_type=MESH,
        ).wait_recv()

    def wait_states(piece):
        level, quarter = piece // quarters, lax.rem(piece, quarters)
        landed(states.at[level, quarter, pl.ds(0, members - pair)], piece_recv.at[piece])

    def result_copy(piece):
        return pltpu.make_async_remote_copy(
            src_ref=passed.at[piece],
            dst_ref=results.at[piece],
            send_sem=result_send,
            recv_sem=piece_recv.at[piece],
            device_id=(beside, tile),
            device_id_type=MESH,
        )

    def stores(piece):
        level, quarter = piece // quarters, lax.rem(piece, quarters)
        return [
            pltpu.make_async_copy(
                results.at[piece, r],
                out.at[:, :, level, quarter * QROWS + r],
                store_sem,
            )
            for r in range(QROWS)
        ]

    def small_copy(source, target, send, recv, at):
        return pltpu.make_async_remote_copy(
            src_ref=source,
            dst_ref=target,
            send_sem=send,
            recv_sem=recv,
            device_id=(me, at),
            device_id_type=MESH,
        )

    def partial_sums():
        for quarter in range(quarters):
            for r in range(QROWS):
                for m in range(members):
                    at = (quarter * QROWS + r) * members + m
                    surface[at : at + 1, :] = states[0, quarter, m, r, 0:1, :]
        picked_from = surface[...]
        width = OBS_STEP // cols
        column_ids = lax.broadcasted_iota(jnp.int32, (cols, OBS_STEP), 0)
        tile_ids = lax.broadcasted_iota(jnp.int32, (tiles, OBS_STEP), 0)

        def flat(ref, step):
            return jnp.concatenate(
                [ref[pl.ds(step * width + i, 1), :] for i in range(width)], axis=1
            )

        def step_obs(step, total):
            local = flat(obs_cell, step) - tile * (rows * cols)
            column = jnp.bitwise_and(local, cols - 1)
            row_of = jnp.right_shift(local, cols.bit_length() - 1)
            one_hot = (column_ids == column).astype(F32)
            picked = jnp.dot(
                picked_from, one_hot, precision=HIGHEST, preferred_element_type=F32
            )
            observed = jnp.zeros((members, OBS_STEP), F32)
            for r in range(rows):
                observed += jnp.where(
                    row_of == r, picked[r * members : (r + 1) * members], 0.0
                )
            inside = (row_of >= 0) & (row_of < rows)
            weight = jnp.where(inside, 1.0 / flat(obs_var, step), 0.0)
            spread = observed - jnp.sum(observed, axis=0, keepdims=True) * (1.0 / members)
            noise = obs_noise[:, pl.ds(pl.multiple_of(step * OBS_STEP, OBS_STEP), OBS_STEP)]
            innov = flat(obs_value, step) + noise - observed
            scaled = spread * weight
            both = jnp.concatenate([spread, innov], axis=0)
            products = jnp.concatenate(
                [scaled[a : a + 1] * both for a in range(members)], axis=0
            )
            chosen = (tile_ids == flat(obs_tile, step)).astype(F32)
            return total + lax.dot_general(
                chosen,
                products,
                (((1,), (1,)), ((), ())),
                precision=HIGHEST,
                preferred_element_type=F32,
            )

        steps = obs_noise.shape[1] // OBS_STEP
        total = lax.fori_loop(0, steps, step_obs, jnp.zeros((tiles, 128), F32))
        for d in range(deeps):
            for b in range(mids):
                at = (d * mids + b) * GROUP
                partial[b, d] = total[at : at + GROUP]

        sums = partial[mid_at]
        if mids > 1:
            for j in range(1, mids):
                small_copy(
                    partial.at[lax.rem(mid_at + j, mids)],
                    recv_mid.at[mid_at],
                    mid_sem.at[0],
                    mid_sem.at[1],
                    mid_tile(j),
                ).start()
            landed(recv_mid.at[pl.ds(0, mids - 1)], mid_sem.at[1])
            for j in range(1, mids):
                sums = sums + recv_mid[lax.rem(mid_at + j, mids)]
        held_group[...] = sums
        for j in range(1, GROUP):
            small_copy(
                held_group,
                recv_group.at[group_at],
                group_sem.at[0],
                group_sem.at[1],
                group_tile(j),
            ).start()
        landed(recv_group.at[pl.ds(0, GROUP - 1)], group_sem.at[1])
        for j in range(1, GROUP):
            sums = sums + recv_group[lax.rem(group_at + j, GROUP)]
        if mids > 1:
            sent(partial.at[pl.ds(0, mids - 1)], mid_sem.at[0])
        sent(recv_group.at[pl.ds(0, GROUP - 1)], group_sem.at[0])
        if deeps == 1:
            return sums[0]
        held_deep[...] = sums
        across_half = small_copy(
            held_deep.at[1 - deep_at], recv_deep, deep_sem.at[0], deep_sem.at[1], other_half
        )
        handed = small_copy(
            recv_deep, recv_deep, deep_sem.at[0], deep_sem.at[1], jnp.minimum(tile + 1, tiles - 1)
        )

        @pl.when(even)
        def _():
            across_half.start()
            across_half.wait()
            handed.start()
            handed.wait_send()

        @pl.when(jnp.logical_not(even))
        def _():
            handed.wait_recv()

        sums = held_deep[deep_at] + recv_deep[...]
        return sums

    def weights_of(sums):
        sub = lax.broadcasted_iota(jnp.int32, (8, 128), 0)
        lane8 = lax.broadcasted_iota(jnp.int32, (8, 128), 1)
        own = jnp.sum(jnp.where(sub == group_at, sums, 0.0), axis=0, keepdims=True)
        parts = jnp.where(
            jnp.right_shift(lane8, 4) == sub, jnp.broadcast_to(own, (8, 128)), 0.0
        )
        fold_from = lax.broadcasted_iota(jnp.int32, (128, 128), 0)
        fold_to = lax.broadcasted_iota(jnp.int32, (128, 128), 1)
        fold = (jnp.bitwise_and(fold_from, 15) == fold_to).astype(F32)
        system = jnp.dot(parts, fold, precision=HIGHEST, preferred_element_type=F32)
        system = system + jnp.where(lane8 == sub, float(members - 1), 0.0)
        for k in range(members):
            column = jnp.sum(jnp.where(lane8 == k, system, 0.0), axis=1, keepdims=True)
            pivot = system[k : k + 1] / column[k : k + 1]
            system = jnp.where(sub == k, pivot, system - column * pivot)
        return system - jnp.sum(system, axis=0, keepdims=True) * (1.0 / members)

    def spread_weights(centered):
        sub = lax.broadcasted_iota(jnp.int32, (8, 128), 0)
        lane8 = lax.broadcasted_iota(jnp.int32, (8, 128), 1)
        for j in range(4):
            member = 2 * me + j if j < 2 else 2 * beside + j - 2
            column = jnp.sum(
                jnp.where(lane8 == members + member, centered, 0.0), axis=1, keepdims=True
            )
            wide = jnp.broadcast_to(column, (8, 128))
            wide = wide + jnp.where(sub == member, 1.0, 0.0)
            for k in range(members):
                splats[j, k] = jnp.broadcast_to(wide[k : k + 1], (8, 128))

        for j in range(4):
            member = 2 * across + j if j < 2 else 2 * (3 - beside) + j - 2
            column = jnp.sum(
                jnp.where(lane8 == members + member, centered, 0.0), axis=1, keepdims=True
            )
            wide = jnp.broadcast_to(column, (8, 128))
            for k in range(4):
                source = 2 * me + k if k < 2 else 2 * beside + k - 2
                row = jnp.sum(jnp.where(sub == source, wide, 0.0), axis=0, keepdims=True)
                splats_across[j, k] = jnp.broadcast_to(row, (8, 128))

    def tail_piece(at):
        return (TAIL_FROM + at // 2) * quarters + 1 + at % 2

    def tail_copy(at, to, which):
        return pltpu.make_async_remote_copy(
            src_ref=tail_out.at[at, which],
            dst_ref=tail_in.at[at],
            send_sem=tail_sem,
            recv_sem=tail_recv.at[at],
            device_id=(to, tile),
            device_id_type=MESH,
        )

    def analyse_tail(at):
        piece = tail_piece(at)
        level, quarter = TAIL_FROM + at // 2, 1 + at % 2
        near_states = states.at[level, quarter, pl.ds(0, pair)]
        landed(near_states, piece_recv.at[piece])

        def tail_part(part, carry):
            r, first = part // (ntr // 8), pl.multiple_of(lax.rem(part, ntr // 8) * 8, 8)
            values = [
                states[level, quarter, 2 * source + k, r, pl.ds(first, 8), :]
                for source in (me, beside)
                for k in range(pair)
            ]
            for j in range(4):
                same_side, other_side = None, None
                for k in range(4):
                    source = 2 * me + k if k < 2 else 2 * beside + k - 2
                    here = values[k] * splats[j, source]
                    there = values[k] * splats_across[j, k]
                    same_side = here if k == 0 else same_side + here
                    other_side = there if k == 0 else other_side + there
                target = results if j < 2 else passed
                target[piece, r, j % 2, pl.ds(first, 8), :] = same_side
                tail_out[at, j // 2, r, j % 2, pl.ds(first, 8), :] = other_side
            return carry

        lax.fori_loop(0, QROWS * (ntr // 8), tail_part, 0)
        result_copy(piece).start()

    def finish_tail(at):
        piece = tail_piece(at)
        landed(tail_in.at[at], tail_recv.at[at])
        results[piece] = results[piece] + tail_in[at]
        for store in stores(piece):
            store.start()

    def analyse(piece):
        level, quarter = piece // quarters, lax.rem(piece, quarters)

        def analyse_part(at, carry):
            r, first = at // (ntr // 8), pl.multiple_of(lax.rem(at, ntr // 8) * 8, 8)
            sums = [None] * 4
            for k in range(members):
                value = states[level, quarter, k, r, pl.ds(first, 8), :]
                for j in range(4):
                    term = value * splats[j, k]
                    sums[j] = term if k == 0 else sums[j] + term
            for m in range(pair):
                results[piece, r, m, pl.ds(first, 8), :] = sums[m]
                passed[piece, r, m, pl.ds(first, 8), :] = sums[2 + m]
            return carry

        lax.fori_loop(0, QROWS * (ntr // 8), analyse_part, 0)
        result_copy(piece).start()
        for store in stores(piece):
            store.start()

    own_states = states.at[:, :, pl.ds(2 * me, 2)]

    @pl.when(tile < tiles - 1)
    def _():
        sent(raw.at[:, rows], halo_send.at[0])

    @pl.when(tile > 0)
    def _():
        sent(raw.at[:, 1], halo_send.at[1])

    if deeps > 1:
        end_pass()

    @pl.when(inner)
    def _():
        for at in range(5, 10):
            small(at).wait()
        for quarter in range(1, quarters - 1):
            wait_states(quarter)
        for quarter in (0, quarters - 1):
            wait_states(quarter)
        spread_weights(weights_of(partial_sums()))
        for at in range(TAIL):
            analyse_tail(at)

        def analyse_next(step, carry):
            piece = in_order(step)

            @pl.when(piece >= quarters)
            def _():
                wait_states(piece)

            analyse(piece)

            @pl.when(step == steps - AHEAD)
            def _():
                for at in range(TAIL):
                    tail_copy(at, 3 - beside, 1).start()
                for at in range(TAIL):
                    tail_copy(at, across, 0).start()

            return carry

        lax.fori_loop(0, steps, analyse_next, 0)
        for at in range(TAIL):
            finish_tail(at)
        sent(tail_out, tail_sem)
        sent(passed, result_send)
        sent(passed.at[pl.ds(0, steps)], state_send.at[0])

    @pl.when(outer)
    def _():
        def take(step, carry):
            piece = in_order(step)
            result_copy(piece).wait_recv()
            for store in stores(piece):
                store.start()
            return carry

        lax.fori_loop(0, steps, take, 0)
        for at in range(TAIL):
            result_copy(tail_piece(at)).wait_recv()
            finish_tail(at)
        sent(passed.at[pl.ds(0, steps)], state_send.at[0])
        sent(own_states, state_send.at[1])

    pltpu.make_async_copy(results, results, store_sem).wait()


def on_device(
    tracers,
    horiz_mix,
    vert_mix,
    sunlit,
    interaction,
    remin,
    obs_cell,
    obs_tile,
    obs_value,
    obs_noise,
    obs_var,
):
    pair, ntr, levels, rows, cols = tracers.shape
    tiles = lax.axis_size("space")
    deeps = DEEP if tiles > GROUP else 1
    mids = tiles // (deeps * GROUP)
    quarters = rows // QROWS
    pieces = levels * quarters
    count = obs_cell.shape[0]
    obs_rows = (count // cols, cols)
    pinned = pl.BlockSpec(memory_space=pltpu.HBM)
    anywhere = pl.BlockSpec(memory_space=pl.ANY)
    dma = pltpu.SemaphoreType.DMA
    operands = (
        tracers,
        horiz_mix,
        vert_mix,
        sunlit.reshape(-1, cols),
        interaction,
        remin.reshape(1, ntr),
        obs_cell.reshape(obs_rows),
        obs_tile.reshape(obs_rows),
        obs_value.reshape(obs_rows),
        obs_noise,
        obs_var.reshape(obs_rows),
    )
    operands = [pltpu.with_memory_space_constraint(value, pltpu.HBM) for value in operands]
    return pl.pallas_call(
        functools.partial(kernel, (tiles, mids, deeps)),
        out_shape=jax.ShapeDtypeStruct(tracers.shape, F32),
        in_specs=[pinned] * len(operands),
        out_specs=anywhere,
        scratch_shapes=[
            *[pltpu.VMEM(value.shape, value.dtype) for value in operands[1:]],
            pltpu.VMEM((rows, cols), F32),
            pltpu.VMEM((pair, ntr, cols), F32),
            pltpu.VMEM((levels, rows + 2, pair, ntr, cols), F32),
            pltpu.VMEM((levels, rows, pair, ntr, cols), F32),
            pltpu.VMEM((levels, quarters, 8, QROWS, ntr, cols), F32),
            pltpu.VMEM((pieces, QROWS, pair, ntr, cols), F32),
            pltpu.VMEM((pieces, QROWS, pair, ntr, cols), F32),
            pltpu.VMEM((rows * 8, cols), F32),
            pltpu.VMEM((mids, deeps, GROUP, 128), F32),
            pltpu.VMEM((mids, deeps, GROUP, 128), F32),
            pltpu.VMEM((deeps, GROUP, 128), F32),
            pltpu.VMEM((GROUP, deeps, GROUP, 128), F32),
            pltpu.VMEM((deeps, GROUP, 128), F32),
            pltpu.VMEM((GROUP, 128), F32),
            pltpu.VMEM((4, 8, 8, 128), F32),
            pltpu.VMEM((4, 4, 8, 128), F32),
            pltpu.VMEM((TAIL, 2, QROWS, pair, ntr, cols), F32),
            pltpu.VMEM((TAIL, QROWS, pair, ntr, cols), F32),
            dma((10,)),
            dma((levels,)),
            dma((levels, 2)),
            dma,
            dma,
            dma((2,)),
            dma((levels, 2)),
            dma((2,)),
            dma((pieces,)),
            dma,
            dma,
            dma,
            dma((TAIL,)),
            dma((2,)),
            dma((2,)),
            dma((2,)),
        ],
        compiler_params=pltpu.CompilerParams(
            collective_id=0, has_side_effects=True, vmem_limit_bytes=VMEM_BYTES
        ),
        cost_estimate=pl.CostEstimate(
            flops=500_000_000, bytes_accessed=8_000_000, transcendentals=3_000_000
        ),
        name="step_and_analysis",
    )(*operands)


def solution(mesh):
    return jax.shard_map(
        on_device,
        mesh=mesh,
        in_specs=(
            P("member", None, None, "space", None),
            P(None, "space", None),
            P(None, "space", None),
            P(),
            P(),
            P(),
            P(),
            P(),
            P(),
            P(),
            P(),
        ),
        out_specs=P("member", None, None, "space", None),
        check_vma=False,
    )
```
